32 devices in a mesh: lag: 4 (over z), probe: 4 (over y, x), sketch: 2 (over core).
Axes of the slice: x: 2, y: 2, z: 4, core: 2. Of those that a mesh axis runs over, the one named last changes fastest.
Arguments:
- markov: bfloat16 [16, 32, 8192], P('lag', None, ('probe', 'sketch')), may hold values from -36 to 36
- test_matrix: bfloat16 [4, 32, 256], P('lag', None, 'sketch'), may hold values from -0.5 to 0.5
Outputs:
- sketch_out: bfloat16 [16, 8192, 256], P('lag', 'probe', 'sketch')
The draws below stay inside these ranges and needn't reach their ends.
All inputs are finite; a program needn't handle non-finite values.
Results may differ from the reference program's by a relative error of at most 0.0004.
Values may be sent and summed in bfloat16 or wider, within the bound.
A program may use at most 64 MiB of HBM per device.

```python
import math
import jax
import jax.numpy as jnp
from jax import lax

P_SIZE = 8192
M_IN = 32
R = 256
S_DEV = 4
STEPS = 16
LAGS = 4
N_LAG = 4


def draw_markov(key, part):
    keys = jax.random.split(jax.random.fold_in(key, 17), 4)
    times = jnp.arange(STEPS, dtype=jnp.float32) / STEPS
    envelope = jnp.exp(-1.2 * times)
    base = jnp.clip(jax.random.normal(keys[0], (STEPS, M_IN, P_SIZE), jnp.float32), -5.0, 5.0)
    probe_scale = jnp.exp(jax.random.uniform(keys[1], (P_SIZE,), jnp.float32, 0.0, math.log(10.0)))
    input_scale = jnp.exp(jax.random.uniform(keys[2], (M_IN,), jnp.float32, 0.0, math.log(3.0)))
    rough = jnp.exp(jax.random.uniform(keys[3], (STEPS,), jnp.float32, -0.35, 0.35))
    values = base * (envelope * rough)[:, None, None] * input_scale[None, :, None] * probe_scale[None, None, :] / 6.0
    return values.astype(jnp.bfloat16)


def block_scale(own_key, shape, cuts, low, top_value):
    gain, own = 1.0, jax.random.fold_in(own_key, 6)
    for axis_at, blocks in cuts:
        draws = jnp.exp(jax.random.uniform(jax.random.fold_in(own, axis_at), (blocks,), jnp.float32, low / len(cuts), top_value / len(cuts)))
        gain = gain * jnp.repeat(draws, shape[axis_at] // blocks).reshape([-1 if axis == axis_at else 1 for axis in range(len(shape))])
    return gain


def noise(own_key, shape, width, most, shards=(), held_as=jnp.bfloat16):
    entries = jax.random.normal(own_key, shape, jnp.float32) * width
    if len(shards) > 0:
        entries = block_scale(own_key, shape, shards, -0.22, 0.18) * entries
    return jnp.clip(entries, min=-most, max=most).astype(held_as)


def setup_inputs(seed: int = 0) -> dict:
    key_list = jax.random.split(jax.random.key(seed), 3)
    return {
        "markov": draw_markov(jax.random.fold_in(key_list[2], 71), 0),
        "test_matrix": noise(key_list[1], (LAGS, M_IN, R), (LAGS * M_IN) ** -0.5, 0.5, ((0, 4), (2, 2))),
    }


def reference(markov, test_matrix):
    step_count = markov.shape[0]
    lag_count = test_matrix.shape[0]
    padded = jnp.concatenate([markov, jnp.zeros((lag_count, M_IN, P_SIZE), markov.dtype)], axis=0)
    flat_matrix = test_matrix.reshape(lag_count * M_IN, R)

    def group_rows(group_index):
        window = lax.dynamic_slice_in_dim(padded, group_index * S_DEV, S_DEV + lag_count, 0)
        pieces = [jnp.dot(window[row_index:row_index + lag_count].reshape(lag_count * M_IN, P_SIZE).T, flat_matrix, preferred_element_type=jnp.float32) for row_index in range(S_DEV)]
        return jnp.stack(pieces)
    sketch_raw = lax.map(group_rows, jnp.arange(N_LAG, dtype=jnp.int32)).reshape(step_count, P_SIZE, R)
    column_sums = lax.optimization_barrier(jnp.sum(sketch_raw * sketch_raw, axis=(0, 1)))
    factor = lax.rsqrt(column_sums / (step_count * P_SIZE) + 1e-06)
    return (sketch_raw * factor).astype(jnp.bfloat16)
```

```python
import functools

import jax
import jax.numpy as jnp
from jax import lax
from jax.experimental import pallas as pl
from jax.experimental.pallas import tpu as pltpu
from jax.sharding import PartitionSpec as P

MESH = pl.DeviceIdType.MESH
UNROLL = 32


def loop(count, body):
    if count <= UNROLL:
        for index in range(count):
            body(index)
    else:
        def step(index, carry):
            body(index)
            return carry
        lax.fori_loop(0, count, step, 0)


def plan(step_count, lag_total):
    steps = step_count + lag_total - 1
    blocks = (steps - 1) // step_count
    pieces = []
    for ahead in range(1, blocks + 1):
        used = min(step_count, steps - ahead * step_count)
        if blocks == 1:
            pieces += [(ahead, at, 1) for at in range(used)]
        else:
            pieces.append((ahead, 0, used))
    return steps, pieces


def gather_kernel(
    sizes, markov, matrix, raw, factor,
    window, held, weights, sums,
    own_sem, matrix_own_sem, matrix_send, matrix_recv,
    pair_send, pair_recv, lag_send, lag_recv, next_send, next_recv, sum_send, sum_recv,
):
    n_lag, n_probe, n_sketch = sizes
    step_count, input_count, half = markov.shape
    matrix_rows = matrix.shape[0]
    columns = matrix.shape[2]
    lag_total = matrix_rows * n_lag
    steps, pieces = plan(step_count, lag_total)
    lag = lax.axis_index("lag")
    probe = lax.axis_index("probe")
    sketch = lax.axis_index("sketch")
    flat = lag * n_probe + probe
    peers = n_lag * n_probe - 1

    def peer(index):
        other = lax.rem(flat + 1 + index, peers + 1)
        return {
            "lag": lax.div(other, n_probe),
            "probe": lax.rem(other, n_probe),
            "sketch": sketch,
        }

    def partner(index):
        return {"lag": lag, "probe": probe, "sketch": lax.rem(sketch + 1 + index, n_sketch)}

    def lag_peer(index):
        return {"lag": lax.rem(lag + 1 + index, n_lag), "probe": probe, "sketch": sketch}

    barrier = pltpu.get_barrier_semaphore()

    def greet(index):
        pl.semaphore_signal(barrier, inc=1, device_id=peer(index), device_id_type=MESH)

    for index in range(n_sketch - 1):
        pl.semaphore_signal(barrier, inc=1, device_id=partner(index), device_id_type=MESH)
    loop(peers, greet)

    own = pltpu.make_async_copy(markov, window.at[sketch, pl.ds(0, step_count)], own_sem)
    own.start()
    matrix_own = pltpu.make_async_copy(
        matrix, held.at[pl.ds(lag * matrix_rows, matrix_rows)], matrix_own_sem
    )
    matrix_own.start()
    weights[...] = jnp.zeros_like(weights)
    for ahead, at, count in pieces:
        @pl.when(lag + ahead >= n_lag)
        def _():
            place = pl.ds(ahead * step_count + at, count)
            window[:, place] = jnp.zeros((n_sketch, count, input_count, half), window.dtype)

    matrix_own.wait()
    pl.semaphore_wait(barrier, peers + n_sketch - 1)

    def lag_copy(number):
        ahead, at, count = pieces[number]
        return pltpu.make_async_remote_copy(
            src_ref=markov.at[pl.ds(at, count)],
            dst_ref=window.at[sketch, pl.ds(ahead * step_count + at, count)],
            send_sem=lag_send.at[number],
            recv_sem=lag_recv.at[number],
            device_id={"lag": lax.max(lag - ahead, 0), "probe": probe, "sketch": sketch},
            device_id_type=MESH,
        )

    def pair_copy(index):
        return pltpu.make_async_remote_copy(
            src_ref=markov,
            dst_ref=window.at[sketch, pl.ds(0, step_count)],
            send_sem=pair_send.at[index],
            recv_sem=pair_recv.at[index],
            device_id=partner(index),
            device_id_type=MESH,
        )

    def next_copy(number, index):
        ahead, at, count = pieces[number]
        place = window.at[sketch, pl.ds(ahead * step_count + at, count)]
        return pltpu.make_async_remote_copy(
            src_ref=place,
            dst_ref=place,
            send_sem=next_send.at[number, index],
            recv_sem=next_recv.at[number, index],
            device_id=partner(index),
            device_id_type=MESH,
        )

    def matrix_copy(index):
        return pltpu.make_async_remote_copy(
            src_ref=held.at[pl.ds(lag * matrix_rows, matrix_rows)],
            dst_ref=held.at[pl.ds(lag * matrix_rows, matrix_rows)],
            send_sem=matrix_send,
            recv_sem=matrix_recv,
            device_id=lag_peer(index),
            device_id_type=MESH,
        )

    loop(n_lag - 1, lambda index: matrix_copy(index).start())
    for number in range(0, 1):
        @pl.when(lag >= pieces[number][0])
        def _():
            lag_copy(number).start()
    for index in range(n_sketch - 1):
        pair_copy(index).start()
    for number in range(1, len(pieces)):
        @pl.when(lag >= pieces[number][0])
        def _():
            lag_copy(number).start()

    if n_lag > 1:
        arrived = held.at[pl.ds(0, (n_lag - 1) * matrix_rows)]
        pltpu.make_async_copy(arrived, arrived, matrix_recv).wait()
        pltpu.make_async_copy(arrived, arrived, matrix_send).wait()
    for row in range(step_count):
        weights[pl.ds(row * input_count, lag_total * input_count), row * columns:(row + 1) * columns] = (
            held[...].reshape(lag_total * input_count, columns)
        )

    def forward(number):
        @pl.when(lag + pieces[number][0] < n_lag)
        def _():
            lag_copy(number).wait_recv()
            for index in range(n_sketch - 1):
                next_copy(number, index).start()

    def landed(number):
        @pl.when(lag + pieces[number][0] < n_lag)
        def _():
            for index in range(n_sketch - 1):
                next_copy(number, index).wait()

    tile = min(256, half)
    group = 2 if step_count % 2 == 0 else 1

    def compute(first, total):
        depth = (lag_total + group - 1) * input_count
        weight = weights[pl.ds(first * input_count, depth), first * columns:(first + group) * columns]
        for side in range(n_sketch):
            def body(at, total):
                start = pl.multiple_of(at * tile, tile)
                block = window[side, pl.ds(first, lag_total + group - 1), :, pl.ds(start, tile)]
                product = lax.dot_general(
                    block.reshape(depth, tile), weight, (((0,), (0,)), ((), ())),
                    preferred_element_type=jnp.float32,
                )
                for row in range(group):
                    part = product[:, row * columns:(row + 1) * columns]
                    raw[first + row, pl.ds(side * half + start, tile), :] = part
                    total = total + jnp.sum((part * part).reshape(tile // 8, 8, columns), axis=0)
                return total
            total = lax.fori_loop(0, half // tile, body, total, unroll=depth <= 512)
        return total

    own.wait()
    total = jnp.zeros((8, columns), jnp.float32)
    done = 0
    paired = False
    for first in range(0, step_count, group):
        need = first + group - 1 + lag_total
        ready = done
        while ready < len(pieces) and pieces[ready][0] * step_count + pieces[ready][1] < need:
            forward(ready)
            ready += 1
        if not paired:
            for index in range(n_sketch - 1):
                pair_copy(index).wait()
            paired = True
        for number in range(done, ready):
            landed(number)
        done = ready
        total = compute(first, total)

    sums[pl.ds(flat, 1), :] = jnp.sum(total, axis=0, keepdims=True)

    def sum_copy(index):
        place = sums.at[pl.ds(flat, 1)]
        return pltpu.make_async_remote_copy(
            src_ref=place,
            dst_ref=place,
            send_sem=sum_send,
            recv_sem=sum_recv,
            device_id=peer(index),
            device_id_type=MESH,
        )

    loop(peers, lambda index: sum_copy(index).start())
    for number in range(len(pieces)):
        @pl.when(lag >= pieces[number][0])
        def _():
            lag_copy(number).wait_send()
    if peers:
        arrived = sums.at[pl.ds(0, peers)]
        pltpu.make_async_copy(arrived, arrived, sum_recv).wait()
        pltpu.make_async_copy(arrived, arrived, sum_send).wait()
    cells = step_count * n_lag * half * n_sketch * n_probe
    mean = jnp.sum(sums[...], axis=0, keepdims=True) / cells
    factor[...] = jnp.broadcast_to(lax.rsqrt(mean + 1e-06), factor.shape)


def near_kernel(
    sizes, cut, markov, matrix, raw, factor,
    window, held, weights, gram, other, sums,
    own_sem, matrix_own_sem, matrix_send, matrix_recv, pair_send, pair_recv,
    down_send, down_recv, up_send, up_recv, pass_send, pass_recv, sum_send, sum_recv, all_in,
):
    n_lag, n_probe, n_sketch = sizes
    step_count, input_count, half = markov.shape
    columns = matrix.shape[2]
    matrix_rows = matrix.shape[0]
    lag_total = matrix_rows * n_lag
    depth = lag_total * input_count
    later = lag_total - 1
    alone = step_count - later
    lag = lax.axis_index("lag")
    probe = lax.axis_index("probe")
    sketch = lax.axis_index("sketch")
    twin = 1 - sketch
    place = (lag * n_probe + probe) * n_sketch + sketch
    devices = n_lag * n_probe * n_sketch
    line = n_lag * n_sketch
    is_first = lag == 0
    is_last = lag == n_lag - 1
    is_head = place == devices - 1
    below = {"lag": lax.max(lag - 1, 0), "probe": probe, "sketch": sketch}
    above = {"lag": lax.min(lag + 1, n_lag - 1), "probe": probe, "sketch": sketch}
    partner = {"lag": lag, "probe": probe, "sketch": twin}

    def device(index):
        group = lax.div(index, n_sketch)
        return {
            "lag": lax.div(group, n_probe),
            "probe": lax.rem(group, n_probe),
            "sketch": lax.rem(index, n_sketch),
        }

    def on_line(index):
        at = lax.rem(lag * n_sketch + sketch + 1 + index, line)
        return {"lag": lax.div(at, n_sketch), "probe": probe, "sketch": lax.rem(at, n_sketch)}

    barrier = pltpu.get_barrier_semaphore()
    loop(line - 1, lambda index: pl.semaphore_signal(
        barrier, inc=1, device_id=on_line(index), device_id_type=MESH
    ))

    @pl.when(probe < n_probe - 1)
    def _():
        pl.semaphore_signal(barrier, inc=1, device_id=device(devices - 1), device_id_type=MESH)

    own_slots = pl.ds(later, step_count)
    next_slots = pl.ds(later + step_count, later)
    own_rows = held.at[sketch, pl.ds(lag * matrix_rows, matrix_rows)]
    matrix_own = pltpu.make_async_copy(matrix, own_rows, matrix_own_sem)
    matrix_own.start()
    own = pltpu.make_async_copy(markov, window.at[sketch, own_slots], own_sem)
    own.start()
    weights[...] = jnp.zeros_like(weights)

    @pl.when(is_last)
    def _():
        window[:, next_slots] = jnp.zeros((n_sketch, later, input_count, half), window.dtype)

    parts = (pl.ds(0, cut), pl.ds(cut, half - cut))

    def remote(src, dst, send, recv, to):
        return pltpu.make_async_remote_copy(
            src_ref=src, dst_ref=dst, send_sem=send, recv_sem=recv, device_id=to, device_id_type=MESH
        )

    def down(part):
        return remote(
            window.at[sketch, pl.ds(later, later), :, parts[part]],
            window.at[sketch, next_slots, :, parts[part]],
            down_send.at[part], down_recv.at[part], below,
        )

    def up():
        return remote(
            window.at[sketch, pl.ds(later + alone, later), :, parts[1]],
            window.at[sketch, pl.ds(0, later), :, parts[1]],
            up_send, up_recv, above,
        )

    def passed(part):
        ref = window.at[sketch, next_slots, :, parts[part]]
        return remote(ref, ref, pass_send.at[part], pass_recv.at[part], partner)

    pair = remote(
        window.at[sketch, own_slots], window.at[sketch, own_slots], pair_send, pair_recv, partner
    )

    matrix_own.wait()
    pl.semaphore_wait(barrier, lax.select(is_head, devices - 1, line - 1))
    loop(line - 1, lambda index: remote(own_rows, own_rows, matrix_send, matrix_recv, on_line(index)).start())
    own.wait()

    @pl.when(jnp.logical_not(is_first))
    def _():
        down(0).start()

    @pl.when(jnp.logical_not(is_last))
    def _():
        up().start()

    pair.start()

    @pl.when(jnp.logical_not(is_first))
    def _():
        down(1).start()

    @pl.when(is_head)
    def _():
        loop(devices - 1, lambda index: pl.semaphore_signal(
            all_in, inc=1, device_id=device(index), device_id_type=MESH
        ))

    def outer(first, second, start, stop):
        def rows(slots):
            slot, count = slots
            return window[sketch, pl.ds(slot, count), :, start:stop].reshape(count * input_count, stop - start)
        return lax.dot_general(
            rows(first), rows(second), (((1,), (1,)), ((), ())), preferred_element_type=jnp.float32
        )

    inner = outer((later, step_count), (later, step_count), 0, half)
    gram[...] = jnp.zeros_like(gram)

    def shift(row):
        low, high = max(0, -row), min(lag_total, step_count - row)
        to = slice(low * input_count, high * input_count)
        at = slice((row + low) * input_count, (row + high) * input_count)
        gram[to, to] += inner[at, at]

    for row in range(step_count):
        shift(row)

    @pl.when(jnp.logical_not(is_first))
    def _():
        for row in range(-later, 0):
            shift(row)

    def cross(edge):
        for row in range(alone, step_count):
            count = (step_count - row) * input_count
            gram[0:count, count:depth] += 2.0 * edge[(row - alone) * input_count:, 0:(row - alone + 1) * input_count]

    @pl.when(jnp.logical_not(is_first))
    def _():
        up().wait_recv()
        cross(outer((0, later), (later, later), cut, half))

    @pl.when(jnp.logical_not(is_last))
    def _():
        down(0).wait_recv()
        passed(0).start()
        cross(outer((later + alone, later), (later + step_count, later), 0, cut))

    whole = gram[...]
    high = whole.astype(jnp.bfloat16)
    rest = whole - high.astype(jnp.float32)
    middle = rest.astype(jnp.bfloat16)
    low = (rest - middle.astype(jnp.float32)).astype(jnp.bfloat16)

    flat = held.reshape(n_sketch * lag_total, input_count, columns)
    arrived = flat.at[pl.ds(0, n_sketch * lag_total - matrix_rows)]
    pltpu.make_async_copy(arrived, arrived, matrix_recv).wait()
    mine = held[sketch].reshape(depth, columns)
    both = jnp.concatenate([mine, held[twin].reshape(depth, columns)], axis=1)
    product = jnp.dot(low, both, preferred_element_type=jnp.float32)
    product = product + jnp.dot(middle, both, preferred_element_type=jnp.float32)
    product = product + jnp.dot(high, both, preferred_element_type=jnp.float32)
    square = jnp.sum(product * both.astype(jnp.float32), axis=0, keepdims=True)
    sums[pl.ds(place, 1), :] = square[:, :columns]
    other[...] = square[:, columns:]

    def sum_copy(index, side):
        at = lax.rem(lag * n_probe + probe + index, n_lag * n_probe)
        to = {"lag": lax.div(at, n_probe), "probe": lax.rem(at, n_probe), "sketch": side}
        ref = sums.at[pl.ds(place, 1)]
        src = other if side is twin else ref
        return remote(src, ref, sum_send, sum_recv, to)

    @pl.when(jnp.logical_not(is_head))
    def _():
        pl.semaphore_wait(all_in, 1)

    loop(n_lag * n_probe - 1, lambda index: sum_copy(index + 1, sketch).start())
    loop(n_lag * n_probe, lambda index: sum_copy(index, twin).start())

    for row in range(step_count):
        weights[pl.ds(row * input_count, depth), row * columns:(row + 1) * columns] = mine

    tile = 256

    def multiply(side, first, last):
        for start in range(first, last, tile):
            block = window[side, pl.ds(later, step_count + later), :, pl.ds(start, tile)]
            product = lax.dot_general(
                block.reshape((step_count + later) * input_count, tile), weights[...], (((0,), (0,)), ((), ())),
                preferred_element_type=jnp.float32,
            )
            for row in range(step_count):
                raw[row, pl.ds(pl.multiple_of(side * half + start, tile), tile), :] = (
                    product[:, row * columns:(row + 1) * columns]
                )

    multiply(sketch, 0, cut)
    pair.wait()

    @pl.when(jnp.logical_not(is_last))
    def _():
        passed(0).wait_recv()

    multiply(twin, 0, cut)

    @pl.when(jnp.logical_not(is_last))
    def _():
        down(1).wait_recv()
        passed(1).start()

    multiply(sketch, cut, half)

    @pl.when(jnp.logical_not(is_last))
    def _():
        passed(1).wait_recv()

    multiply(twin, cut, half)

    @pl.when(jnp.logical_not(is_last))
    def _():
        passed(0).wait_send()
        passed(1).wait_send()
        up().wait_send()

    @pl.when(jnp.logical_not(is_first))
    def _():
        down(0).wait_send()
        down(1).wait_send()

    pltpu.make_async_copy(arrived, arrived, matrix_send).wait()
    landed = sums.at[pl.ds(0, devices - 1)]
    pltpu.make_async_copy(landed, landed, sum_send).wait()
    pltpu.make_async_copy(landed, landed, sum_recv).wait()
    cells = step_count * n_lag * half * n_sketch * n_probe
    mean = lax.max(jnp.sum(sums[...], axis=0, keepdims=True), 0.0) / cells
    factor[...] = jnp.broadcast_to(lax.rsqrt(mean + 1e-06), factor.shape)


def near(sizes, markov, test_matrix):
    n_lag, n_probe, n_sketch = sizes
    step_count, input_count, half = markov.shape
    matrix_rows, _, columns = test_matrix.shape
    lag_total = matrix_rows * n_lag
    later = lag_total - 1
    dma = pltpu.SemaphoreType.DMA
    return pl.pallas_call(
        functools.partial(near_kernel, sizes, half * 3 // 4),
        out_shape=[
            pltpu.VMEM((step_count, half * n_sketch, columns), jnp.float32),
            pltpu.VMEM((8, columns), jnp.float32),
        ],
        in_specs=[pl.BlockSpec(memory_space=pltpu.HBM)] * 2,
        out_specs=[pl.BlockSpec(memory_space=pltpu.VMEM)] * 2,
        scratch_shapes=[
            pltpu.VMEM((n_sketch, step_count + 2 * later, input_count, half), jnp.bfloat16),
            pltpu.VMEM((n_sketch, lag_total, input_count, columns), jnp.bfloat16),
            pltpu.VMEM(((step_count + later) * input_count, step_count * columns), jnp.bfloat16),
            pltpu.VMEM((lag_total * input_count, lag_total * input_count), jnp.float32),
            pltpu.VMEM((1, columns), jnp.float32),
            pltpu.VMEM((n_lag * n_probe * n_sketch, columns), jnp.float32),
            dma, dma, dma, dma, dma, dma,
            dma((2,)), dma((2,)), dma, dma, dma((2,)), dma((2,)), dma, dma,
            pltpu.SemaphoreType.REGULAR,
        ],
        compiler_params=pltpu.CompilerParams(
            collective_id=1, has_side_effects=True, vmem_limit_bytes=59 * 1024 * 1024
        ),
    )(markov, test_matrix)


def is_near(sizes, markov, test_matrix):
    n_lag, n_probe, n_sketch = sizes
    step_count, input_count, half = markov.shape
    lag_total = test_matrix.shape[0] * n_lag
    return n_sketch == 2 and n_lag > 1 and 1 < lag_total <= step_count and half % 512 == 0


def scale_kernel(raw, factor, out, held, sem):
    step_count, probes, columns = raw.shape
    pieces = 2
    part = probes // pieces
    copies = []
    gain = factor[0:1, :]
    for row in range(step_count):
        for piece in range(pieces):
            place = pl.ds(piece * part, part)
            held[row, place] = (raw[row, place] * gain).astype(held.dtype)
            copy = pltpu.make_async_copy(
                held.at[row, place], out.at[row, place], sem.at[row * pieces + piece]
            )
            copy.start()
            copies.append(copy)
    for copy in copies:
        copy.wait()


def scale(raw, factor):
    step_count, probes, columns = raw.shape
    return pl.pallas_call(
        scale_kernel,
        out_shape=jax.ShapeDtypeStruct(raw.shape, jnp.bfloat16),
        in_specs=[pl.BlockSpec(memory_space=pltpu.VMEM)] * 2,
        out_specs=pl.BlockSpec(memory_space=pltpu.HBM),
        scratch_shapes=[
            pltpu.VMEM(raw.shape, jnp.bfloat16),
            pltpu.SemaphoreType.DMA((step_count * 2,)),
        ],
        compiler_params=pltpu.CompilerParams(vmem_limit_bytes=16 * 1024 * 1024),
    )(raw, factor)


def local(sizes, markov, test_matrix):
    if is_near(sizes, markov, test_matrix):
        return scale(*near(sizes, markov, test_matrix))
    n_lag, n_probe, n_sketch = sizes
    step_count, input_count, half = markov.shape
    matrix_rows, _, columns = test_matrix.shape
    lag_total = matrix_rows * n_lag
    steps, pieces = plan(step_count, lag_total)
    count = max(len(pieces), 1)
    pairs = max(n_sketch - 1, 1)
    probes = half * n_sketch
    dma = pltpu.SemaphoreType.DMA
    raw, factor = pl.pallas_call(
        functools.partial(gather_kernel, sizes),
        out_shape=[
            pltpu.VMEM((step_count, probes, columns), jnp.float32),
            pltpu.VMEM((8, columns), jnp.float32),
        ],
        in_specs=[pl.BlockSpec(memory_space=pltpu.HBM)] * 2,
        out_specs=[pl.BlockSpec(memory_space=pltpu.VMEM)] * 2,
        scratch_shapes=[
            pltpu.VMEM((n_sketch, steps, input_count, half), jnp.bfloat16),
            pltpu.VMEM((lag_total, input_count, columns), jnp.bfloat16),
            pltpu.VMEM((steps * input_count, step_count * columns), jnp.bfloat16),
            pltpu.VMEM((n_lag * n_probe, columns), jnp.float32),
            dma, dma, dma, dma,
            dma((pairs,)), dma((pairs,)),
            dma((count,)), dma((count,)),
            dma((count, pairs)), dma((count, pairs)),
            dma, dma,
        ],
        compiler_params=pltpu.CompilerParams(
            collective_id=0, has_side_effects=True, vmem_limit_bytes=59 * 1024 * 1024
        ),
    )(markov, test_matrix)
    return scale(raw, factor)


def solution(mesh):
    sizes = tuple(mesh.shape[name] for name in ("lag", "probe", "sketch"))
    return jax.shard_map(
        functools.partial(local, sizes),
        mesh=mesh,
        in_specs=(P("lag", None, ("probe", "sketch")), P("lag", None, "sketch")),
        out_specs=P("lag", "probe", "sketch"),
        check_vma=False,
    )
```

```python
import functools

import jax
import jax.numpy as jnp
from jax import lax
from jax.experimental import pallas as pl
from jax.experimental.pallas import tpu as pltpu
from jax.sharding import PartitionSpec as P

MESH = pl.DeviceIdType.MESH
UNROLL = 32


def loop(count, body):
    if count <= UNROLL:
        for index in range(count):
            body(index)
    else:
        def step(index, carry):
            body(index)
            return carry
        lax.fori_loop(0, count, step, 0)


def plan(step_count, lag_total):
    steps = step_count + lag_total - 1
    blocks = (steps - 1) // step_count
    pieces = []
    for ahead in range(1, blocks + 1):
        used = min(step_count, steps - ahead * step_count)
        if blocks == 1:
            pieces += [(ahead, at, 1) for at in range(used)]
        else:
            pieces.append((ahead, 0, used))
    return steps, pieces


def gather_kernel(
    sizes, markov, matrix, raw, factor,
    window, held, weights, sums,
    own_sem, matrix_own_sem, matrix_send, matrix_recv,
    pair_send, pair_recv, lag_send, lag_recv, next_send, next_recv, sum_send, sum_recv,
):
    n_lag, n_probe, n_sketch = sizes
    step_count, input_count, half = markov.shape
    matrix_rows = matrix.shape[0]
    columns = matrix.shape[2]
    lag_total = matrix_rows * n_lag
    steps, pieces = plan(step_count, lag_total)
    lag = lax.axis_index("lag")
    probe = lax.axis_index("probe")
    sketch = lax.axis_index("sketch")
    flat = lag * n_probe + probe
    peers = n_lag * n_probe - 1

    def peer(index):
        other = lax.rem(flat + 1 + index, peers + 1)
        return {
            "lag": lax.div(other, n_probe),
            "probe": lax.rem(other, n_probe),
            "sketch": sketch,
        }

    def partner(index):
        return {"lag": lag, "probe": probe, "sketch": lax.rem(sketch + 1 + index, n_sketch)}

    def lag_peer(index):
        return {"lag": lax.rem(lag + 1 + index, n_lag), "probe": probe, "sketch": sketch}

    barrier = pltpu.get_barrier_semaphore()

    def greet(index):
        pl.semaphore_signal(barrier, inc=1, device_id=peer(index), device_id_type=MESH)

    for index in range(n_sketch - 1):
        pl.semaphore_signal(barrier, inc=1, device_id=partner(index), device_id_type=MESH)
    loop(peers, greet)

    own = pltpu.make_async_copy(markov, window.at[sketch, pl.ds(0, step_count)], own_sem)
    own.start()
    matrix_own = pltpu.make_async_copy(
        matrix, held.at[pl.ds(lag * matrix_rows, matrix_rows)], matrix_own_sem
    )
    matrix_own.start()
    weights[...] = jnp.zeros_like(weights)
    for ahead, at, count in pieces:
        @pl.when(lag + ahead >= n_lag)
        def _():
            place = pl.ds(ahead * step_count + at, count)
            window[:, place] = jnp.zeros((n_sketch, count, input_count, half), window.dtype)

    matrix_own.wait()
    pl.semaphore_wait(barrier, peers + n_sketch - 1)

    def lag_copy(number):
        ahead, at, count = pieces[number]
        return pltpu.make_async_remote_copy(
            src_ref=markov.at[pl.ds(at, count)],
            dst_ref=window.at[sketch, pl.ds(ahead * step_count + at, count)],
            send_sem=lag_send.at[number],
            recv_sem=lag_recv.at[number],
            device_id={"lag": lax.max(lag - ahead, 0), "probe": probe, "sketch": sketch},
            device_id_type=MESH,
        )

    def pair_copy(index):
        return pltpu.make_async_remote_copy(
            src_ref=markov,
            dst_ref=window.at[sketch, pl.ds(0, step_count)],
            send_sem=pair_send.at[index],
            recv_sem=pair_recv.at[index],
            device_id=partner(index),
            device_id_type=MESH,
        )

    def next_copy(number, index):
        ahead, at, count = pieces[number]
        place = window.at[sketch, pl.ds(ahead * step_count + at, count)]
        return pltpu.make_async_remote_copy(
            src_ref=place,
            dst_ref=place,
            send_sem=next_send.at[number, index],
            recv_sem=next_recv.at[number, index],
            device_id=partner(index),
            device_id_type=MESH,
        )

    def matrix_copy(index):
        return pltpu.make_async_remote_copy(
            src_ref=held.at[pl.ds(lag * matrix_rows, matrix_rows)],
            dst_ref=held.at[pl.ds(lag * matrix_rows, matrix_rows)],
            send_sem=matrix_send,
            recv_sem=matrix_recv,
            device_id=lag_peer(index),
            device_id_type=MESH,
        )

    loop(n_lag - 1, lambda index: matrix_copy(index).start())
    for number in range(0, 1):
        @pl.when(lag >= pieces[number][0])
        def _():
            lag_copy(number).start()
    for index in range(n_sketch - 1):
        pair_copy(index).start()
    for number in range(1, len(pieces)):
        @pl.when(lag >= pieces[number][0])
        def _():
            lag_copy(number).start()

    if n_lag > 1:
        arrived = held.at[pl.ds(0, (n_lag - 1) * matrix_rows)]
        pltpu.make_async_copy(arrived, arrived, matrix_recv).wait()
        pltpu.make_async_copy(arrived, arrived, matrix_send).wait()
    for row in range(step_count):
        weights[pl.ds(row * input_count, lag_total * input_count), row * columns:(row + 1) * columns] = (
            held[...].reshape(lag_total * input_count, columns)
        )

    def forward(number):
        @pl.when(lag + pieces[number][0] < n_lag)
        def _():
            lag_copy(number).wait_recv()
            for index in range(n_sketch - 1):
                next_copy(number, index).start()

    def landed(number):
        @pl.when(lag + pieces[number][0] < n_lag)
        def _():
            for index in range(n_sketch - 1):
                next_copy(number, index).wait()

    tile = min(256, half)
    group = 2 if step_count % 2 == 0 else 1

    def compute(first, total):
        depth = (lag_total + group - 1) * input_count
        weight = weights[pl.ds(first * input_count, depth), first * columns:(first + group) * columns]
        for side in range(n_sketch):
            def body(at, total):
                start = pl.multiple_of(at * tile, tile)
                block = window[side, pl.ds(first, lag_total + group - 1), :, pl.ds(start, tile)]
                product = lax.dot_general(
                    block.reshape(depth, tile), weight, (((0,), (0,)), ((), ())),
                    preferred_element_type=jnp.float32,
                )
                for row in range(group):
                    part = product[:, row * columns:(row + 1) * columns]
                    raw[first + row, pl.ds(side * half + start, tile), :] = part
                    total = total + jnp.sum((part * part).reshape(tile // 8, 8, columns), axis=0)
                return total
            total = lax.fori_loop(0, half // tile, body, total, unroll=depth <= 512)
        return total

    own.wait()
    total = jnp.zeros((8, columns), jnp.float32)
    done = 0
    paired = False
    for first in range(0, step_count, group):
        need = first + group - 1 + lag_total
        ready = done
        while ready < len(pieces) and pieces[ready][0] * step_count + pieces[ready][1] < need:
            forward(ready)
            ready += 1
        if not paired:
            for index in range(n_sketch - 1):
                pair_copy(index).wait()
            paired = True
        for number in range(done, ready):
            landed(number)
        done = ready
        total = compute(first, total)

    sums[pl.ds(flat, 1), :] = jnp.sum(total, axis=0, keepdims=True)

    def sum_copy(index):
        place = sums.at[pl.ds(flat, 1)]
        return pltpu.make_async_remote_copy(
            src_ref=place,
            dst_ref=place,
            send_sem=sum_send,
            recv_sem=sum_recv,
            device_id=peer(index),
            device_id_type=MESH,
        )

    loop(peers, lambda index: sum_copy(index).start())
    for number in range(len(pieces)):
        @pl.when(lag >= pieces[number][0])
        def _():
            lag_copy(number).wait_send()
    if peers:
        arrived = sums.at[pl.ds(0, peers)]
        pltpu.make_async_copy(arrived, arrived, sum_recv).wait()
        pltpu.make_async_copy(arrived, arrived, sum_send).wait()
    cells = step_count * n_lag * half * n_sketch * n_probe
    mean = jnp.sum(sums[...], axis=0, keepdims=True) / cells
    factor[...] = jnp.broadcast_to(lax.rsqrt(mean + 1e-06), factor.shape)


def near_kernel(
    sizes, cut, markov, matrix, raw, factor,
    window, held, weights, gram, other, sums,
    own_sem, matrix_own_sem, matrix_send, matrix_recv, hand_send, pair_send, pair_recv,
    down_send, down_recv, up_send, up_recv, pass_send, pass_recv, sum_send, sum_recv, all_in,
):
    n_lag, n_probe, n_sketch = sizes
    step_count, input_count, half = markov.shape
    columns = matrix.shape[2]
    matrix_rows = matrix.shape[0]
    lag_total = matrix_rows * n_lag
    depth = lag_total * input_count
    later = lag_total - 1
    alone = step_count - later
    lag = lax.axis_index("lag")
    probe = lax.axis_index("probe")
    sketch = lax.axis_index("sketch")
    twin = 1 - sketch
    place = (lag * n_probe + probe) * n_sketch + sketch
    devices = n_lag * n_probe * n_sketch
    line = n_lag * n_sketch
    is_first = lag == 0
    is_last = lag == n_lag - 1
    is_head = place == devices - 1
    below = {"lag": lax.max(lag - 1, 0), "probe": probe, "sketch": sketch}
    above = {"lag": lax.min(lag + 1, n_lag - 1), "probe": probe, "sketch": sketch}
    partner = {"lag": lag, "probe": probe, "sketch": twin}

    def device(index):
        group = lax.div(index, n_sketch)
        return {
            "lag": lax.div(group, n_probe),
            "probe": lax.rem(group, n_probe),
            "sketch": lax.rem(index, n_sketch),
        }

    def on_line(index):
        at = lax.rem(lag * n_sketch + sketch + 1 + index, line)
        return {"lag": lax.div(at, n_sketch), "probe": probe, "sketch": lax.rem(at, n_sketch)}

    barrier = pltpu.get_barrier_semaphore()
    loop(line - 1, lambda index: pl.semaphore_signal(
        barrier, inc=1, device_id=on_line(index), device_id_type=MESH
    ))

    @pl.when(probe < n_probe - 1)
    def _():
        pl.semaphore_signal(barrier, inc=1, device_id=device(devices - 1), device_id_type=MESH)

    own_slots = pl.ds(later, step_count)
    next_slots = pl.ds(later + step_count, later)
    own_rows = held.at[sketch, pl.ds(lag * matrix_rows, matrix_rows)]
    matrix_own = pltpu.make_async_copy(matrix, own_rows, matrix_own_sem)
    matrix_own.start()
    own = pltpu.make_async_copy(markov, window.at[sketch, own_slots], own_sem)
    own.start()
    weights[...] = jnp.zeros_like(weights)

    @pl.when(is_last)
    def _():
        window[:, next_slots] = jnp.zeros((n_sketch, later, input_count, half), window.dtype)

    parts = (pl.ds(0, cut), pl.ds(cut, half - cut))

    def remote(src, dst, send, recv, to):
        return pltpu.make_async_remote_copy(
            src_ref=src, dst_ref=dst, send_sem=send, recv_sem=recv, device_id=to, device_id_type=MESH
        )

    def down(part):
        return remote(
            window.at[sketch, pl.ds(later, later), :, parts[part]],
            window.at[sketch, next_slots, :, parts[part]],
            down_send.at[part], down_recv.at[part], below,
        )

    def up():
        return remote(
            window.at[sketch, pl.ds(later + alone, later), :, parts[1]],
            window.at[sketch, pl.ds(0, later), :, parts[1]],
            up_send, up_recv, above,
        )

    def passed(part):
        ref = window.at[sketch, next_slots, :, parts[part]]
        return remote(ref, ref, pass_send.at[part], pass_recv.at[part], partner)

    pair = remote(
        window.at[sketch, own_slots], window.at[sketch, own_slots], pair_send, pair_recv, partner
    )

    matrix_own.wait()
    pl.semaphore_wait(barrier, lax.select(is_head, devices - 1, line - 1))

    def rows_of(index):
        return held.at[sketch, pl.ds(index * matrix_rows, matrix_rows)]

    def matrix_copy(to_lag, side):
        return remote(
            own_rows, own_rows, matrix_send.at[side, to_lag], matrix_recv.at[side, lag],
            {"lag": to_lag, "probe": probe, "sketch": sketch if side == 0 else twin},
        )

    def matrix_hand(index):
        return remote(
            rows_of(index), rows_of(index), hand_send.at[index], matrix_recv.at[1, index], partner
        )

    def matrix_landed(index, side):
        ref = held.at[sketch if side == 0 else twin, pl.ds(index * matrix_rows, matrix_rows)]
        pltpu.make_async_copy(ref, ref, matrix_recv.at[side, index]).wait()

    for to_lag in reversed(range(n_lag)):
        @pl.when(lag != to_lag)
        def _():
            matrix_copy(to_lag, 0).start()
            if to_lag == n_lag - 1:
                matrix_copy(to_lag, 1).start()
    own_hand = remote(own_rows, own_rows, matrix_send.at[1, 0], matrix_recv.at[1, lag], partner)
    own_hand.start()
    own.wait()

    @pl.when(jnp.logical_not(is_first))
    def _():
        down(0).start()

    @pl.when(jnp.logical_not(is_last))
    def _():
        up().start()

    pair.start()

    @pl.when(jnp.logical_not(is_first))
    def _():
        down(1).start()

    @pl.when(is_head)
    def _():
        loop(devices - 1, lambda index: pl.semaphore_signal(
            all_in, inc=1, device_id=device(index), device_id_type=MESH
        ))

    def outer(first, second, start, stop):
        def rows(slots):
            slot, count = slots
            return window[sketch, pl.ds(slot, count), :, start:stop].reshape(count * input_count, stop - start)
        return lax.dot_general(
            rows(first), rows(second), (((1,), (1,)), ((), ())), preferred_element_type=jnp.float32
        )

    inner = outer((later, step_count), (later, step_count), 0, half)
    gram[...] = jnp.zeros_like(gram)

    def shift(row):
        low, high = max(0, -row), min(lag_total, step_count - row)
        to = slice(low * input_count, high * input_count)
        at = slice((row + low) * input_count, (row + high) * input_count)
        gram[to, to] += inner[at, at]

    for row in range(step_count):
        shift(row)

    @pl.when(jnp.logical_not(is_first))
    def _():
        for row in range(-later, 0):
            shift(row)

    def cross(edge):
        for row in range(alone, step_count):
            count = (step_count - row) * input_count
            gram[0:count, count:depth] += 2.0 * edge[(row - alone) * input_count:, 0:(row - alone + 1) * input_count]

    def gather_matrix():
        for index in reversed(range(n_lag)):
            @pl.when(lag != index)
            def _():
                matrix_landed(index, 0)
                matrix_hand(index).start()

    @pl.when(jnp.logical_not(is_last))
    def _():
        gather_matrix()

    @pl.when(jnp.logical_not(is_first))
    def _():
        up().wait_recv()
        cross(outer((0, later), (later, later), cut, half))

    @pl.when(jnp.logical_not(is_last))
    def _():
        down(0).wait_recv()
        passed(0).start()
        cross(outer((later + alone, later), (later + step_count, later), 0, cut))

    whole = gram[...]
    high = whole.astype(jnp.bfloat16)
    rest = whole - high.astype(jnp.float32)
    middle = rest.astype(jnp.bfloat16)
    low = (rest - middle.astype(jnp.float32)).astype(jnp.bfloat16)

    @pl.when(is_last)
    def _():
        for index in range(n_lag - 1):
            matrix_landed(index, 0)
    for index in range(n_lag):
        matrix_landed(index, 1)
    mine = held[sketch].reshape(depth, columns)
    both = jnp.concatenate([mine, held[twin].reshape(depth, columns)], axis=1)
    product = jnp.dot(low, both, preferred_element_type=jnp.float32)
    product = product + jnp.dot(middle, both, preferred_element_type=jnp.float32)
    product = product + jnp.dot(high, both, preferred_element_type=jnp.float32)
    square = jnp.sum(product * both.astype(jnp.float32), axis=0, keepdims=True)
    sums[pl.ds(place, 1), :] = square[:, :columns]
    other[...] = square[:, columns:]

    def sum_copy(index, side):
        at = lax.rem(lag * n_probe + probe + index, n_lag * n_probe)
        to = {"lag": lax.div(at, n_probe), "probe": lax.rem(at, n_probe), "sketch": side}
        ref = sums.at[pl.ds(place, 1)]
        src = other if side is twin else ref
        return remote(src, ref, sum_send, sum_recv, to)

    @pl.when(jnp.logical_not(is_head))
    def _():
        pl.semaphore_wait(all_in, 1)

    loop(n_lag * n_probe - 1, lambda index: sum_copy(index + 1, sketch).start())
    loop(n_lag * n_probe, lambda index: sum_copy(index, twin).start())

    for row in range(step_count):
        weights[pl.ds(row * input_count, depth), row * columns:(row + 1) * columns] = mine

    tile = 256

    def multiply(side, first, last):
        for start in range(first, last, tile):
            block = window[side, pl.ds(later, step_count + later), :, pl.ds(start, tile)]
            product = lax.dot_general(
                block.reshape((step_count + later) * input_count, tile), weights[...], (((0,), (0,)), ((), ())),
                preferred_element_type=jnp.float32,
            )
            for row in range(step_count):
                raw[row, pl.ds(pl.multiple_of(side * half + start, tile), tile), :] = (
                    product[:, row * columns:(row + 1) * columns]
                )

    multiply(sketch, 0, cut)
    pair.wait()

    @pl.when(jnp.logical_not(is_last))
    def _():
        passed(0).wait_recv()

    multiply(twin, 0, cut)

    @pl.when(jnp.logical_not(is_last))
    def _():
        down(1).wait_recv()
        passed(1).start()

    multiply(sketch, cut, half)

    @pl.when(jnp.logical_not(is_last))
    def _():
        passed(1).wait_recv()

    multiply(twin, cut, half)

    @pl.when(jnp.logical_not(is_last))
    def _():
        passed(0).wait_send()
        passed(1).wait_send()
        up().wait_send()

    @pl.when(jnp.logical_not(is_first))
    def _():
        down(0).wait_send()
        down(1).wait_send()

    own_hand.wait_send()
    for index in range(n_lag):
        @pl.when(lag != index)
        def _():
            matrix_copy(index, 0).wait_send()
            if index == n_lag - 1:
                matrix_copy(index, 1).wait_send()

            @pl.when(jnp.logical_not(is_last))
            def _():
                matrix_hand(index).wait_send()
    landed = sums.at[pl.ds(0, devices - 1)]
    pltpu.make_async_copy(landed, landed, sum_send).wait()
    pltpu.make_async_copy(landed, landed, sum_recv).wait()
    cells = step_count * n_lag * half * n_sketch * n_probe
    mean = lax.max(jnp.sum(sums[...], axis=0, keepdims=True), 0.0) / cells
    factor[...] = jnp.broadcast_to(lax.rsqrt(mean + 1e-06), factor.shape)


def near(sizes, markov, test_matrix):
    n_lag, n_probe, n_sketch = sizes
    step_count, input_count, half = markov.shape
    matrix_rows, _, columns = test_matrix.shape
    lag_total = matrix_rows * n_lag
    later = lag_total - 1
    dma = pltpu.SemaphoreType.DMA
    return pl.pallas_call(
        functools.partial(near_kernel, sizes, half * 3 // 4),
        out_shape=[
            pltpu.VMEM((step_count, half * n_sketch, columns), jnp.float32),
            pltpu.VMEM((8, columns), jnp.float32),
        ],
        in_specs=[pl.BlockSpec(memory_space=pltpu.HBM)] * 2,
        out_specs=[pl.BlockSpec(memory_space=pltpu.VMEM)] * 2,
        scratch_shapes=[
            pltpu.VMEM((n_sketch, step_count + 2 * later, input_count, half), jnp.bfloat16),
            pltpu.VMEM((n_sketch, lag_total, input_count, columns), jnp.bfloat16),
            pltpu.VMEM(((step_count + later) * input_count, step_count * columns), jnp.bfloat16),
            pltpu.VMEM((lag_total * input_count, lag_total * input_count), jnp.float32),
            pltpu.VMEM((1, columns), jnp.float32),
            pltpu.VMEM((n_lag * n_probe * n_sketch, columns), jnp.float32),
            dma, dma, dma((2, n_lag)), dma((2, n_lag)), dma((n_lag,)), dma, dma,
            dma((2,)), dma((2,)), dma, dma, dma((2,)), dma((2,)), dma, dma,
            pltpu.SemaphoreType.REGULAR,
        ],
        compiler_params=pltpu.CompilerParams(
            collective_id=1, has_side_effects=True, vmem_limit_bytes=59 * 1024 * 1024
        ),
    )(markov, test_matrix)


def is_near(sizes, markov, test_matrix):
    n_lag, n_probe, n_sketch = sizes
    step_count, input_count, half = markov.shape
    lag_total = test_matrix.shape[0] * n_lag
    return n_sketch == 2 and n_lag > 1 and 1 < lag_total <= step_count and half % 512 == 0


def scale_kernel(raw, factor, out, held, sem):
    step_count, probes, columns = raw.shape
    pieces = 2
    part = probes // pieces
    copies = []
    gain = factor[0:1, :]
    for row in range(step_count):
        for piece in range(pieces):
            place = pl.ds(piece * part, part)
            held[row, place] = (raw[row, place] * gain).astype(held.dtype)
            copy = pltpu.make_async_copy(
                held.at[row, place], out.at[row, place], sem.at[row * pieces + piece]
            )
            copy.start()
            copies.append(copy)
    for copy in copies:
        copy.wait()


def scale(raw, factor):
    step_count, probes, columns = raw.shape
    return pl.pallas_call(
        scale_kernel,
        out_shape=jax.ShapeDtypeStruct(raw.shape, jnp.bfloat16),
        in_specs=[pl.BlockSpec(memory_space=pltpu.VMEM)] * 2,
        out_specs=pl.BlockSpec(memory_space=pltpu.HBM),
        scratch_shapes=[
            pltpu.VMEM(raw.shape, jnp.bfloat16),
            pltpu.SemaphoreType.DMA((step_count * 2,)),
        ],
        compiler_params=pltpu.CompilerParams(vmem_limit_bytes=16 * 1024 * 1024),
    )(raw, factor)


def local(sizes, markov, test_matrix):
    if is_near(sizes, markov, test_matrix):
        return scale(*near(sizes, markov, test_matrix))
    n_lag, n_probe, n_sketch = sizes
    step_count, input_count, half = markov.shape
    matrix_rows, _, columns = test_matrix.shape
    lag_total = matrix_rows * n_lag
    steps, pieces = plan(step_count, lag_total)
    count = max(len(pieces), 1)
    pairs = max(n_sketch - 1, 1)
    probes = half * n_sketch
    dma = pltpu.SemaphoreType.DMA
    raw, factor = pl.pallas_call(
        functools.partial(gather_kernel, sizes),
        out_shape=[
            pltpu.VMEM((step_count, probes, columns), jnp.float32),
            pltpu.VMEM((8, columns), jnp.float32),
        ],
        in_specs=[pl.BlockSpec(memory_space=pltpu.HBM)] * 2,
        out_specs=[pl.BlockSpec(memory_space=pltpu.VMEM)] * 2,
        scratch_shapes=[
            pltpu.VMEM((n_sketch, steps, input_count, half), jnp.bfloat16),
            pltpu.VMEM((lag_total, input_count, columns), jnp.bfloat16),
            pltpu.VMEM((steps * input_count, step_count * columns), jnp.bfloat16),
            pltpu.VMEM((n_lag * n_probe, columns), jnp.float32),
            dma, dma, dma, dma,
            dma((pairs,)), dma((pairs,)),
            dma((count,)), dma((count,)),
            dma((count, pairs)), dma((count, pairs)),
            dma, dma,
        ],
        compiler_params=pltpu.CompilerParams(
            collective_id=0, has_side_effects=True, vmem_limit_bytes=59 * 1024 * 1024
        ),
    )(markov, test_matrix)
    return scale(raw, factor)


def solution(mesh):
    sizes = tuple(mesh.shape[name] for name in ("lag", "probe", "sketch"))
    return jax.shard_map(
        functools.partial(local, sizes),
        mesh=mesh,
        in_specs=(P("lag", None, ("probe", "sketch")), P("lag", None, "sketch")),
        out_specs=P("lag", "probe", "sketch"),
        check_vma=False,
    )
```

```python
import functools

import jax
import jax.numpy as jnp
from jax import lax
from jax.experimental import pallas as pl
from jax.experimental.pallas import tpu as pltpu
from jax.sharding import PartitionSpec as P

MESH = pl.DeviceIdType.MESH
UNROLL = 32


def loop(count, body):
    if count <= UNROLL:
        for index in range(count):
            body(index)
    else:
        def step(index, carry):
            body(index)
            return carry
        lax.fori_loop(0, count, step, 0)


def plan(step_count, lag_total):
    steps = step_count + lag_total - 1
    blocks = (steps - 1) // step_count
    pieces = []
    for ahead in range(1, blocks + 1):
        used = min(step_count, steps - ahead * step_count)
        if blocks == 1:
            pieces += [(ahead, at, 1) for at in range(used)]
        else:
            pieces.append((ahead, 0, used))
    return steps, pieces


def gather_kernel(
    sizes, markov, matrix, raw, factor,
    window, held, weights, sums,
    own_sem, matrix_own_sem, matrix_send, matrix_recv,
    pair_send, pair_recv, lag_send, lag_recv, next_send, next_recv, sum_send, sum_recv,
):
    n_lag, n_probe, n_sketch = sizes
    step_count, input_count, half = markov.shape
    matrix_rows = matrix.shape[0]
    columns = matrix.shape[2]
    lag_total = matrix_rows * n_lag
    steps, pieces = plan(step_count, lag_total)
    lag = lax.axis_index("lag")
    probe = lax.axis_index("probe")
    sketch = lax.axis_index("sketch")
    flat = lag * n_probe + probe
    peers = n_lag * n_probe - 1

    def peer(index):
        other = lax.rem(flat + 1 + index, peers + 1)
        return {
            "lag": lax.div(other, n_probe),
            "probe": lax.rem(other, n_probe),
            "sketch": sketch,
        }

    def partner(index):
        return {"lag": lag, "probe": probe, "sketch": lax.rem(sketch + 1 + index, n_sketch)}

    def lag_peer(index):
        return {"lag": lax.rem(lag + 1 + index, n_lag), "probe": probe, "sketch": sketch}

    barrier = pltpu.get_barrier_semaphore()

    def greet(index):
        pl.semaphore_signal(barrier, inc=1, device_id=peer(index), device_id_type=MESH)

    for index in range(n_sketch - 1):
        pl.semaphore_signal(barrier, inc=1, device_id=partner(index), device_id_type=MESH)
    loop(peers, greet)

    own = pltpu.make_async_copy(markov, window.at[sketch, pl.ds(0, step_count)], own_sem)
    own.start()
    matrix_own = pltpu.make_async_copy(
        matrix, held.at[pl.ds(lag * matrix_rows, matrix_rows)], matrix_own_sem
    )
    matrix_own.start()
    weights[...] = jnp.zeros_like(weights)
    for ahead, at, count in pieces:
        @pl.when(lag + ahead >= n_lag)
        def _():
            place = pl.ds(ahead * step_count + at, count)
            window[:, place] = jnp.zeros((n_sketch, count, input_count, half), window.dtype)

    matrix_own.wait()
    pl.semaphore_wait(barrier, peers + n_sketch - 1)

    def lag_copy(number):
        ahead, at, count = pieces[number]
        return pltpu.make_async_remote_copy(
            src_ref=markov.at[pl.ds(at, count)],
            dst_ref=window.at[sketch, pl.ds(ahead * step_count + at, count)],
            send_sem=lag_send.at[number],
            recv_sem=lag_recv.at[number],
            device_id={"lag": lax.max(lag - ahead, 0), "probe": probe, "sketch": sketch},
            device_id_type=MESH,
        )

    def pair_copy(index):
        return pltpu.make_async_remote_copy(
            src_ref=markov,
            dst_ref=window.at[sketch, pl.ds(0, step_count)],
            send_sem=pair_send.at[index],
            recv_sem=pair_recv.at[index],
            device_id=partner(index),
            device_id_type=MESH,
        )

    def next_copy(number, index):
        ahead, at, count = pieces[number]
        place = window.at[sketch, pl.ds(ahead * step_count + at, count)]
        return pltpu.make_async_remote_copy(
            src_ref=place,
            dst_ref=place,
            send_sem=next_send.at[number, index],
            recv_sem=next_recv.at[number, index],
            device_id=partner(index),
            device_id_type=MESH,
        )

    def matrix_copy(index):
        return pltpu.make_async_remote_copy(
            src_ref=held.at[pl.ds(lag * matrix_rows, matrix_rows)],
            dst_ref=held.at[pl.ds(lag * matrix_rows, matrix_rows)],
            send_sem=matrix_send,
            recv_sem=matrix_recv,
            device_id=lag_peer(index),
            device_id_type=MESH,
        )

    loop(n_lag - 1, lambda index: matrix_copy(index).start())
    for number in range(0, 1):
        @pl.when(lag >= pieces[number][0])
        def _():
            lag_copy(number).start()
    for index in range(n_sketch - 1):
        pair_copy(index).start()
    for number in range(1, len(pieces)):
        @pl.when(lag >= pieces[number][0])
        def _():
            lag_copy(number).start()

    if n_lag > 1:
        arrived = held.at[pl.ds(0, (n_lag - 1) * matrix_rows)]
        pltpu.make_async_copy(arrived, arrived, matrix_recv).wait()
        pltpu.make_async_copy(arrived, arrived, matrix_send).wait()
    for row in range(step_count):
        weights[pl.ds(row * input_count, lag_total * input_count), row * columns:(row + 1) * columns] = (
            held[...].reshape(lag_total * input_count, columns)
        )

    def forward(number):
        @pl.when(lag + pieces[number][0] < n_lag)
        def _():
            lag_copy(number).wait_recv()
            for index in range(n_sketch - 1):
                next_copy(number, index).start()

    def landed(number):
        @pl.when(lag + pieces[number][0] < n_lag)
        def _():
            for index in range(n_sketch - 1):
                next_copy(number, index).wait()

    tile = min(256, half)
    group = 2 if step_count % 2 == 0 else 1

    def compute(first, total):
        depth = (lag_total + group - 1) * input_count
        weight = weights[pl.ds(first * input_count, depth), first * columns:(first + group) * columns]
        for side in range(n_sketch):
            def body(at, total):
                start = pl.multiple_of(at * tile, tile)
                block = window[side, pl.ds(first, lag_total + group - 1), :, pl.ds(start, tile)]
                product = lax.dot_general(
                    block.reshape(depth, tile), weight, (((0,), (0,)), ((), ())),
                    preferred_element_type=jnp.float32,
                )
                for row in range(group):
                    part = product[:, row * columns:(row + 1) * columns]
                    raw[first + row, pl.ds(side * half + start, tile), :] = part
                    total = total + jnp.sum((part * part).reshape(tile // 8, 8, columns), axis=0)
                return total
            total = lax.fori_loop(0, half // tile, body, total, unroll=depth <= 512)
        return total

    own.wait()
    total = jnp.zeros((8, columns), jnp.float32)
    done = 0
    paired = False
    for first in range(0, step_count, group):
        need = first + group - 1 + lag_total
        ready = done
        while ready < len(pieces) and pieces[ready][0] * step_count + pieces[ready][1] < need:
            forward(ready)
            ready += 1
        if not paired:
            for index in range(n_sketch - 1):
                pair_copy(index).wait()
            paired = True
        for number in range(done, ready):
            landed(number)
        done = ready
        total = compute(first, total)

    sums[pl.ds(flat, 1), :] = jnp.sum(total, axis=0, keepdims=True)

    def sum_copy(index):
        place = sums.at[pl.ds(flat, 1)]
        return pltpu.make_async_remote_copy(
            src_ref=place,
            dst_ref=place,
            send_sem=sum_send,
            recv_sem=sum_recv,
            device_id=peer(index),
            device_id_type=MESH,
        )

    loop(peers, lambda index: sum_copy(index).start())
    for number in range(len(pieces)):
        @pl.when(lag >= pieces[number][0])
        def _():
            lag_copy(number).wait_send()
    if peers:
        arrived = sums.at[pl.ds(0, peers)]
        pltpu.make_async_copy(arrived, arrived, sum_recv).wait()
        pltpu.make_async_copy(arrived, arrived, sum_send).wait()
    cells = step_count * n_lag * half * n_sketch * n_probe
    mean = jnp.sum(sums[...], axis=0, keepdims=True) / cells
    factor[...] = jnp.broadcast_to(lax.rsqrt(mean + 1e-06), factor.shape)


def near_kernel(
    sizes, cut, markov, matrix, raw, factor,
    window, held, weights, gram, other, sums,
    own_sem, matrix_own_sem, matrix_send, matrix_recv, twin_send, twin_recv, hand_send, pair_send, pair_recv,
    down_send, down_recv, up_send, up_recv, pass_send, pass_recv, sum_send, sum_recv, all_in,
):
    n_lag, n_probe, n_sketch = sizes
    step_count, input_count, half = markov.shape
    columns = matrix.shape[2]
    matrix_rows = matrix.shape[0]
    lag_total = matrix_rows * n_lag
    depth = lag_total * input_count
    later = lag_total - 1
    alone = step_count - later
    lag = lax.axis_index("lag")
    probe = lax.axis_index("probe")
    sketch = lax.axis_index("sketch")
    twin = 1 - sketch
    place = (lag * n_probe + probe) * n_sketch + sketch
    devices = n_lag * n_probe * n_sketch
    line = n_lag * n_sketch
    is_first = lag == 0
    is_last = lag == n_lag - 1
    is_head = place == devices - 1
    below = {"lag": lax.max(lag - 1, 0), "probe": probe, "sketch": sketch}
    above = {"lag": lax.min(lag + 1, n_lag - 1), "probe": probe, "sketch": sketch}
    partner = {"lag": lag, "probe": probe, "sketch": twin}

    def device(index):
        group = lax.div(index, n_sketch)
        return {
            "lag": lax.div(group, n_probe),
            "probe": lax.rem(group, n_probe),
            "sketch": lax.rem(index, n_sketch),
        }

    def on_line(index):
        at = lax.rem(lag * n_sketch + sketch + 1 + index, line)
        return {"lag": lax.div(at, n_sketch), "probe": probe, "sketch": lax.rem(at, n_sketch)}

    barrier = pltpu.get_barrier_semaphore()
    loop(line - 1, lambda index: pl.semaphore_signal(
        barrier, inc=1, device_id=on_line(index), device_id_type=MESH
    ))

    @pl.when(probe < n_probe - 1)
    def _():
        pl.semaphore_signal(barrier, inc=1, device_id=device(devices - 1), device_id_type=MESH)

    own_slots = pl.ds(later, step_count)
    next_slots = pl.ds(later + step_count, later)
    own_rows = held.at[sketch, pl.ds(lag * matrix_rows, matrix_rows)]
    matrix_own = pltpu.make_async_copy(matrix, own_rows, matrix_own_sem)
    matrix_own.start()
    own = pltpu.make_async_copy(markov, window.at[sketch, own_slots], own_sem)
    own.start()
    weights[...] = jnp.zeros_like(weights)

    @pl.when(is_last)
    def _():
        window[:, next_slots] = jnp.zeros((n_sketch, later, input_count, half), window.dtype)

    parts = (pl.ds(0, cut), pl.ds(cut, half - cut))

    def remote(src, dst, send, recv, to):
        return pltpu.make_async_remote_copy(
            src_ref=src, dst_ref=dst, send_sem=send, recv_sem=recv, device_id=to, device_id_type=MESH
        )

    def down(part):
        return remote(
            window.at[sketch, pl.ds(later, later), :, parts[part]],
            window.at[sketch, next_slots, :, parts[part]],
            down_send, down_recv.at[part], below,
        )

    def up():
        return remote(
            window.at[sketch, pl.ds(later + alone, later), :, parts[1]],
            window.at[sketch, pl.ds(0, later), :, parts[1]],
            up_send, up_recv, above,
        )

    def passed(part):
        ref = window.at[sketch, next_slots, :, parts[part]]
        return remote(ref, ref, pass_send, pass_recv.at[part], partner)

    pair = remote(
        window.at[sketch, own_slots], window.at[sketch, own_slots], pair_send, pair_recv, partner
    )

    matrix_own.wait()
    pl.semaphore_wait(barrier, lax.select(is_head, devices - 1, line - 1))

    def matrix_copy(to_lag):
        to = {"lag": to_lag, "probe": probe, "sketch": sketch}
        return remote(own_rows, own_rows, matrix_send, matrix_recv, to)

    matrix_twin = remote(
        own_rows, own_rows, twin_send, twin_recv, {"lag": n_lag - 1, "probe": probe, "sketch": twin}
    )
    matrix_hand = remote(held.at[sketch], held.at[sketch], hand_send, twin_recv, partner)
    for to_lag in reversed(range(n_lag)):
        @pl.when(lag != to_lag)
        def _():
            matrix_copy(to_lag).start()
        if to_lag == n_lag - 1:
            matrix_twin.start()
    own.wait()

    @pl.when(jnp.logical_not(is_first))
    def _():
        down(0).start()

    @pl.when(jnp.logical_not(is_last))
    def _():
        up().start()

    @pl.when(is_head)
    def _():
        loop(devices - 1, lambda index: pl.semaphore_signal(
            all_in, inc=1, device_id=device(index), device_id_type=MESH
        ))

    def outer(first, second, start, stop):
        def rows(slots):
            slot, count = slots
            return window[sketch, pl.ds(slot, count), :, start:stop].reshape(count * input_count, stop - start)
        return lax.dot_general(
            rows(first), rows(second), (((1,), (1,)), ((), ())), preferred_element_type=jnp.float32
        )

    inner = outer((later, step_count), (later, step_count), 0, half)
    gram[...] = jnp.zeros_like(gram)

    def shift(row):
        low, high = max(0, -row), min(lag_total, step_count - row)
        to = slice(low * input_count, high * input_count)
        at = slice((row + low) * input_count, (row + high) * input_count)
        gram[to, to] += inner[at, at]

    for row in range(step_count):
        shift(row)

    @pl.when(jnp.logical_not(is_first))
    def _():
        for row in range(-later, 0):
            shift(row)

    def cross(edge):
        for row in range(alone, step_count):
            count = (step_count - row) * input_count
            gram[0:count, count:depth] += 2.0 * edge[(row - alone) * input_count:, 0:(row - alone + 1) * input_count]

    others = held.at[sketch, pl.ds(0, lag_total - matrix_rows)]

    @pl.when(jnp.logical_not(is_last))
    def _():
        pltpu.make_async_copy(others, others, matrix_recv).wait()
        matrix_hand.start()

    @pl.when(jnp.logical_not(is_first))
    def _():
        up().wait_recv()
        cross(outer((0, later), (later, later), cut, half))

    @pl.when(jnp.logical_not(is_last))
    def _():
        down(0).wait_recv()
        cross(outer((later + alone, later), (later + step_count, later), 0, cut))

    whole = gram[...]
    high = whole.astype(jnp.bfloat16)
    rest = whole - high.astype(jnp.float32)
    middle = rest.astype(jnp.bfloat16)
    low = (rest - middle.astype(jnp.float32)).astype(jnp.bfloat16)

    @pl.when(is_last)
    def _():
        pltpu.make_async_copy(others, others, matrix_recv).wait()

    matrix_hand.wait_recv()
    mine = held[sketch].reshape(depth, columns)
    both = jnp.concatenate([mine, held[twin].reshape(depth, columns)], axis=1)
    product = jnp.dot(low, both, preferred_element_type=jnp.float32)
    product = product + jnp.dot(middle, both, preferred_element_type=jnp.float32)
    product = product + jnp.dot(high, both, preferred_element_type=jnp.float32)
    square = jnp.sum(product * both.astype(jnp.float32), axis=0, keepdims=True)
    sums[pl.ds(place, 1), :] = square[:, :columns]
    other[...] = square[:, columns:]

    def sum_copy(index, side):
        at = lax.rem(lag * n_probe + probe + index, n_lag * n_probe)
        to = {"lag": lax.div(at, n_probe), "probe": lax.rem(at, n_probe), "sketch": side}
        ref = sums.at[pl.ds(place, 1)]
        src = other if side is twin else ref
        return remote(src, ref, sum_send, sum_recv, to)

    @pl.when(jnp.logical_not(is_head))
    def _():
        pl.semaphore_wait(all_in, 1)

    loop(n_lag * n_probe - 1, lambda index: sum_copy(index + 1, sketch).start())
    loop(n_lag * n_probe, lambda index: sum_copy(index, twin).start())

    pair.start()

    @pl.when(jnp.logical_not(is_first))
    def _():
        down(1).start()

    @pl.when(jnp.logical_not(is_last))
    def _():
        passed(0).start()

    for row in range(step_count):
        weights[pl.ds(row * input_count, depth), row * columns:(row + 1) * columns] = mine

    tile = 256

    def multiply(side, first, last):
        for start in range(first, last, tile):
            block = window[side, pl.ds(later, step_count + later), :, pl.ds(start, tile)]
            product = lax.dot_general(
                block.reshape((step_count + later) * input_count, tile), weights[...], (((0,), (0,)), ((), ())),
                preferred_element_type=jnp.float32,
            )
            for row in range(step_count):
                raw[row, pl.ds(pl.multiple_of(side * half + start, tile), tile), :] = (
                    product[:, row * columns:(row + 1) * columns]
                )

    multiply(sketch, 0, cut)
    pair.wait()

    @pl.when(jnp.logical_not(is_last))
    def _():
        passed(0).wait_recv()

    multiply(twin, 0, cut)

    @pl.when(jnp.logical_not(is_last))
    def _():
        down(1).wait_recv()
        passed(1).start()

    multiply(sketch, cut, half)

    @pl.when(jnp.logical_not(is_last))
    def _():
        passed(1).wait_recv()

    multiply(twin, cut, half)

    received = window.at[sketch, next_slots]

    @pl.when(jnp.logical_not(is_last))
    def _():
        pltpu.make_async_copy(received, received, pass_send).wait()
        matrix_hand.wait_send()
        up().wait_send()

    @pl.when(jnp.logical_not(is_first))
    def _():
        pltpu.make_async_copy(received, received, down_send).wait()

    pltpu.make_async_copy(others, others, matrix_send).wait()
    matrix_twin.wait_send()
    landed = sums.at[pl.ds(0, devices - 1)]
    pltpu.make_async_copy(landed, landed, sum_send).wait()
    pltpu.make_async_copy(landed, landed, sum_recv).wait()
    cells = step_count * n_lag * half * n_sketch * n_probe
    mean = lax.max(jnp.sum(sums[...], axis=0, keepdims=True), 0.0) / cells
    factor[...] = jnp.broadcast_to(lax.rsqrt(mean + 1e-06), factor.shape)


def near(sizes, markov, test_matrix):
    n_lag, n_probe, n_sketch = sizes
    step_count, input_count, half = markov.shape
    matrix_rows, _, columns = test_matrix.shape
    lag_total = matrix_rows * n_lag
    later = lag_total - 1
    dma = pltpu.SemaphoreType.DMA
    return pl.pallas_call(
        functools.partial(near_kernel, sizes, half * 3 // 4),
        out_shape=[
            pltpu.VMEM((step_count, half * n_sketch, columns), jnp.float32),
            pltpu.VMEM((8, columns), jnp.float32),
        ],
        in_specs=[pl.BlockSpec(memory_space=pltpu.HBM)] * 2,
        out_specs=[pl.BlockSpec(memory_space=pltpu.VMEM)] * 2,
        scratch_shapes=[
            pltpu.VMEM((n_sketch, step_count + 2 * later, input_count, half), jnp.bfloat16),
            pltpu.VMEM((n_sketch, lag_total, input_count, columns), jnp.bfloat16),
            pltpu.VMEM(((step_count + later) * input_count, step_count * columns), jnp.bfloat16),
            pltpu.VMEM((lag_total * input_count, lag_total * input_count), jnp.float32),
            pltpu.VMEM((1, columns), jnp.float32),
            pltpu.VMEM((n_lag * n_probe * n_sketch, columns), jnp.float32),
            dma, dma, dma, dma, dma, dma, dma, dma, dma,
            dma, dma((2,)), dma, dma, dma, dma((2,)), dma, dma,
            pltpu.SemaphoreType.REGULAR,
        ],
        compiler_params=pltpu.CompilerParams(
            collective_id=1, has_side_effects=True, vmem_limit_bytes=59 * 1024 * 1024
        ),
    )(markov, test_matrix)


def is_near(sizes, markov, test_matrix):
    n_lag, n_probe, n_sketch = sizes
    step_count, input_count, half = markov.shape
    lag_total = test_matrix.shape[0] * n_lag
    return n_sketch == 2 and n_lag > 1 and 1 < lag_total <= step_count and half % 512 == 0


def scale_kernel(raw, factor, out, held, sem):
    step_count, probes, columns = raw.shape
    pieces = 2
    part = probes // pieces
    gain = factor[0:1, :]
    for row in range(step_count):
        for piece in range(pieces):
            place = pl.ds(piece * part, part)
            held[row, place] = (raw[row, place] * gain).astype(held.dtype)
            pltpu.make_async_copy(held.at[row, place], out.at[row, place], sem).start()
    pltpu.make_async_copy(held, out, sem).wait()


def scale(raw, factor):
    step_count, probes, columns = raw.shape
    return pl.pallas_call(
        scale_kernel,
        out_shape=jax.ShapeDtypeStruct(raw.shape, jnp.bfloat16),
        in_specs=[pl.BlockSpec(memory_space=pltpu.VMEM)] * 2,
        out_specs=pl.BlockSpec(memory_space=pltpu.HBM),
        scratch_shapes=[
            pltpu.VMEM(raw.shape, jnp.bfloat16),
            pltpu.SemaphoreType.DMA,
        ],
        compiler_params=pltpu.CompilerParams(vmem_limit_bytes=16 * 1024 * 1024),
    )(raw, factor)


def local(sizes, markov, test_matrix):
    if is_near(sizes, markov, test_matrix):
        return scale(*near(sizes, markov, test_matrix))
    n_lag, n_probe, n_sketch = sizes
    step_count, input_count, half = markov.shape
    matrix_rows, _, columns = test_matrix.shape
    lag_total = matrix_rows * n_lag
    steps, pieces = plan(step_count, lag_total)
    count = max(len(pieces), 1)
    pairs = max(n_sketch - 1, 1)
    probes = half * n_sketch
    dma = pltpu.SemaphoreType.DMA
    raw, factor = pl.pallas_call(
        functools.partial(gather_kernel, sizes),
        out_shape=[
            pltpu.VMEM((step_count, probes, columns), jnp.float32),
            pltpu.VMEM((8, columns), jnp.float32),
        ],
        in_specs=[pl.BlockSpec(memory_space=pltpu.HBM)] * 2,
        out_specs=[pl.BlockSpec(memory_space=pltpu.VMEM)] * 2,
        scratch_shapes=[
            pltpu.VMEM((n_sketch, steps, input_count, half), jnp.bfloat16),
            pltpu.VMEM((lag_total, input_count, columns), jnp.bfloat16),
            pltpu.VMEM((steps * input_count, step_count * columns), jnp.bfloat16),
            pltpu.VMEM((n_lag * n_probe, columns), jnp.float32),
            dma, dma, dma, dma,
            dma((pairs,)), dma((pairs,)),
            dma((count,)), dma((count,)),
            dma((count, pairs)), dma((count, pairs)),
            dma, dma,
        ],
        compiler_params=pltpu.CompilerParams(
            collective_id=0, has_side_effects=True, vmem_limit_bytes=59 * 1024 * 1024
        ),
    )(markov, test_matrix)
    return scale(raw, factor)


def solution(mesh):
    sizes = tuple(mesh.shape[name] for name in ("lag", "probe", "sketch"))
    return jax.shard_map(
        functools.partial(local, sizes),
        mesh=mesh,
        in_specs=(P("lag", None, ("probe", "sketch")), P("lag", None, "sketch")),
        out_specs=P("lag", "probe", "sketch"),
        check_vma=False,
    )
```

```python
import functools

import jax
import jax.numpy as jnp
from jax import lax
from jax.experimental import pallas as pl
from jax.experimental.pallas import tpu as pltpu
from jax.sharding import PartitionSpec as P

MESH = pl.DeviceIdType.MESH
UNROLL = 32


def loop(count, body):
    if count <= UNROLL:
        for index in range(count):
            body(index)
    else:
        def step(index, carry):
            body(index)
            return carry
        lax.fori_loop(0, count, step, 0)


def plan(step_count, lag_total):
    steps = step_count + lag_total - 1
    blocks = (steps - 1) // step_count
    pieces = []
    for ahead in range(1, blocks + 1):
        used = min(step_count, steps - ahead * step_count)
        if blocks == 1:
            pieces += [(ahead, at, 1) for at in range(used)]
        else:
            pieces.append((ahead, 0, used))
    return steps, pieces


def gather_kernel(
    sizes, markov, matrix, raw, factor,
    window, held, weights, sums,
    own_sem, matrix_own_sem, matrix_send, matrix_recv,
    pair_send, pair_recv, lag_send, lag_recv, next_send, next_recv, sum_send, sum_recv,
):
    n_lag, n_probe, n_sketch = sizes
    step_count, input_count, half = markov.shape
    matrix_rows = matrix.shape[0]
    columns = matrix.shape[2]
    lag_total = matrix_rows * n_lag
    steps, pieces = plan(step_count, lag_total)
    lag = lax.axis_index("lag")
    probe = lax.axis_index("probe")
    sketch = lax.axis_index("sketch")
    flat = lag * n_probe + probe
    peers = n_lag * n_probe - 1

    def peer(index):
        other = lax.rem(flat + 1 + index, peers + 1)
        return {
            "lag": lax.div(other, n_probe),
            "probe": lax.rem(other, n_probe),
            "sketch": sketch,
        }

    def partner(index):
        return {"lag": lag, "probe": probe, "sketch": lax.rem(sketch + 1 + index, n_sketch)}

    def lag_peer(index):
        return {"lag": lax.rem(lag + 1 + index, n_lag), "probe": probe, "sketch": sketch}

    barrier = pltpu.get_barrier_semaphore()

    def greet(index):
        pl.semaphore_signal(barrier, inc=1, device_id=peer(index), device_id_type=MESH)

    for index in range(n_sketch - 1):
        pl.semaphore_signal(barrier, inc=1, device_id=partner(index), device_id_type=MESH)
    loop(peers, greet)

    own = pltpu.make_async_copy(markov, window.at[sketch, pl.ds(0, step_count)], own_sem)
    own.start()
    matrix_own = pltpu.make_async_copy(
        matrix, held.at[pl.ds(lag * matrix_rows, matrix_rows)], matrix_own_sem
    )
    matrix_own.start()
    weights[...] = jnp.zeros_like(weights)
    for ahead, at, count in pieces:
        @pl.when(lag + ahead >= n_lag)
        def _():
            place = pl.ds(ahead * step_count + at, count)
            window[:, place] = jnp.zeros((n_sketch, count, input_count, half), window.dtype)

    matrix_own.wait()
    pl.semaphore_wait(barrier, peers + n_sketch - 1)

    def lag_copy(number):
        ahead, at, count = pieces[number]
        return pltpu.make_async_remote_copy(
            src_ref=markov.at[pl.ds(at, count)],
            dst_ref=window.at[sketch, pl.ds(ahead * step_count + at, count)],
            send_sem=lag_send.at[number],
            recv_sem=lag_recv.at[number],
            device_id={"lag": lax.max(lag - ahead, 0), "probe": probe, "sketch": sketch},
            device_id_type=MESH,
        )

    def pair_copy(index):
        return pltpu.make_async_remote_copy(
            src_ref=markov,
            dst_ref=window.at[sketch, pl.ds(0, step_count)],
            send_sem=pair_send.at[index],
            recv_sem=pair_recv.at[index],
            device_id=partner(index),
            device_id_type=MESH,
        )

    def next_copy(number, index):
        ahead, at, count = pieces[number]
        place = window.at[sketch, pl.ds(ahead * step_count + at, count)]
        return pltpu.make_async_remote_copy(
            src_ref=place,
            dst_ref=place,
            send_sem=next_send.at[number, index],
            recv_sem=next_recv.at[number, index],
            device_id=partner(index),
            device_id_type=MESH,
        )

    def matrix_copy(index):
        return pltpu.make_async_remote_copy(
            src_ref=held.at[pl.ds(lag * matrix_rows, matrix_rows)],
            dst_ref=held.at[pl.ds(lag * matrix_rows, matrix_rows)],
            send_sem=matrix_send,
            recv_sem=matrix_recv,
            device_id=lag_peer(index),
            device_id_type=MESH,
        )

    loop(n_lag - 1, lambda index: matrix_copy(index).start())
    for number in range(0, 1):
        @pl.when(lag >= pieces[number][0])
        def _():
            lag_copy(number).start()
    for index in range(n_sketch - 1):
        pair_copy(index).start()
    for number in range(1, len(pieces)):
        @pl.when(lag >= pieces[number][0])
        def _():
            lag_copy(number).start()

    if n_lag > 1:
        arrived = held.at[pl.ds(0, (n_lag - 1) * matrix_rows)]
        pltpu.make_async_copy(arrived, arrived, matrix_recv).wait()
        pltpu.make_async_copy(arrived, arrived, matrix_send).wait()
    for row in range(step_count):
        weights[pl.ds(row * input_count, lag_total * input_count), row * columns:(row + 1) * columns] = (
            held[...].reshape(lag_total * input_count, columns)
        )

    def forward(number):
        @pl.when(lag + pieces[number][0] < n_lag)
        def _():
            lag_copy(number).wait_recv()
            for index in range(n_sketch - 1):
                next_copy(number, index).start()

    def landed(number):
        @pl.when(lag + pieces[number][0] < n_lag)
        def _():
            for index in range(n_sketch - 1):
                next_copy(number, index).wait()

    tile = min(256, half)
    group = 2 if step_count % 2 == 0 else 1

    def compute(first, total):
        depth = (lag_total + group - 1) * input_count
        weight = weights[pl.ds(first * input_count, depth), first * columns:(first + group) * columns]
        for side in range(n_sketch):
            def body(at, total):
                start = pl.multiple_of(at * tile, tile)
                block = window[side, pl.ds(first, lag_total + group - 1), :, pl.ds(start, tile)]
                product = lax.dot_general(
                    block.reshape(depth, tile), weight, (((0,), (0,)), ((), ())),
                    preferred_element_type=jnp.float32,
                )
                for row in range(group):
                    part = product[:, row * columns:(row + 1) * columns]
                    raw[first + row, pl.ds(side * half + start, tile), :] = part
                    total = total + jnp.sum((part * part).reshape(tile // 8, 8, columns), axis=0)
                return total
            total = lax.fori_loop(0, half // tile, body, total, unroll=depth <= 512)
        return total

    own.wait()
    total = jnp.zeros((8, columns), jnp.float32)
    done = 0
    paired = False
    for first in range(0, step_count, group):
        need = first + group - 1 + lag_total
        ready = done
        while ready < len(pieces) and pieces[ready][0] * step_count + pieces[ready][1] < need:
            forward(ready)
            ready += 1
        if not paired:
            for index in range(n_sketch - 1):
                pair_copy(index).wait()
            paired = True
        for number in range(done, ready):
            landed(number)
        done = ready
        total = compute(first, total)

    sums[pl.ds(flat, 1), :] = jnp.sum(total, axis=0, keepdims=True)

    def sum_copy(index):
        place = sums.at[pl.ds(flat, 1)]
        return pltpu.make_async_remote_copy(
            src_ref=place,
            dst_ref=place,
            send_sem=sum_send,
            recv_sem=sum_recv,
            device_id=peer(index),
            device_id_type=MESH,
        )

    loop(peers, lambda index: sum_copy(index).start())
    for number in range(len(pieces)):
        @pl.when(lag >= pieces[number][0])
        def _():
            lag_copy(number).wait_send()
    if peers:
        arrived = sums.at[pl.ds(0, peers)]
        pltpu.make_async_copy(arrived, arrived, sum_recv).wait()
        pltpu.make_async_copy(arrived, arrived, sum_send).wait()
    cells = step_count * n_lag * half * n_sketch * n_probe
    mean = jnp.sum(sums[...], axis=0, keepdims=True) / cells
    factor[...] = jnp.broadcast_to(lax.rsqrt(mean + 1e-06), factor.shape)


def near_kernel(
    sizes, cut, markov, matrix, raw, factor,
    window, held, weights, gram, other, sums,
    own_sem, matrix_own_sem, matrix_send, matrix_recv, twin_send, twin_recv, hand_send, pair_send, pair_recv,
    down_send, down_recv, up_send, up_recv, pass_send, pass_recv, sum_send, sum_recv, all_in, risen,
):
    n_lag, n_probe, n_sketch = sizes
    step_count, input_count, half = markov.shape
    columns = matrix.shape[2]
    matrix_rows = matrix.shape[0]
    lag_total = matrix_rows * n_lag
    depth = lag_total * input_count
    later = lag_total - 1
    alone = step_count - later
    lag = lax.axis_index("lag")
    probe = lax.axis_index("probe")
    sketch = lax.axis_index("sketch")
    twin = 1 - sketch
    place = (lag * n_probe + probe) * n_sketch + sketch
    devices = n_lag * n_probe * n_sketch
    is_first = lag == 0
    is_last = lag == n_lag - 1
    is_head = place == devices - 1
    below = {"lag": lax.max(lag - 1, 0), "probe": probe, "sketch": sketch}
    above = {"lag": lax.min(lag + 1, n_lag - 1), "probe": probe, "sketch": sketch}
    partner = {"lag": lag, "probe": probe, "sketch": twin}

    def device(index):
        group = lax.div(index, n_sketch)
        return {
            "lag": lax.div(group, n_probe),
            "probe": lax.rem(group, n_probe),
            "sketch": lax.rem(index, n_sketch),
        }

    last = n_lag - 1

    def at_lag(to_lag, side):
        return {"lag": to_lag, "probe": probe, "sketch": side}

    barrier = pltpu.get_barrier_semaphore()

    def greet(to):
        pl.semaphore_signal(barrier, inc=1, device_id=to, device_id_type=MESH)

    @pl.when(jnp.logical_not(is_first))
    def _():
        greet(at_lag(0, sketch))

    @pl.when(is_last)
    def _():
        greet(at_lag(0, twin))

    @pl.when(jnp.logical_not(is_last))
    def _():
        greet(at_lag(last, twin))

    for to_lag in range(1, n_lag):
        @pl.when(lag < to_lag)
        def _():
            greet(at_lag(to_lag, sketch))

    greet(partner)

    @pl.when(probe < n_probe - 1)
    def _():
        greet(device(devices - 1))

    expected = lax.select(is_first, n_lag + 1, lax.select(is_last, 2 * n_lag - 1, lag + 1))

    own_slots = pl.ds(later, step_count)
    next_slots = pl.ds(later + step_count, later)
    own_rows = held.at[sketch, pl.ds(lag * matrix_rows, matrix_rows)]
    matrix_own = pltpu.make_async_copy(matrix, own_rows, matrix_own_sem)
    matrix_own.start()
    own = pltpu.make_async_copy(markov, window.at[sketch, own_slots], own_sem)
    own.start()
    weights[...] = jnp.zeros_like(weights)

    @pl.when(is_last)
    def _():
        window[:, next_slots] = jnp.zeros((n_sketch, later, input_count, half), window.dtype)

    parts = (pl.ds(0, cut), pl.ds(cut, half - cut))

    def remote(src, dst, send, recv, to):
        return pltpu.make_async_remote_copy(
            src_ref=src, dst_ref=dst, send_sem=send, recv_sem=recv, device_id=to, device_id_type=MESH
        )

    def down(part):
        return remote(
            window.at[sketch, pl.ds(later, later), :, parts[part]],
            window.at[sketch, next_slots, :, parts[part]],
            down_send, down_recv.at[part], below,
        )

    def up():
        return remote(
            window.at[sketch, pl.ds(later + alone, later), :, parts[1]],
            window.at[sketch, pl.ds(0, later), :, parts[1]],
            up_send, up_recv, above,
        )

    def passed(part):
        ref = window.at[sketch, next_slots, :, parts[part]]
        return remote(ref, ref, pass_send, pass_recv.at[part], partner)

    pair = remote(
        window.at[sketch, own_slots], window.at[sketch, own_slots], pair_send, pair_recv, partner
    )

    def outer(first, second, start, stop):
        def rows(slots):
            slot, count = slots
            return window[sketch, pl.ds(slot, count), :, start:stop].reshape(count * input_count, stop - start)
        return lax.dot_general(
            rows(first), rows(second), (((1,), (1,)), ((), ())), preferred_element_type=jnp.float32
        )

    def own_gram():
        inner = outer((later, step_count), (later, step_count), 0, half)
        gram[...] = jnp.zeros_like(gram)

        def shift(row):
            low, high = max(0, -row), min(lag_total, step_count - row)
            to = slice(low * input_count, high * input_count)
            at = slice((row + low) * input_count, (row + high) * input_count)
            gram[to, to] += inner[at, at]

        for row in range(step_count):
            shift(row)

        @pl.when(jnp.logical_not(is_first))
        def _():
            for row in range(-later, 0):
                shift(row)

    def matrix_copy(to_lag):
        return remote(own_rows, own_rows, matrix_send, matrix_recv, at_lag(to_lag, sketch))

    matrix_twin = remote(own_rows, own_rows, twin_send, twin_recv, at_lag(last, twin))
    matrix_hand = remote(held.at[sketch], held.at[sketch], hand_send, twin_recv, partner)

    def rise(to_lag, semaphore, side):
        pl.semaphore_signal(semaphore, inc=1, device_id=at_lag(to_lag, side), device_id_type=MESH)

    @pl.when(is_first)
    def _():
        own.wait()
        own_gram()

    pl.semaphore_wait(barrier, lax.select(is_head, devices - 1, expected))
    for from_lag in range(2, n_lag):
        @pl.when(lag == from_lag)
        def _():
            for to_lag in range(1, from_lag):
                rise(to_lag, risen.at[from_lag], sketch)
                if from_lag == last:
                    rise(to_lag, risen.at[0], twin)

    matrix_own.wait()

    @pl.when(is_first)
    def _():
        matrix_copy(last).start()
        matrix_twin.start()
        for to_lag in reversed(range(1, last)):
            matrix_copy(to_lag).start()
        up().start()

    @pl.when(jnp.logical_not(is_first))
    def _():
        own.wait()
        for to_lag in range(last):
            @pl.when(lag > to_lag)
            def _():
                matrix_copy(to_lag).start()
        down(0).start()

        @pl.when(is_last)
        def _():
            matrix_twin.start()

        own_gram()

    for here in range(1, last):
        @pl.when(lag == here)
        def _():
            for to_lag in range(here + 1, n_lag):
                pl.semaphore_wait(risen.at[to_lag], 1)
                if to_lag == here + 1:
                    up().start()
                matrix_copy(to_lag).start()
            pl.semaphore_wait(risen.at[0], 1)
            matrix_twin.start()

    @pl.when(is_head)
    def _():
        loop(devices - 1, lambda index: pl.semaphore_signal(
            all_in, inc=1, device_id=device(index), device_id_type=MESH
        ))

    def cross(edge):
        for row in range(alone, step_count):
            count = (step_count - row) * input_count
            gram[0:count, count:depth] += 2.0 * edge[(row - alone) * input_count:, 0:(row - alone + 1) * input_count]

    others = held.at[sketch, pl.ds(0, lag_total - matrix_rows)]

    @pl.when(jnp.logical_not(is_last))
    def _():
        pltpu.make_async_copy(others, others, matrix_recv).wait()
        matrix_hand.start()

    @pl.when(jnp.logical_not(jnp.logical_or(is_first, is_last)))
    def _():
        down(1).start()

    @pl.when(jnp.logical_not(is_first))
    def _():
        up().wait_recv()
        cross(outer((0, later), (later, later), cut, half))

    @pl.when(jnp.logical_not(is_last))
    def _():
        down(0).wait_recv()
        cross(outer((later + alone, later), (later + step_count, later), 0, cut))

    whole = gram[...]
    high = whole.astype(jnp.bfloat16)
    rest = whole - high.astype(jnp.float32)
    middle = rest.astype(jnp.bfloat16)
    low = (rest - middle.astype(jnp.float32)).astype(jnp.bfloat16)

    @pl.when(is_last)
    def _():
        pltpu.make_async_copy(others, others, matrix_recv).wait()

    matrix_hand.wait_recv()
    mine = held[sketch].reshape(depth, columns)
    both = jnp.concatenate([mine, held[twin].reshape(depth, columns)], axis=1)
    product = jnp.dot(low, both, preferred_element_type=jnp.float32)
    product = product + jnp.dot(middle, both, preferred_element_type=jnp.float32)
    product = product + jnp.dot(high, both, preferred_element_type=jnp.float32)
    square = jnp.sum(product * both.astype(jnp.float32), axis=0, keepdims=True)
    sums[pl.ds(place, 1), :] = square[:, :columns]
    other[...] = square[:, columns:]

    def sum_copy(index, side):
        at = lax.rem(lag * n_probe + probe + index, n_lag * n_probe)
        to = {"lag": lax.div(at, n_probe), "probe": lax.rem(at, n_probe), "sketch": side}
        ref = sums.at[pl.ds(place, 1)]
        src = other if side is twin else ref
        return remote(src, ref, sum_send, sum_recv, to)

    @pl.when(jnp.logical_not(is_head))
    def _():
        pl.semaphore_wait(all_in, 1)

    loop(n_lag * n_probe - 1, lambda index: sum_copy(index + 1, sketch).start())
    loop(n_lag * n_probe, lambda index: sum_copy(index, twin).start())

    @pl.when(is_last)
    def _():
        down(1).start()

    pair.start()

    @pl.when(jnp.logical_not(is_last))
    def _():
        passed(0).start()

    for row in range(step_count):
        weights[pl.ds(row * input_count, depth), row * columns:(row + 1) * columns] = mine

    tile = 128

    def multiply(side, first, last):
        for start in range(first, last, tile):
            block = window[side, pl.ds(later, step_count + later), :, pl.ds(start, tile)]
            product = lax.dot_general(
                block.reshape((step_count + later) * input_count, tile), weights[...], (((0,), (0,)), ((), ())),
                preferred_element_type=jnp.float32,
            )
            for row in range(step_count):
                raw[row, pl.ds(pl.multiple_of(side * half + start, tile), tile), :] = (
                    product[:, row * columns:(row + 1) * columns]
                )

    multiply(sketch, 0, cut)
    pair.wait()

    @pl.when(jnp.logical_not(is_last))
    def _():
        passed(0).wait_recv()

    multiply(twin, 0, cut)

    @pl.when(jnp.logical_not(is_last))
    def _():
        down(1).wait_recv()
        passed(1).start()

    multiply(sketch, cut, half)

    @pl.when(jnp.logical_not(is_last))
    def _():
        passed(1).wait_recv()

    multiply(twin, cut, half)

    received = window.at[sketch, next_slots]

    @pl.when(jnp.logical_not(is_last))
    def _():
        pltpu.make_async_copy(received, received, pass_send).wait()
        matrix_hand.wait_send()
        up().wait_send()

    @pl.when(jnp.logical_not(is_first))
    def _():
        pltpu.make_async_copy(received, received, down_send).wait()

    pltpu.make_async_copy(others, others, matrix_send).wait()
    matrix_twin.wait_send()
    landed = sums.at[pl.ds(0, devices - 1)]
    pltpu.make_async_copy(landed, landed, sum_send).wait()
    pltpu.make_async_copy(landed, landed, sum_recv).wait()
    cells = step_count * n_lag * half * n_sketch * n_probe
    mean = lax.max(jnp.sum(sums[...], axis=0, keepdims=True), 0.0) / cells
    factor[...] = jnp.broadcast_to(lax.rsqrt(mean + 1e-06), factor.shape)


def near(sizes, markov, test_matrix):
    n_lag, n_probe, n_sketch = sizes
    step_count, input_count, half = markov.shape
    matrix_rows, _, columns = test_matrix.shape
    lag_total = matrix_rows * n_lag
    later = lag_total - 1
    dma = pltpu.SemaphoreType.DMA
    return pl.pallas_call(
        functools.partial(near_kernel, sizes, half * 5 // 8),
        out_shape=[
            pltpu.VMEM((step_count, half * n_sketch, columns), jnp.float32),
            pltpu.VMEM((8, columns), jnp.float32),
        ],
        in_specs=[pl.BlockSpec(memory_space=pltpu.HBM)] * 2,
        out_specs=[pl.BlockSpec(memory_space=pltpu.VMEM)] * 2,
        scratch_shapes=[
            pltpu.VMEM((n_sketch, step_count + 2 * later, input_count, half), jnp.bfloat16),
            pltpu.VMEM((n_sketch, lag_total, input_count, columns), jnp.bfloat16),
            pltpu.VMEM(((step_count + later) * input_count, step_count * columns), jnp.bfloat16),
            pltpu.VMEM((lag_total * input_count, lag_total * input_count), jnp.float32),
            pltpu.VMEM((1, columns), jnp.float32),
            pltpu.VMEM((n_lag * n_probe * n_sketch, columns), jnp.float32),
            dma, dma, dma, dma, dma, dma, dma, dma, dma,
            dma, dma((2,)), dma, dma, dma, dma((2,)), dma, dma,
            pltpu.SemaphoreType.REGULAR,
            pltpu.SemaphoreType.REGULAR((n_lag,)),
        ],
        compiler_params=pltpu.CompilerParams(
            collective_id=1, has_side_effects=True, vmem_limit_bytes=59 * 1024 * 1024
        ),
    )(markov, test_matrix)


def is_near(sizes, markov, test_matrix):
    n_lag, n_probe, n_sketch = sizes
    step_count, input_count, half = markov.shape
    lag_total = test_matrix.shape[0] * n_lag
    return n_sketch == 2 and n_lag > 1 and 1 < lag_total <= step_count and half % 512 == 0


def scale_kernel(raw, factor, out, held, sem):
    step_count, probes, columns = raw.shape
    pieces = 2
    part = probes // pieces
    gain = factor[0:1, :]
    for row in range(step_count):
        for piece in range(pieces):
            place = pl.ds(piece * part, part)
            held[row, place] = (raw[row, place] * gain).astype(held.dtype)
            pltpu.make_async_copy(held.at[row, place], out.at[row, place], sem).start()
    pltpu.make_async_copy(held, out, sem).wait()


def scale(raw, factor):
    step_count, probes, columns = raw.shape
    return pl.pallas_call(
        scale_kernel,
        out_shape=jax.ShapeDtypeStruct(raw.shape, jnp.bfloat16),
        in_specs=[pl.BlockSpec(memory_space=pltpu.VMEM)] * 2,
        out_specs=pl.BlockSpec(memory_space=pltpu.HBM),
        scratch_shapes=[
            pltpu.VMEM(raw.shape, jnp.bfloat16),
            pltpu.SemaphoreType.DMA,
        ],
        compiler_params=pltpu.CompilerParams(vmem_limit_bytes=16 * 1024 * 1024),
    )(raw, factor)


def local(sizes, markov, test_matrix):
    if is_near(sizes, markov, test_matrix):
        return scale(*near(sizes, markov, test_matrix))
    n_lag, n_probe, n_sketch = sizes
    step_count, input_count, half = markov.shape
    matrix_rows, _, columns = test_matrix.shape
    lag_total = matrix_rows * n_lag
    steps, pieces = plan(step_count, lag_total)
    count = max(len(pieces), 1)
    pairs = max(n_sketch - 1, 1)
    probes = half * n_sketch
    dma = pltpu.SemaphoreType.DMA
    raw, factor = pl.pallas_call(
        functools.partial(gather_kernel, sizes),
        out_shape=[
            pltpu.VMEM((step_count, probes, columns), jnp.float32),
            pltpu.VMEM((8, columns), jnp.float32),
        ],
        in_specs=[pl.BlockSpec(memory_space=pltpu.HBM)] * 2,
        out_specs=[pl.BlockSpec(memory_space=pltpu.VMEM)] * 2,
        scratch_shapes=[
            pltpu.VMEM((n_sketch, steps, input_count, half), jnp.bfloat16),
            pltpu.VMEM((lag_total, input_count, columns), jnp.bfloat16),
            pltpu.VMEM((steps * input_count, step_count * columns), jnp.bfloat16),
            pltpu.VMEM((n_lag * n_probe, columns), jnp.float32),
            dma, dma, dma, dma,
            dma((pairs,)), dma((pairs,)),
            dma((count,)), dma((count,)),
            dma((count, pairs)), dma((count, pairs)),
            dma, dma,
        ],
        compiler_params=pltpu.CompilerParams(
            collective_id=0, has_side_effects=True, vmem_limit_bytes=59 * 1024 * 1024
        ),
    )(markov, test_matrix)
    return scale(raw, factor)


def solution(mesh):
    sizes = tuple(mesh.shape[name] for name in ("lag", "probe", "sketch"))
    return jax.shard_map(
        functools.partial(local, sizes),
        mesh=mesh,
        in_specs=(P("lag", None, ("probe", "sketch")), P("lag", None, "sketch")),
        out_specs=P("lag", "probe", "sketch"),
        check_vma=False,
    )
```

```python
import functools

import jax
import jax.numpy as jnp
from jax import lax
from jax.experimental import pallas as pl
from jax.experimental.pallas import tpu as pltpu
from jax.sharding import PartitionSpec as P

MESH = pl.DeviceIdType.MESH
UNROLL = 32


def loop(count, body):
    if count <= UNROLL:
        for index in range(count):
            body(index)
    else:
        def step(index, carry):
            body(index)
            return carry
        lax.fori_loop(0, count, step, 0)


def plan(step_count, lag_total):
    steps = step_count + lag_total - 1
    blocks = (steps - 1) // step_count
    pieces = []
    for ahead in range(1, blocks + 1):
        used = min(step_count, steps - ahead * step_count)
        if blocks == 1:
            pieces += [(ahead, at, 1) for at in range(used)]
        else:
            pieces.append((ahead, 0, used))
    return steps, pieces


def gather_kernel(
    sizes, markov, matrix, raw, factor,
    window, held, weights, sums,
    own_sem, matrix_own_sem, matrix_send, matrix_recv,
    pair_send, pair_recv, lag_send, lag_recv, next_send, next_recv, sum_send, sum_recv,
):
    n_lag, n_probe, n_sketch = sizes
    step_count, input_count, half = markov.shape
    matrix_rows = matrix.shape[0]
    columns = matrix.shape[2]
    lag_total = matrix_rows * n_lag
    steps, pieces = plan(step_count, lag_total)
    lag = lax.axis_index("lag")
    probe = lax.axis_index("probe")
    sketch = lax.axis_index("sketch")
    flat = lag * n_probe + probe
    peers = n_lag * n_probe - 1

    def peer(index):
        other = lax.rem(flat + 1 + index, peers + 1)
        return {
            "lag": lax.div(other, n_probe),
            "probe": lax.rem(other, n_probe),
            "sketch": sketch,
        }

    def partner(index):
        return {"lag": lag, "probe": probe, "sketch": lax.rem(sketch + 1 + index, n_sketch)}

    def lag_peer(index):
        return {"lag": lax.rem(lag + 1 + index, n_lag), "probe": probe, "sketch": sketch}

    barrier = pltpu.get_barrier_semaphore()

    def greet(index):
        pl.semaphore_signal(barrier, inc=1, device_id=peer(index), device_id_type=MESH)

    for index in range(n_sketch - 1):
        pl.semaphore_signal(barrier, inc=1, device_id=partner(index), device_id_type=MESH)
    loop(peers, greet)

    own = pltpu.make_async_copy(markov, window.at[sketch, pl.ds(0, step_count)], own_sem)
    own.start()
    matrix_own = pltpu.make_async_copy(
        matrix, held.at[pl.ds(lag * matrix_rows, matrix_rows)], matrix_own_sem
    )
    matrix_own.start()
    weights[...] = jnp.zeros_like(weights)
    for ahead, at, count in pieces:
        @pl.when(lag + ahead >= n_lag)
        def _():
            place = pl.ds(ahead * step_count + at, count)
            window[:, place] = jnp.zeros((n_sketch, count, input_count, half), window.dtype)

    matrix_own.wait()
    pl.semaphore_wait(barrier, peers + n_sketch - 1)

    def lag_copy(number):
        ahead, at, count = pieces[number]
        return pltpu.make_async_remote_copy(
            src_ref=markov.at[pl.ds(at, count)],
            dst_ref=window.at[sketch, pl.ds(ahead * step_count + at, count)],
            send_sem=lag_send.at[number],
            recv_sem=lag_recv.at[number],
            device_id={"lag": lax.max(lag - ahead, 0), "probe": probe, "sketch": sketch},
            device_id_type=MESH,
        )

    def pair_copy(index):
        return pltpu.make_async_remote_copy(
            src_ref=markov,
            dst_ref=window.at[sketch, pl.ds(0, step_count)],
            send_sem=pair_send.at[index],
            recv_sem=pair_recv.at[index],
            device_id=partner(index),
            device_id_type=MESH,
        )

    def next_copy(number, index):
        ahead, at, count = pieces[number]
        place = window.at[sketch, pl.ds(ahead * step_count + at, count)]
        return pltpu.make_async_remote_copy(
            src_ref=place,
            dst_ref=place,
            send_sem=next_send.at[number, index],
            recv_sem=next_recv.at[number, index],
            device_id=partner(index),
            device_id_type=MESH,
        )

    def matrix_copy(index):
        return pltpu.make_async_remote_copy(
            src_ref=held.at[pl.ds(lag * matrix_rows, matrix_rows)],
            dst_ref=held.at[pl.ds(lag * matrix_rows, matrix_rows)],
            send_sem=matrix_send,
            recv_sem=matrix_recv,
            device_id=lag_peer(index),
            device_id_type=MESH,
        )

    loop(n_lag - 1, lambda index: matrix_copy(index).start())
    for number in range(0, 1):
        @pl.when(lag >= pieces[number][0])
        def _():
            lag_copy(number).start()
    for index in range(n_sketch - 1):
        pair_copy(index).start()
    for number in range(1, len(pieces)):
        @pl.when(lag >= pieces[number][0])
        def _():
            lag_copy(number).start()

    if n_lag > 1:
        arrived = held.at[pl.ds(0, (n_lag - 1) * matrix_rows)]
        pltpu.make_async_copy(arrived, arrived, matrix_recv).wait()
        pltpu.make_async_copy(arrived, arrived, matrix_send).wait()
    for row in range(step_count):
        weights[pl.ds(row * input_count, lag_total * input_count), row * columns:(row + 1) * columns] = (
            held[...].reshape(lag_total * input_count, columns)
        )

    def forward(number):
        @pl.when(lag + pieces[number][0] < n_lag)
        def _():
            lag_copy(number).wait_recv()
            for index in range(n_sketch - 1):
                next_copy(number, index).start()

    def landed(number):
        @pl.when(lag + pieces[number][0] < n_lag)
        def _():
            for index in range(n_sketch - 1):
                next_copy(number, index).wait()

    tile = min(256, half)
    group = 2 if step_count % 2 == 0 else 1

    def compute(first, total):
        depth = (lag_total + group - 1) * input_count
        weight = weights[pl.ds(first * input_count, depth), first * columns:(first + group) * columns]
        for side in range(n_sketch):
            def body(at, total):
                start = pl.multiple_of(at * tile, tile)
                block = window[side, pl.ds(first, lag_total + group - 1), :, pl.ds(start, tile)]
                product = lax.dot_general(
                    block.reshape(depth, tile), weight, (((0,), (0,)), ((), ())),
                    preferred_element_type=jnp.float32,
                )
                for row in range(group):
                    part = product[:, row * columns:(row + 1) * columns]
                    raw[first + row, pl.ds(side * half + start, tile), :] = part
                    total = total + jnp.sum((part * part).reshape(tile // 8, 8, columns), axis=0)
                return total
            total = lax.fori_loop(0, half // tile, body, total, unroll=depth <= 512)
        return total

    own.wait()
    total = jnp.zeros((8, columns), jnp.float32)
    done = 0
    paired = False
    for first in range(0, step_count, group):
        need = first + group - 1 + lag_total
        ready = done
        while ready < len(pieces) and pieces[ready][0] * step_count + pieces[ready][1] < need:
            forward(ready)
            ready += 1
        if not paired:
            for index in range(n_sketch - 1):
                pair_copy(index).wait()
            paired = True
        for number in range(done, ready):
            landed(number)
        done = ready
        total = compute(first, total)

    sums[pl.ds(flat, 1), :] = jnp.sum(total, axis=0, keepdims=True)

    def sum_copy(index):
        place = sums.at[pl.ds(flat, 1)]
        return pltpu.make_async_remote_copy(
            src_ref=place,
            dst_ref=place,
            send_sem=sum_send,
            recv_sem=sum_recv,
            device_id=peer(index),
            device_id_type=MESH,
        )

    loop(peers, lambda index: sum_copy(index).start())
    for number in range(len(pieces)):
        @pl.when(lag >= pieces[number][0])
        def _():
            lag_copy(number).wait_send()
    if peers:
        arrived = sums.at[pl.ds(0, peers)]
        pltpu.make_async_copy(arrived, arrived, sum_recv).wait()
        pltpu.make_async_copy(arrived, arrived, sum_send).wait()
    cells = step_count * n_lag * half * n_sketch * n_probe
    mean = jnp.sum(sums[...], axis=0, keepdims=True) / cells
    factor[...] = jnp.broadcast_to(lax.rsqrt(mean + 1e-06), factor.shape)


def near_kernel(
    sizes, cuts, markov, matrix, raw, factor,
    window, held, weights, gram, other, sums,
    own_sem, matrix_own_sem, matrix_send, matrix_recv, first_recv, twin_send, twin_recv, hand_send, pair_send, pair_recv,
    down_send, down_recv, up_send, up_recv, pass_send, pass_recv, sum_send, sum_recv, all_in, risen,
):
    n_lag, n_probe, n_sketch = sizes
    step_count, input_count, half = markov.shape
    columns = matrix.shape[2]
    matrix_rows = matrix.shape[0]
    lag_total = matrix_rows * n_lag
    depth = lag_total * input_count
    later = lag_total - 1
    alone = step_count - later
    lag = lax.axis_index("lag")
    probe = lax.axis_index("probe")
    sketch = lax.axis_index("sketch")
    twin = 1 - sketch
    place = (lag * n_probe + probe) * n_sketch + sketch
    devices = n_lag * n_probe * n_sketch
    is_first = lag == 0
    is_last = lag == n_lag - 1
    is_middle = jnp.logical_not(jnp.logical_or(is_first, is_last))
    head = n_probe * n_sketch - 1
    is_head = place == head
    below = {"lag": lax.max(lag - 1, 0), "probe": probe, "sketch": sketch}
    above = {"lag": lax.min(lag + 1, n_lag - 1), "probe": probe, "sketch": sketch}
    partner = {"lag": lag, "probe": probe, "sketch": twin}

    def device(index):
        group = lax.div(index, n_sketch)
        return {
            "lag": lax.div(group, n_probe),
            "probe": lax.rem(group, n_probe),
            "sketch": lax.rem(index, n_sketch),
        }

    last = n_lag - 1

    def at_lag(to_lag, side):
        return {"lag": to_lag, "probe": probe, "sketch": side}

    barrier = pltpu.get_barrier_semaphore()

    def greet(to):
        pl.semaphore_signal(barrier, inc=1, device_id=to, device_id_type=MESH)

    @pl.when(jnp.logical_not(is_first))
    def _():
        greet(at_lag(0, sketch))
        greet(at_lag(0, twin))

    for to_lag in range(1, n_lag):
        @pl.when(lag < to_lag)
        def _():
            greet(at_lag(to_lag, sketch))

    greet(partner)

    @pl.when(probe < n_probe - 1)
    def _():
        greet(device(head))

    expected = lax.select(is_first, 2 * n_lag - 1, lag + 1)

    own_slots = pl.ds(later, step_count)
    next_slots = pl.ds(later + step_count, later)
    own_rows = held.at[sketch, pl.ds(lag * matrix_rows, matrix_rows)]
    matrix_own = pltpu.make_async_copy(matrix, own_rows, matrix_own_sem)
    matrix_own.start()
    own = pltpu.make_async_copy(markov, window.at[sketch, own_slots], own_sem)
    own.start()
    weights[...] = jnp.zeros_like(weights)

    @pl.when(is_last)
    def _():
        window[:, next_slots] = jnp.zeros((n_sketch, later, input_count, half), window.dtype)

    def parts(edge):
        return pl.ds(0, cuts[edge]), pl.ds(cuts[edge], half - cuts[edge])

    def remote(src, dst, send, recv, to):
        return pltpu.make_async_remote_copy(
            src_ref=src, dst_ref=dst, send_sem=send, recv_sem=recv, device_id=to, device_id_type=MESH
        )

    def down(part, edge):
        return remote(
            window.at[sketch, pl.ds(later, later), :, parts(edge)[part]],
            window.at[sketch, next_slots, :, parts(edge)[part]],
            down_send, down_recv.at[part], below,
        )

    def up(edge):
        return remote(
            window.at[sketch, pl.ds(later + alone, later), :, parts(edge)[1]],
            window.at[sketch, pl.ds(0, later), :, parts(edge)[1]],
            up_send, up_recv, above,
        )

    def edge_above(body):
        for edge in range(2):
            pl.when(is_first if edge == 0 else is_middle)(functools.partial(body, edge))

    def edge_below(body):
        for edge in range(2):
            pl.when(lag == 1 if edge == 0 else lag > 1)(functools.partial(body, edge))

    def passed(part, edge):
        ref = window.at[sketch, next_slots, :, parts(edge)[part]]
        return remote(ref, ref, pass_send, pass_recv.at[part], partner)

    pair = remote(
        window.at[sketch, own_slots], window.at[sketch, own_slots], pair_send, pair_recv, partner
    )

    def outer(first, second, start, stop):
        def rows(slots):
            slot, count = slots
            return window[sketch, pl.ds(slot, count), :, start:stop].reshape(count * input_count, stop - start)
        return lax.dot_general(
            rows(first), rows(second), (((1,), (1,)), ((), ())), preferred_element_type=jnp.float32
        )

    def own_gram():
        inner = outer((later, step_count), (later, step_count), 0, half)
        gram[...] = jnp.zeros_like(gram)

        def shift(row):
            low, high = max(0, -row), min(lag_total, step_count - row)
            to = slice(low * input_count, high * input_count)
            at = slice((row + low) * input_count, (row + high) * input_count)
            gram[to, to] += inner[at, at]

        for row in range(step_count):
            shift(row)

        @pl.when(jnp.logical_not(is_first))
        def _():
            for row in range(-later, 0):
                shift(row)

    def matrix_copy(to_lag, recv=matrix_recv):
        return remote(own_rows, own_rows, matrix_send, recv, at_lag(to_lag, sketch))

    def matrix_twin(to_lag):
        return remote(own_rows, own_rows, twin_send, twin_recv, at_lag(to_lag, twin))

    matrix_hand = remote(held.at[sketch], held.at[sketch], hand_send, twin_recv, partner)
    rest_rows = held.at[sketch, pl.ds(matrix_rows, lag_total - matrix_rows)]
    rest_hand = remote(rest_rows, rest_rows, hand_send, twin_recv, partner)

    @pl.when(is_first)
    def _():
        own.wait()
        own_gram()

    pl.semaphore_wait(barrier, lax.select(is_head, devices - 1, expected))
    for from_lag in range(2, n_lag):
        @pl.when(lag == from_lag)
        def _():
            for to_lag in range(1, from_lag):
                pl.semaphore_signal(
                    risen.at[from_lag], inc=1, device_id=at_lag(to_lag, sketch), device_id_type=MESH
                )

    matrix_own.wait()

    @pl.when(is_first)
    def _():
        for to_lag in reversed(range(1, n_lag)):
            matrix_copy(to_lag, first_recv).start()
            matrix_twin(to_lag).start()
        up(0).start()

    @pl.when(jnp.logical_not(is_first))
    def _():
        own.wait()
        for to_lag in range(last):
            @pl.when(lag > to_lag)
            def _():
                matrix_copy(to_lag).start()
        edge_below(lambda edge: down(0, edge).start())

        @pl.when(is_last)
        def _():
            matrix_twin(last).start()

        own_gram()

    for here in range(1, last):
        @pl.when(lag == here)
        def _():
            for to_lag in range(here + 1, n_lag):
                pl.semaphore_wait(risen.at[to_lag], 1)
                if to_lag == here + 1:
                    up(1).start()
                matrix_copy(to_lag).start()
            matrix_twin(last).start()

    @pl.when(is_head)
    def _():
        loop(devices - 1, lambda index: pl.semaphore_signal(
            all_in, inc=1, device_id=device(lax.rem(place + 1 + index, devices)), device_id_type=MESH
        ))

    def cross(edge):
        for row in range(alone, step_count):
            count = (step_count - row) * input_count
            gram[0:count, count:depth] += 2.0 * edge[(row - alone) * input_count:, 0:(row - alone + 1) * input_count]

    others = held.at[sketch, pl.ds(0, lag_total - matrix_rows)]

    middle_rows = held.at[sketch, pl.ds(0, lag_total - 2 * matrix_rows)]

    @pl.when(is_first)
    def _():
        pltpu.make_async_copy(others, others, matrix_recv).wait()
        matrix_hand.start()

    @pl.when(is_middle)
    def _():
        pltpu.make_async_copy(middle_rows, middle_rows, matrix_recv).wait()
        rest_hand.start()

    @pl.when(is_middle)
    def _():
        edge_below(lambda edge: down(1, edge).start())

    def from_below(edge):
        up(edge).wait_recv()
        cross(outer((0, later), (later, later), cuts[edge], half))

    def from_above(edge):
        down(0, edge).wait_recv()
        cross(outer((later + alone, later), (later + step_count, later), 0, cuts[edge]))

    edge_below(from_below)
    edge_above(from_above)

    whole = gram[...]
    high = whole.astype(jnp.bfloat16)
    rest = whole - high.astype(jnp.float32)
    middle = rest.astype(jnp.bfloat16)
    low = (rest - middle.astype(jnp.float32)).astype(jnp.bfloat16)

    @pl.when(is_last)
    def _():
        if n_lag > 2:
            pltpu.make_async_copy(middle_rows, middle_rows, matrix_recv).wait()

    @pl.when(jnp.logical_not(is_first))
    def _():
        pltpu.make_async_copy(own_rows, own_rows, first_recv).wait()

    matrix_hand.wait_recv()
    mine = held[sketch].reshape(depth, columns)
    both = jnp.concatenate([mine, held[twin].reshape(depth, columns)], axis=1)
    product = jnp.dot(low, both, preferred_element_type=jnp.float32)
    product = product + jnp.dot(middle, both, preferred_element_type=jnp.float32)
    product = product + jnp.dot(high, both, preferred_element_type=jnp.float32)
    square = jnp.sum(product * both.astype(jnp.float32), axis=0, keepdims=True)
    sums[pl.ds(place, 1), :] = square[:, :columns]
    other[...] = square[:, columns:]

    def sum_copy(index, side):
        at = lax.rem(lag * n_probe + probe + index, n_lag * n_probe)
        to = {"lag": lax.div(at, n_probe), "probe": lax.rem(at, n_probe), "sketch": side}
        ref = sums.at[pl.ds(place, 1)]
        src = other if side is twin else ref
        return remote(src, ref, sum_send, sum_recv, to)

    @pl.when(jnp.logical_not(is_head))
    def _():
        pl.semaphore_wait(all_in, 1)

    loop(n_lag * n_probe - 1, lambda index: sum_copy(index + 1, sketch).start())
    loop(n_lag * n_probe, lambda index: sum_copy(index, twin).start())

    @pl.when(is_last)
    def _():
        down(1, 1).start()

    pair.start()

    edge_above(lambda edge: passed(0, edge).start())

    for row in range(step_count):
        weights[pl.ds(row * input_count, depth), row * columns:(row + 1) * columns] = mine

    tile = 128

    def multiply(side, first, last):
        for start in range(first, last, tile):
            block = window[side, pl.ds(later, step_count + later), :, pl.ds(start, tile)]
            product = lax.dot_general(
                block.reshape((step_count + later) * input_count, tile), weights[...], (((0,), (0,)), ((), ())),
                preferred_element_type=jnp.float32,
            )
            for row in range(step_count):
                raw[row, pl.ds(pl.multiple_of(side * half + start, tile), tile), :] = (
                    product[:, row * columns:(row + 1) * columns]
                )

    cut = min(cuts)
    multiply(sketch, 0, cut)
    pair.wait()

    edge_above(lambda edge: passed(0, edge).wait_recv())

    multiply(twin, 0, cut)

    def hand_rest(edge):
        down(1, edge).wait_recv()
        passed(1, edge).start()

    edge_above(hand_rest)

    multiply(sketch, cut, half)

    edge_above(lambda edge: passed(1, edge).wait_recv())

    multiply(twin, cut, half)

    received = window.at[sketch, next_slots]

    @pl.when(jnp.logical_not(is_last))
    def _():
        pltpu.make_async_copy(received, received, pass_send).wait()
        edge_above(lambda edge: up(edge).wait_send())

    @pl.when(is_first)
    def _():
        matrix_hand.wait_send()
        pltpu.make_async_copy(others, others, twin_send).wait()

    @pl.when(jnp.logical_not(is_first))
    def _():
        matrix_twin(last).wait_send()

        @pl.when(jnp.logical_not(is_last))
        def _():
            rest_hand.wait_send()

    @pl.when(jnp.logical_not(is_first))
    def _():
        pltpu.make_async_copy(received, received, down_send).wait()

    pltpu.make_async_copy(others, others, matrix_send).wait()
    landed = sums.at[pl.ds(0, devices - 1)]
    pltpu.make_async_copy(landed, landed, sum_send).wait()
    pltpu.make_async_copy(landed, landed, sum_recv).wait()
    cells = step_count * n_lag * half * n_sketch * n_probe
    mean = lax.max(jnp.sum(sums[...], axis=0, keepdims=True), 0.0) / cells
    factor[...] = jnp.broadcast_to(lax.rsqrt(mean + 1e-06), factor.shape)


def near(sizes, markov, test_matrix):
    n_lag, n_probe, n_sketch = sizes
    step_count, input_count, half = markov.shape
    matrix_rows, _, columns = test_matrix.shape
    lag_total = matrix_rows * n_lag
    later = lag_total - 1
    dma = pltpu.SemaphoreType.DMA
    return pl.pallas_call(
        functools.partial(near_kernel, sizes, (half * 3 // 4, half * 5 // 8)),
        out_shape=[
            pltpu.VMEM((step_count, half * n_sketch, columns), jnp.float32),
            pltpu.VMEM((8, columns), jnp.float32),
        ],
        in_specs=[pl.BlockSpec(memory_space=pltpu.HBM)] * 2,
        out_specs=[pl.BlockSpec(memory_space=pltpu.VMEM)] * 2,
        scratch_shapes=[
            pltpu.VMEM((n_sketch, step_count + 2 * later, input_count, half), jnp.bfloat16),
            pltpu.VMEM((n_sketch, lag_total, input_count, columns), jnp.bfloat16),
            pltpu.VMEM(((step_count + later) * input_count, step_count * columns), jnp.bfloat16),
            pltpu.VMEM((lag_total * input_count, lag_total * input_count), jnp.float32),
            pltpu.VMEM((1, columns), jnp.float32),
            pltpu.VMEM((n_lag * n_probe * n_sketch, columns), jnp.float32),
            dma, dma, dma, dma, dma, dma, dma, dma, dma, dma,
            dma, dma((2,)), dma, dma, dma, dma((2,)), dma, dma,
            pltpu.SemaphoreType.REGULAR,
            pltpu.SemaphoreType.REGULAR((n_lag,)),
        ],
        compiler_params=pltpu.CompilerParams(
            collective_id=1, has_side_effects=True, vmem_limit_bytes=59 * 1024 * 1024
        ),
    )(markov, test_matrix)


def is_near(sizes, markov, test_matrix):
    n_lag, n_probe, n_sketch = sizes
    step_count, input_count, half = markov.shape
    lag_total = test_matrix.shape[0] * n_lag
    return n_sketch == 2 and n_lag > 2 and 1 < lag_total <= step_count and half % 512 == 0


def scale_kernel(raw, factor, out, held, sem):
    step_count, probes, columns = raw.shape
    pieces = 2
    part = probes // pieces
    gain = factor[0:1, :]
    for row in range(step_count):
        for piece in range(pieces):
            place = pl.ds(piece * part, part)
            held[row, place] = (raw[row, place] * gain).astype(held.dtype)
            pltpu.make_async_copy(held.at[row, place], out.at[row, place], sem).start()
    pltpu.make_async_copy(held, out, sem).wait()


def scale(raw, factor):
    step_count, probes, columns = raw.shape
    return pl.pallas_call(
        scale_kernel,
        out_shape=jax.ShapeDtypeStruct(raw.shape, jnp.bfloat16),
        in_specs=[pl.BlockSpec(memory_space=pltpu.VMEM)] * 2,
        out_specs=pl.BlockSpec(memory_space=pltpu.HBM),
        scratch_shapes=[
            pltpu.VMEM(raw.shape, jnp.bfloat16),
            pltpu.SemaphoreType.DMA,
        ],
        compiler_params=pltpu.CompilerParams(vmem_limit_bytes=16 * 1024 * 1024),
    )(raw, factor)


def local(sizes, markov, test_matrix):
    if is_near(sizes, markov, test_matrix):
        return scale(*near(sizes, markov, test_matrix))
    n_lag, n_probe, n_sketch = sizes
    step_count, input_count, half = markov.shape
    matrix_rows, _, columns = test_matrix.shape
    lag_total = matrix_rows * n_lag
    steps, pieces = plan(step_count, lag_total)
    count = max(len(pieces), 1)
    pairs = max(n_sketch - 1, 1)
    probes = half * n_sketch
    dma = pltpu.SemaphoreType.DMA
    raw, factor = pl.pallas_call(
        functools.partial(gather_kernel, sizes),
        out_shape=[
            pltpu.VMEM((step_count, probes, columns), jnp.float32),
            pltpu.VMEM((8, columns), jnp.float32),
        ],
        in_specs=[pl.BlockSpec(memory_space=pltpu.HBM)] * 2,
        out_specs=[pl.BlockSpec(memory_space=pltpu.VMEM)] * 2,
        scratch_shapes=[
            pltpu.VMEM((n_sketch, steps, input_count, half), jnp.bfloat16),
            pltpu.VMEM((lag_total, input_count, columns), jnp.bfloat16),
            pltpu.VMEM((steps * input_count, step_count * columns), jnp.bfloat16),
            pltpu.VMEM((n_lag * n_probe, columns), jnp.float32),
            dma, dma, dma, dma,
            dma((pairs,)), dma((pairs,)),
            dma((count,)), dma((count,)),
            dma((count, pairs)), dma((count, pairs)),
            dma, dma,
        ],
        compiler_params=pltpu.CompilerParams(
            collective_id=0, has_side_effects=True, vmem_limit_bytes=59 * 1024 * 1024
        ),
    )(markov, test_matrix)
    return scale(raw, factor)


def solution(mesh):
    sizes = tuple(mesh.shape[name] for name in ("lag", "probe", "sketch"))
    return jax.shard_map(
        functools.partial(local, sizes),
        mesh=mesh,
        in_specs=(P("lag", None, ("probe", "sketch")), P("lag", None, "sketch")),
        out_specs=P("lag", "probe", "sketch"),
        check_vma=False,
    )
```

```python
import functools

import jax
import jax.numpy as jnp
from jax import lax
from jax.experimental import pallas as pl
from jax.experimental.pallas import tpu as pltpu
from jax.sharding import PartitionSpec as P

MESH = pl.DeviceIdType.MESH
UNROLL = 32


def loop(count, body):
    if count <= UNROLL:
        for index in range(count):
            body(index)
    else:
        def step(index, carry):
            body(index)
            return carry
        lax.fori_loop(0, count, step, 0)


def plan(step_count, lag_total):
    steps = step_count + lag_total - 1
    blocks = (steps - 1) // step_count
    pieces = []
    for ahead in range(1, blocks + 1):
        used = min(step_count, steps - ahead * step_count)
        if blocks == 1:
            pieces += [(ahead, at, 1) for at in range(used)]
        else:
            pieces.append((ahead, 0, used))
    return steps, pieces


def gather_kernel(
    sizes, markov, matrix, raw, factor,
    window, held, weights, sums,
    own_sem, matrix_own_sem, matrix_send, matrix_recv,
    pair_send, pair_recv, lag_send, lag_recv, next_send, next_recv, sum_send, sum_recv,
):
    n_lag, n_probe, n_sketch = sizes
    step_count, input_count, half = markov.shape
    matrix_rows = matrix.shape[0]
    columns = matrix.shape[2]
    lag_total = matrix_rows * n_lag
    steps, pieces = plan(step_count, lag_total)
    lag = lax.axis_index("lag")
    probe = lax.axis_index("probe")
    sketch = lax.axis_index("sketch")
    flat = lag * n_probe + probe
    peers = n_lag * n_probe - 1

    def peer(index):
        other = lax.rem(flat + 1 + index, peers + 1)
        return {
            "lag": lax.div(other, n_probe),
            "probe": lax.rem(other, n_probe),
            "sketch": sketch,
        }

    def partner(index):
        return {"lag": lag, "probe": probe, "sketch": lax.rem(sketch + 1 + index, n_sketch)}

    def lag_peer(index):
        return {"lag": lax.rem(lag + 1 + index, n_lag), "probe": probe, "sketch": sketch}

    barrier = pltpu.get_barrier_semaphore()

    def greet(index):
        pl.semaphore_signal(barrier, inc=1, device_id=peer(index), device_id_type=MESH)

    for index in range(n_sketch - 1):
        pl.semaphore_signal(barrier, inc=1, device_id=partner(index), device_id_type=MESH)
    loop(peers, greet)

    own = pltpu.make_async_copy(markov, window.at[sketch, pl.ds(0, step_count)], own_sem)
    own.start()
    matrix_own = pltpu.make_async_copy(
        matrix, held.at[pl.ds(lag * matrix_rows, matrix_rows)], matrix_own_sem
    )
    matrix_own.start()
    weights[...] = jnp.zeros_like(weights)
    for ahead, at, count in pieces:
        @pl.when(lag + ahead >= n_lag)
        def _():
            place = pl.ds(ahead * step_count + at, count)
            window[:, place] = jnp.zeros((n_sketch, count, input_count, half), window.dtype)

    matrix_own.wait()
    pl.semaphore_wait(barrier, peers + n_sketch - 1)

    def lag_copy(number):
        ahead, at, count = pieces[number]
        return pltpu.make_async_remote_copy(
            src_ref=markov.at[pl.ds(at, count)],
            dst_ref=window.at[sketch, pl.ds(ahead * step_count + at, count)],
            send_sem=lag_send.at[number],
            recv_sem=lag_recv.at[number],
            device_id={"lag": lax.max(lag - ahead, 0), "probe": probe, "sketch": sketch},
            device_id_type=MESH,
        )

    def pair_copy(index):
        return pltpu.make_async_remote_copy(
            src_ref=markov,
            dst_ref=window.at[sketch, pl.ds(0, step_count)],
            send_sem=pair_send.at[index],
            recv_sem=pair_recv.at[index],
            device_id=partner(index),
            device_id_type=MESH,
        )

    def next_copy(number, index):
        ahead, at, count = pieces[number]
        place = window.at[sketch, pl.ds(ahead * step_count + at, count)]
        return pltpu.make_async_remote_copy(
            src_ref=place,
            dst_ref=place,
            send_sem=next_send.at[number, index],
            recv_sem=next_recv.at[number, index],
            device_id=partner(index),
            device_id_type=MESH,
        )

    def matrix_copy(index):
        return pltpu.make_async_remote_copy(
            src_ref=held.at[pl.ds(lag * matrix_rows, matrix_rows)],
            dst_ref=held.at[pl.ds(lag * matrix_rows, matrix_rows)],
            send_sem=matrix_send,
            recv_sem=matrix_recv,
            device_id=lag_peer(index),
            device_id_type=MESH,
        )

    loop(n_lag - 1, lambda index: matrix_copy(index).start())
    for number in range(0, 1):
        @pl.when(lag >= pieces[number][0])
        def _():
            lag_copy(number).start()
    for index in range(n_sketch - 1):
        pair_copy(index).start()
    for number in range(1, len(pieces)):
        @pl.when(lag >= pieces[number][0])
        def _():
            lag_copy(number).start()

    if n_lag > 1:
        arrived = held.at[pl.ds(0, (n_lag - 1) * matrix_rows)]
        pltpu.make_async_copy(arrived, arrived, matrix_recv).wait()
        pltpu.make_async_copy(arrived, arrived, matrix_send).wait()
    for row in range(step_count):
        weights[pl.ds(row * input_count, lag_total * input_count), row * columns:(row + 1) * columns] = (
            held[...].reshape(lag_total * input_count, columns)
        )

    def forward(number):
        @pl.when(lag + pieces[number][0] < n_lag)
        def _():
            lag_copy(number).wait_recv()
            for index in range(n_sketch - 1):
                next_copy(number, index).start()

    def landed(number):
        @pl.when(lag + pieces[number][0] < n_lag)
        def _():
            for index in range(n_sketch - 1):
                next_copy(number, index).wait()

    tile = min(256, half)
    group = 2 if step_count % 2 == 0 else 1

    def compute(first, total):
        depth = (lag_total + group - 1) * input_count
        weight = weights[pl.ds(first * input_count, depth), first * columns:(first + group) * columns]
        for side in range(n_sketch):
            def body(at, total):
                start = pl.multiple_of(at * tile, tile)
                block = window[side, pl.ds(first, lag_total + group - 1), :, pl.ds(start, tile)]
                product = lax.dot_general(
                    block.reshape(depth, tile), weight, (((0,), (0,)), ((), ())),
                    preferred_element_type=jnp.float32,
                )
                for row in range(group):
                    part = product[:, row * columns:(row + 1) * columns]
                    raw[first + row, pl.ds(side * half + start, tile), :] = part
                    total = total + jnp.sum((part * part).reshape(tile // 8, 8, columns), axis=0)
                return total
            total = lax.fori_loop(0, half // tile, body, total, unroll=depth <= 512)
        return total

    own.wait()
    total = jnp.zeros((8, columns), jnp.float32)
    done = 0
    paired = False
    for first in range(0, step_count, group):
        need = first + group - 1 + lag_total
        ready = done
        while ready < len(pieces) and pieces[ready][0] * step_count + pieces[ready][1] < need:
            forward(ready)
            ready += 1
        if not paired:
            for index in range(n_sketch - 1):
                pair_copy(index).wait()
            paired = True
        for number in range(done, ready):
            landed(number)
        done = ready
        total = compute(first, total)

    sums[pl.ds(flat, 1), :] = jnp.sum(total, axis=0, keepdims=True)

    def sum_copy(index):
        place = sums.at[pl.ds(flat, 1)]
        return pltpu.make_async_remote_copy(
            src_ref=place,
            dst_ref=place,
            send_sem=sum_send,
            recv_sem=sum_recv,
            device_id=peer(index),
            device_id_type=MESH,
        )

    loop(peers, lambda index: sum_copy(index).start())
    for number in range(len(pieces)):
        @pl.when(lag >= pieces[number][0])
        def _():
            lag_copy(number).wait_send()
    if peers:
        arrived = sums.at[pl.ds(0, peers)]
        pltpu.make_async_copy(arrived, arrived, sum_recv).wait()
        pltpu.make_async_copy(arrived, arrived, sum_send).wait()
    cells = step_count * n_lag * half * n_sketch * n_probe
    mean = jnp.sum(sums[...], axis=0, keepdims=True) / cells
    factor[...] = jnp.broadcast_to(lax.rsqrt(mean + 1e-06), factor.shape)


def near_kernel(
    sizes, cuts, markov, matrix, raw, factor,
    window, held, weights, gram, joint, other, sums,
    own_sem, matrix_own_sem, matrix_send, matrix_recv, first_recv, twin_send, twin_recv, hand_send, pair_send, pair_recv,
    down_send, down_recv, up_send, up_recv, pass_send, pass_recv, sum_send, sum_recv, all_in, risen,
):
    n_lag, n_probe, n_sketch = sizes
    step_count, input_count, half = markov.shape
    columns = matrix.shape[2]
    matrix_rows = matrix.shape[0]
    lag_total = matrix_rows * n_lag
    depth = lag_total * input_count
    later = lag_total - 1
    alone = step_count - later
    lag = lax.axis_index("lag")
    probe = lax.axis_index("probe")
    sketch = lax.axis_index("sketch")
    twin = 1 - sketch
    place = (lag * n_probe + probe) * n_sketch + sketch
    devices = n_lag * n_probe * n_sketch
    is_first = lag == 0
    is_last = lag == n_lag - 1
    is_middle = jnp.logical_not(jnp.logical_or(is_first, is_last))
    head = n_probe * n_sketch - 1
    is_head = place == head
    below = {"lag": lax.max(lag - 1, 0), "probe": probe, "sketch": sketch}
    above = {"lag": lax.min(lag + 1, n_lag - 1), "probe": probe, "sketch": sketch}
    partner = {"lag": lag, "probe": probe, "sketch": twin}

    def device(index):
        group = lax.div(index, n_sketch)
        return {
            "lag": lax.div(group, n_probe),
            "probe": lax.rem(group, n_probe),
            "sketch": lax.rem(index, n_sketch),
        }

    last = n_lag - 1

    def at_lag(to_lag, side):
        return {"lag": to_lag, "probe": probe, "sketch": side}

    barrier = pltpu.get_barrier_semaphore()

    def greet(to):
        pl.semaphore_signal(barrier, inc=1, device_id=to, device_id_type=MESH)

    @pl.when(jnp.logical_not(is_first))
    def _():
        greet(at_lag(0, sketch))
        greet(at_lag(0, twin))

    for to_lag in range(1, n_lag):
        @pl.when(lag < to_lag)
        def _():
            greet(at_lag(to_lag, sketch))

    greet(partner)

    @pl.when(probe < n_probe - 1)
    def _():
        greet(device(head))

    expected = lax.select(is_first, 2 * n_lag - 1, lag + 1)

    own_slots = pl.ds(later, step_count)
    next_slots = pl.ds(later + step_count, later)
    own_rows = held.at[sketch, pl.ds(lag * matrix_rows, matrix_rows)]
    matrix_own = pltpu.make_async_copy(matrix, own_rows, matrix_own_sem)
    matrix_own.start()
    own = pltpu.make_async_copy(markov, window.at[sketch, own_slots], own_sem)
    own.start()
    weights[...] = jnp.zeros_like(weights)

    @pl.when(is_last)
    def _():
        window[:, next_slots] = jnp.zeros((n_sketch, later, input_count, half), window.dtype)

    def parts(edge):
        return pl.ds(0, cuts[edge]), pl.ds(cuts[edge], half - cuts[edge])

    def remote(src, dst, send, recv, to):
        return pltpu.make_async_remote_copy(
            src_ref=src, dst_ref=dst, send_sem=send, recv_sem=recv, device_id=to, device_id_type=MESH
        )

    def down(part, edge):
        return remote(
            window.at[sketch, pl.ds(later, later), :, parts(edge)[part]],
            window.at[sketch, next_slots, :, parts(edge)[part]],
            down_send, down_recv.at[part], below,
        )

    def up(edge):
        return remote(
            window.at[sketch, pl.ds(later + alone, later), :, parts(edge)[1]],
            window.at[sketch, pl.ds(0, later), :, parts(edge)[1]],
            up_send, up_recv, above,
        )

    def edge_above(body):
        for edge in range(2):
            pl.when(is_first if edge == 0 else is_middle)(functools.partial(body, edge))

    def edge_below(body):
        for edge in range(2):
            pl.when(lag == 1 if edge == 0 else lag > 1)(functools.partial(body, edge))

    def passed(part, edge):
        ref = window.at[sketch, next_slots, :, parts(edge)[part]]
        return remote(ref, ref, pass_send, pass_recv.at[part], partner)

    pair = remote(
        window.at[sketch, own_slots], window.at[sketch, own_slots], pair_send, pair_recv, partner
    )

    def outer(first, second, start, stop):
        def rows(slots):
            slot, count = slots
            return window[sketch, pl.ds(slot, count), :, start:stop].reshape(count * input_count, stop - start)
        return lax.dot_general(
            rows(first), rows(second), (((1,), (1,)), ((), ())), preferred_element_type=jnp.float32
        )

    def own_gram():
        inner = outer((later, step_count), (later, step_count), 0, half)
        gram[...] = jnp.zeros_like(gram)
        joint[...] = jnp.zeros_like(joint)

        def shift(row):
            low, high = max(0, -row), min(lag_total, step_count - row)
            to = slice(low * input_count, high * input_count)
            at = slice((row + low) * input_count, (row + high) * input_count)
            gram[to, to] += inner[at, at]

        for row in range(step_count):
            shift(row)

        @pl.when(jnp.logical_not(is_first))
        def _():
            for row in range(-later, 0):
                shift(row)

    def matrix_copy(to_lag, recv=matrix_recv):
        return remote(own_rows, own_rows, matrix_send, recv, at_lag(to_lag, sketch))

    def matrix_twin(to_lag):
        return remote(own_rows, own_rows, twin_send, twin_recv, at_lag(to_lag, twin))

    matrix_hand = remote(held.at[sketch], held.at[sketch], hand_send, twin_recv, partner)
    rest_rows = held.at[sketch, pl.ds(matrix_rows, lag_total - matrix_rows)]
    rest_hand = remote(rest_rows, rest_rows, hand_send, twin_recv, partner)

    @pl.when(is_first)
    def _():
        own.wait()
        own_gram()

    pl.semaphore_wait(barrier, lax.select(is_head, devices - 1, expected))
    for from_lag in range(2, n_lag):
        @pl.when(lag == from_lag)
        def _():
            for to_lag in range(1, from_lag):
                pl.semaphore_signal(
                    risen.at[from_lag], inc=1, device_id=at_lag(to_lag, sketch), device_id_type=MESH
                )

    matrix_own.wait()

    @pl.when(is_first)
    def _():
        for to_lag in reversed(range(1, n_lag)):
            matrix_copy(to_lag, first_recv).start()
            matrix_twin(to_lag).start()
        up(0).start()

    @pl.when(jnp.logical_not(is_first))
    def _():
        own.wait()
        for to_lag in range(last):
            @pl.when(lag > to_lag)
            def _():
                matrix_copy(to_lag).start()
        edge_below(lambda edge: down(0, edge).start())

        @pl.when(is_last)
        def _():
            matrix_twin(last).start()

        own_gram()

    for here in range(1, last):
        @pl.when(lag == here)
        def _():
            for to_lag in range(here + 1, n_lag):
                pl.semaphore_wait(risen.at[to_lag], 1)
                if to_lag == here + 1:
                    up(1).start()
                matrix_copy(to_lag).start()
            matrix_twin(last).start()

    @pl.when(is_head)
    def _():
        loop(devices - 1, lambda index: pl.semaphore_signal(
            all_in, inc=1, device_id=device(lax.rem(place + 1 + index, devices)), device_id_type=MESH
        ))

    def cross(edge):
        for row in range(alone, step_count):
            count = (step_count - row) * input_count
            gram[0:count, count:depth] += 2.0 * edge[(row - alone) * input_count:, 0:(row - alone + 1) * input_count]

    others = held.at[sketch, pl.ds(0, lag_total - matrix_rows)]

    middle_rows = held.at[sketch, pl.ds(0, lag_total - 2 * matrix_rows)]

    @pl.when(is_first)
    def _():
        pltpu.make_async_copy(others, others, matrix_recv).wait()
        matrix_hand.start()

    @pl.when(is_middle)
    def _():
        pltpu.make_async_copy(middle_rows, middle_rows, matrix_recv).wait()
        rest_hand.start()

    @pl.when(is_middle)
    def _():
        edge_below(lambda edge: down(1, edge).start())

    def from_below(edge):
        up(edge).wait_recv()
        joint[...] += outer((0, later), (later, later), cuts[edge], half)

    def from_above(edge):
        down(0, edge).wait_recv()
        joint[...] += outer((later + alone, later), (later + step_count, later), 0, cuts[edge])

    edge_below(from_below)
    edge_above(from_above)
    cross(joint[...])

    whole = gram[...]
    high = whole.astype(jnp.bfloat16)
    rest = whole - high.astype(jnp.float32)
    middle = rest.astype(jnp.bfloat16)
    low = (rest - middle.astype(jnp.float32)).astype(jnp.bfloat16)

    @pl.when(is_last)
    def _():
        if n_lag > 2:
            pltpu.make_async_copy(middle_rows, middle_rows, matrix_recv).wait()

    @pl.when(jnp.logical_not(is_first))
    def _():
        pltpu.make_async_copy(own_rows, own_rows, first_recv).wait()

    matrix_hand.wait_recv()
    mine = held[sketch].reshape(depth, columns)
    both = jnp.concatenate([mine, held[twin].reshape(depth, columns)], axis=1)
    product = jnp.dot(low, both, preferred_element_type=jnp.float32)
    product = product + jnp.dot(middle, both, preferred_element_type=jnp.float32)
    product = product + jnp.dot(high, both, preferred_element_type=jnp.float32)
    square = jnp.sum(product * both.astype(jnp.float32), axis=0, keepdims=True)
    sums[pl.ds(place, 1), :] = square[:, :columns]
    other[...] = square[:, columns:]

    def sum_copy(at, side):
        to = {"lag": lax.div(at, n_probe), "probe": lax.rem(at, n_probe), "sketch": side}
        ref = sums.at[pl.ds(place, 1)]
        src = other if side is twin else ref
        return remote(src, ref, sum_send, sum_recv, to)

    @pl.when(jnp.logical_not(is_head))
    def _():
        pl.semaphore_wait(all_in, 1)

    group = lag * n_probe + probe

    def send_sums(index):
        sum_copy(index, twin).start()
        sum_copy(lax.select(index < group, index, index + 1), sketch).start()

    loop(n_lag * n_probe - 1, send_sums)
    sum_copy(n_lag * n_probe - 1, twin).start()

    @pl.when(is_last)
    def _():
        down(1, 1).start()

    pair.start()

    edge_above(lambda edge: passed(0, edge).start())

    for row in range(step_count):
        weights[pl.ds(row * input_count, depth), row * columns:(row + 1) * columns] = mine

    tile = 128

    def multiply(side, first, last):
        for start in range(first, last, tile):
            block = window[side, pl.ds(later, step_count + later), :, pl.ds(start, tile)]
            product = lax.dot_general(
                block.reshape((step_count + later) * input_count, tile), weights[...], (((0,), (0,)), ((), ())),
                preferred_element_type=jnp.float32,
            )
            for row in range(step_count):
                raw[row, pl.ds(pl.multiple_of(side * half + start, tile), tile), :] = (
                    product[:, row * columns:(row + 1) * columns]
                )

    cut = min(cuts)
    multiply(sketch, 0, cut)
    pair.wait()

    edge_above(lambda edge: passed(0, edge).wait_recv())

    multiply(twin, 0, cut)

    def hand_rest(edge):
        down(1, edge).wait_recv()
        passed(1, edge).start()

    edge_above(hand_rest)

    multiply(sketch, cut, half)

    edge_above(lambda edge: passed(1, edge).wait_recv())

    multiply(twin, cut, half)

    received = window.at[sketch, next_slots]

    @pl.when(jnp.logical_not(is_last))
    def _():
        pltpu.make_async_copy(received, received, pass_send).wait()
        edge_above(lambda edge: up(edge).wait_send())

    @pl.when(is_first)
    def _():
        matrix_hand.wait_send()
        pltpu.make_async_copy(others, others, twin_send).wait()

    @pl.when(jnp.logical_not(is_first))
    def _():
        matrix_twin(last).wait_send()

        @pl.when(jnp.logical_not(is_last))
        def _():
            rest_hand.wait_send()

    @pl.when(jnp.logical_not(is_first))
    def _():
        pltpu.make_async_copy(received, received, down_send).wait()

    pltpu.make_async_copy(others, others, matrix_send).wait()
    landed = sums.at[pl.ds(0, devices - 1)]
    pltpu.make_async_copy(landed, landed, sum_send).wait()
    pltpu.make_async_copy(landed, landed, sum_recv).wait()
    cells = step_count * n_lag * half * n_sketch * n_probe
    mean = lax.max(jnp.sum(sums[...], axis=0, keepdims=True), 0.0) / cells
    factor[...] = jnp.broadcast_to(lax.rsqrt(mean + 1e-06), factor.shape)


def near(sizes, markov, test_matrix):
    n_lag, n_probe, n_sketch = sizes
    step_count, input_count, half = markov.shape
    matrix_rows, _, columns = test_matrix.shape
    lag_total = matrix_rows * n_lag
    later = lag_total - 1
    dma = pltpu.SemaphoreType.DMA
    return pl.pallas_call(
        functools.partial(near_kernel, sizes, (half * 3 // 4, half * 5 // 8)),
        out_shape=[
            pltpu.VMEM((step_count, half * n_sketch, columns), jnp.float32),
            pltpu.VMEM((8, columns), jnp.float32),
        ],
        in_specs=[pl.BlockSpec(memory_space=pltpu.HBM)] * 2,
        out_specs=[pl.BlockSpec(memory_space=pltpu.VMEM)] * 2,
        scratch_shapes=[
            pltpu.VMEM((n_sketch, step_count + 2 * later, input_count, half), jnp.bfloat16),
            pltpu.VMEM((n_sketch, lag_total, input_count, columns), jnp.bfloat16),
            pltpu.VMEM(((step_count + later) * input_count, step_count * columns), jnp.bfloat16),
            pltpu.VMEM((lag_total * input_count, lag_total * input_count), jnp.float32),
            pltpu.VMEM((later * input_count, later * input_count), jnp.float32),
            pltpu.VMEM((1, columns), jnp.float32),
            pltpu.VMEM((n_lag * n_probe * n_sketch, columns), jnp.float32),
            dma, dma, dma, dma, dma, dma, dma, dma, dma, dma,
            dma, dma((2,)), dma, dma, dma, dma((2,)), dma, dma,
            pltpu.SemaphoreType.REGULAR,
            pltpu.SemaphoreType.REGULAR((n_lag,)),
        ],
        compiler_params=pltpu.CompilerParams(
            collective_id=1, has_side_effects=True, vmem_limit_bytes=59 * 1024 * 1024
        ),
    )(markov, test_matrix)


def is_near(sizes, markov, test_matrix):
    n_lag, n_probe, n_sketch = sizes
    step_count, input_count, half = markov.shape
    lag_total = test_matrix.shape[0] * n_lag
    return n_sketch == 2 and n_lag > 2 and 1 < lag_total <= step_count and half % 512 == 0


def scale_kernel(raw, factor, out, held, sem):
    step_count, probes, columns = raw.shape
    pieces = 8
    part = probes // pieces
    gain = factor[0:1, :]
    for row in range(step_count):
        for piece in range(pieces):
            place = pl.ds(piece * part, part)
            held[row, place] = (raw[row, place] * gain).astype(held.dtype)
            pltpu.make_async_copy(held.at[row, place], out.at[row, place], sem).start()
    pltpu.make_async_copy(held, out, sem).wait()


def scale(raw, factor):
    step_count, probes, columns = raw.shape
    return pl.pallas_call(
        scale_kernel,
        out_shape=jax.ShapeDtypeStruct(raw.shape, jnp.bfloat16),
        in_specs=[pl.BlockSpec(memory_space=pltpu.VMEM)] * 2,
        out_specs=pl.BlockSpec(memory_space=pltpu.HBM),
        scratch_shapes=[
            pltpu.VMEM(raw.shape, jnp.bfloat16),
            pltpu.SemaphoreType.DMA,
        ],
        compiler_params=pltpu.CompilerParams(vmem_limit_bytes=16 * 1024 * 1024),
    )(raw, factor)


def local(sizes, markov, test_matrix):
    if is_near(sizes, markov, test_matrix):
        return scale(*near(sizes, markov, test_matrix))
    n_lag, n_probe, n_sketch = sizes
    step_count, input_count, half = markov.shape
    matrix_rows, _, columns = test_matrix.shape
    lag_total = matrix_rows * n_lag
    steps, pieces = plan(step_count, lag_total)
    count = max(len(pieces), 1)
    pairs = max(n_sketch - 1, 1)
    probes = half * n_sketch
    dma = pltpu.SemaphoreType.DMA
    raw, factor = pl.pallas_call(
        functools.partial(gather_kernel, sizes),
        out_shape=[
            pltpu.VMEM((step_count, probes, columns), jnp.float32),
            pltpu.VMEM((8, columns), jnp.float32),
        ],
        in_specs=[pl.BlockSpec(memory_space=pltpu.HBM)] * 2,
        out_specs=[pl.BlockSpec(memory_space=pltpu.VMEM)] * 2,
        scratch_shapes=[
            pltpu.VMEM((n_sketch, steps, input_count, half), jnp.bfloat16),
            pltpu.VMEM((lag_total, input_count, columns), jnp.bfloat16),
            pltpu.VMEM((steps * input_count, step_count * columns), jnp.bfloat16),
            pltpu.VMEM((n_lag * n_probe, columns), jnp.float32),
            dma, dma, dma, dma,
            dma((pairs,)), dma((pairs,)),
            dma((count,)), dma((count,)),
            dma((count, pairs)), dma((count, pairs)),
            dma, dma,
        ],
        compiler_params=pltpu.CompilerParams(
            collective_id=0, has_side_effects=True, vmem_limit_bytes=59 * 1024 * 1024
        ),
    )(markov, test_matrix)
    return scale(raw, factor)


def solution(mesh):
    sizes = tuple(mesh.shape[name] for name in ("lag", "probe", "sketch"))
    return jax.shard_map(
        functools.partial(local, sizes),
        mesh=mesh,
        in_specs=(P("lag", None, ("probe", "sketch")), P("lag", None, "sketch")),
        out_specs=P("lag", "probe", "sketch"),
        check_vma=False,
    )
```

```python
import functools

import jax
import jax.numpy as jnp
from jax import lax
from jax.experimental import pallas as pl
from jax.experimental.pallas import tpu as pltpu
from jax.sharding import PartitionSpec as P

MESH = pl.DeviceIdType.MESH
UNROLL = 32


def loop(count, body):
    if count <= UNROLL:
        for index in range(count):
            body(index)
    else:
        def step(index, carry):
            body(index)
            return carry
        lax.fori_loop(0, count, step, 0)


def plan(step_count, lag_total):
    steps = step_count + lag_total - 1
    blocks = (steps - 1) // step_count
    pieces = []
    for ahead in range(1, blocks + 1):
        used = min(step_count, steps - ahead * step_count)
        if blocks == 1:
            pieces += [(ahead, at, 1) for at in range(used)]
        else:
            pieces.append((ahead, 0, used))
    return steps, pieces


def gather_kernel(
    sizes, markov, matrix, raw, factor,
    window, held, weights, sums,
    own_sem, matrix_own_sem, matrix_send, matrix_recv,
    pair_send, pair_recv, lag_send, lag_recv, next_send, next_recv, sum_send, sum_recv,
):
    n_lag, n_probe, n_sketch = sizes
    step_count, input_count, half = markov.shape
    matrix_rows = matrix.shape[0]
    columns = matrix.shape[2]
    lag_total = matrix_rows * n_lag
    steps, pieces = plan(step_count, lag_total)
    lag = lax.axis_index("lag")
    probe = lax.axis_index("probe")
    sketch = lax.axis_index("sketch")
    flat = lag * n_probe + probe
    peers = n_lag * n_probe - 1

    def peer(index):
        other = lax.rem(flat + 1 + index, peers + 1)
        return {
            "lag": lax.div(other, n_probe),
            "probe": lax.rem(other, n_probe),
            "sketch": sketch,
        }

    def partner(index):
        return {"lag": lag, "probe": probe, "sketch": lax.rem(sketch + 1 + index, n_sketch)}

    def lag_peer(index):
        return {"lag": lax.rem(lag + 1 + index, n_lag), "probe": probe, "sketch": sketch}

    barrier = pltpu.get_barrier_semaphore()

    def greet(index):
        pl.semaphore_signal(barrier, inc=1, device_id=peer(index), device_id_type=MESH)

    for index in range(n_sketch - 1):
        pl.semaphore_signal(barrier, inc=1, device_id=partner(index), device_id_type=MESH)
    loop(peers, greet)

    own = pltpu.make_async_copy(markov, window.at[sketch, pl.ds(0, step_count)], own_sem)
    own.start()
    matrix_own = pltpu.make_async_copy(
        matrix, held.at[pl.ds(lag * matrix_rows, matrix_rows)], matrix_own_sem
    )
    matrix_own.start()
    weights[...] = jnp.zeros_like(weights)
    for ahead, at, count in pieces:
        @pl.when(lag + ahead >= n_lag)
        def _():
            place = pl.ds(ahead * step_count + at, count)
            window[:, place] = jnp.zeros((n_sketch, count, input_count, half), window.dtype)

    matrix_own.wait()
    pl.semaphore_wait(barrier, peers + n_sketch - 1)

    def lag_copy(number):
        ahead, at, count = pieces[number]
        return pltpu.make_async_remote_copy(
            src_ref=markov.at[pl.ds(at, count)],
            dst_ref=window.at[sketch, pl.ds(ahead * step_count + at, count)],
            send_sem=lag_send.at[number],
            recv_sem=lag_recv.at[number],
            device_id={"lag": lax.max(lag - ahead, 0), "probe": probe, "sketch": sketch},
            device_id_type=MESH,
        )

    def pair_copy(index):
        return pltpu.make_async_remote_copy(
            src_ref=markov,
            dst_ref=window.at[sketch, pl.ds(0, step_count)],
            send_sem=pair_send.at[index],
            recv_sem=pair_recv.at[index],
            device_id=partner(index),
            device_id_type=MESH,
        )

    def next_copy(number, index):
        ahead, at, count = pieces[number]
        place = window.at[sketch, pl.ds(ahead * step_count + at, count)]
        return pltpu.make_async_remote_copy(
            src_ref=place,
            dst_ref=place,
            send_sem=next_send.at[number, index],
            recv_sem=next_recv.at[number, index],
            device_id=partner(index),
            device_id_type=MESH,
        )

    def matrix_copy(index):
        return pltpu.make_async_remote_copy(
            src_ref=held.at[pl.ds(lag * matrix_rows, matrix_rows)],
            dst_ref=held.at[pl.ds(lag * matrix_rows, matrix_rows)],
            send_sem=matrix_send,
            recv_sem=matrix_recv,
            device_id=lag_peer(index),
            device_id_type=MESH,
        )

    loop(n_lag - 1, lambda index: matrix_copy(index).start())
    for number in range(0, 1):
        @pl.when(lag >= pieces[number][0])
        def _():
            lag_copy(number).start()
    for index in range(n_sketch - 1):
        pair_copy(index).start()
    for number in range(1, len(pieces)):
        @pl.when(lag >= pieces[number][0])
        def _():
            lag_copy(number).start()

    if n_lag > 1:
        arrived = held.at[pl.ds(0, (n_lag - 1) * matrix_rows)]
        pltpu.make_async_copy(arrived, arrived, matrix_recv).wait()
        pltpu.make_async_copy(arrived, arrived, matrix_send).wait()
    for row in range(step_count):
        weights[pl.ds(row * input_count, lag_total * input_count), row * columns:(row + 1) * columns] = (
            held[...].reshape(lag_total * input_count, columns)
        )

    def forward(number):
        @pl.when(lag + pieces[number][0] < n_lag)
        def _():
            lag_copy(number).wait_recv()
            for index in range(n_sketch - 1):
                next_copy(number, index).start()

    def landed(number):
        @pl.when(lag + pieces[number][0] < n_lag)
        def _():
            for index in range(n_sketch - 1):
                next_copy(number, index).wait()

    tile = min(256, half)
    group = 2 if step_count % 2 == 0 else 1

    def compute(first, total):
        depth = (lag_total + group - 1) * input_count
        weight = weights[pl.ds(first * input_count, depth), first * columns:(first + group) * columns]
        for side in range(n_sketch):
            def body(at, total):
                start = pl.multiple_of(at * tile, tile)
                block = window[side, pl.ds(first, lag_total + group - 1), :, pl.ds(start, tile)]
                product = lax.dot_general(
                    block.reshape(depth, tile), weight, (((0,), (0,)), ((), ())),
                    preferred_element_type=jnp.float32,
                )
                for row in range(group):
                    part = product[:, row * columns:(row + 1) * columns]
                    raw[first + row, pl.ds(side * half + start, tile), :] = part
                    total = total + jnp.sum((part * part).reshape(tile // 8, 8, columns), axis=0)
                return total
            total = lax.fori_loop(0, half // tile, body, total, unroll=depth <= 512)
        return total

    own.wait()
    total = jnp.zeros((8, columns), jnp.float32)
    done = 0
    paired = False
    for first in range(0, step_count, group):
        need = first + group - 1 + lag_total
        ready = done
        while ready < len(pieces) and pieces[ready][0] * step_count + pieces[ready][1] < need:
            forward(ready)
            ready += 1
        if not paired:
            for index in range(n_sketch - 1):
                pair_copy(index).wait()
            paired = True
        for number in range(done, ready):
            landed(number)
        done = ready
        total = compute(first, total)

    sums[pl.ds(flat, 1), :] = jnp.sum(total, axis=0, keepdims=True)

    def sum_copy(index):
        place = sums.at[pl.ds(flat, 1)]
        return pltpu.make_async_remote_copy(
            src_ref=place,
            dst_ref=place,
            send_sem=sum_send,
            recv_sem=sum_recv,
            device_id=peer(index),
            device_id_type=MESH,
        )

    loop(peers, lambda index: sum_copy(index).start())
    for number in range(len(pieces)):
        @pl.when(lag >= pieces[number][0])
        def _():
            lag_copy(number).wait_send()
    if peers:
        arrived = sums.at[pl.ds(0, peers)]
        pltpu.make_async_copy(arrived, arrived, sum_recv).wait()
        pltpu.make_async_copy(arrived, arrived, sum_send).wait()
    cells = step_count * n_lag * half * n_sketch * n_probe
    mean = jnp.sum(sums[...], axis=0, keepdims=True) / cells
    factor[...] = jnp.broadcast_to(lax.rsqrt(mean + 1e-06), factor.shape)


def near_kernel(
    sizes, cuts, markov, matrix, raw, factor,
    window, held, weights, gram, joint, other, sums,
    own_sem, matrix_own_sem, matrix_send, matrix_recv, first_recv, twin_send, twin_recv, hand_send, pair_send, pair_recv,
    down_send, down_recv, up_send, up_recv, pass_recv, sum_send, sum_recv, all_in, risen,
):
    n_lag, n_probe, n_sketch = sizes
    step_count, input_count, half = markov.shape
    columns = matrix.shape[2]
    matrix_rows = matrix.shape[0]
    lag_total = matrix_rows * n_lag
    depth = lag_total * input_count
    later = lag_total - 1
    alone = step_count - later
    lag = lax.axis_index("lag")
    probe = lax.axis_index("probe")
    sketch = lax.axis_index("sketch")
    twin = 1 - sketch
    place = (lag * n_probe + probe) * n_sketch + sketch
    devices = n_lag * n_probe * n_sketch
    is_first = lag == 0
    is_last = lag == n_lag - 1
    is_middle = jnp.logical_not(jnp.logical_or(is_first, is_last))
    head = n_probe * n_sketch - 1
    is_head = place == head
    below = {"lag": lax.max(lag - 1, 0), "probe": probe, "sketch": sketch}
    above = {"lag": lax.min(lag + 1, n_lag - 1), "probe": probe, "sketch": sketch}
    partner = {"lag": lag, "probe": probe, "sketch": twin}

    def device(index):
        group = lax.div(index, n_sketch)
        return {
            "lag": lax.div(group, n_probe),
            "probe": lax.rem(group, n_probe),
            "sketch": lax.rem(index, n_sketch),
        }

    last = n_lag - 1

    def at_lag(to_lag, side):
        return {"lag": to_lag, "probe": probe, "sketch": side}

    barrier = pltpu.get_barrier_semaphore()

    def greet(to):
        pl.semaphore_signal(barrier, inc=1, device_id=to, device_id_type=MESH)

    @pl.when(jnp.logical_not(is_first))
    def _():
        greet(at_lag(0, sketch))
        greet(at_lag(0, twin))

    for to_lag in range(1, n_lag):
        @pl.when(lag < to_lag)
        def _():
            greet(at_lag(to_lag, sketch))

    greet(partner)

    @pl.when(probe < n_probe - 1)
    def _():
        greet(device(head))

    expected = lax.select(is_first, 2 * n_lag - 1, lag + 1)

    own_slots = pl.ds(later, step_count)
    next_slots = pl.ds(later + step_count, later)
    own_rows = held.at[sketch, pl.ds(lag * matrix_rows, matrix_rows)]
    matrix_own = pltpu.make_async_copy(matrix, own_rows, matrix_own_sem)
    matrix_own.start()
    own = pltpu.make_async_copy(markov, window.at[sketch, own_slots], own_sem)
    own.start()
    weights[...] = jnp.zeros_like(weights)

    @pl.when(is_last)
    def _():
        window[:, next_slots] = jnp.zeros((n_sketch, later, input_count, half), window.dtype)

    def parts(edge):
        return pl.ds(0, cuts[edge]), pl.ds(cuts[edge], half - cuts[edge])

    def remote(src, dst, send, recv, to):
        return pltpu.make_async_remote_copy(
            src_ref=src, dst_ref=dst, send_sem=send, recv_sem=recv, device_id=to, device_id_type=MESH
        )

    def down(part, edge):
        return remote(
            window.at[sketch, pl.ds(later, later), :, parts(edge)[part]],
            window.at[sketch, next_slots, :, parts(edge)[part]],
            down_send, down_recv.at[part], below,
        )

    def up(edge):
        return remote(
            window.at[sketch, pl.ds(later + alone, later), :, parts(edge)[1]],
            window.at[sketch, pl.ds(0, later), :, parts(edge)[1]],
            up_send, up_recv, above,
        )

    def edge_above(body):
        for edge in range(2):
            pl.when(is_first if edge == 0 else is_middle)(functools.partial(body, edge))

    def edge_below(body):
        for edge in range(2):
            pl.when(lag == 1 if edge == 0 else lag > 1)(functools.partial(body, edge))

    def passed(part, edge):
        ref = window.at[sketch, next_slots, :, parts(edge)[part]]
        return remote(ref, ref, pair_send, pass_recv.at[part], partner)

    pair = remote(
        window.at[sketch, own_slots], window.at[sketch, own_slots], pair_send, pair_recv, partner
    )

    def outer(first, second, start, stop):
        def rows(slots):
            slot, count = slots
            return window[sketch, pl.ds(slot, count), :, start:stop].reshape(count * input_count, stop - start)
        return lax.dot_general(
            rows(first), rows(second), (((1,), (1,)), ((), ())), preferred_element_type=jnp.float32
        )

    def own_gram():
        inner = outer((later, step_count), (later, step_count), 0, half)
        gram[...] = jnp.zeros_like(gram)
        joint[...] = jnp.zeros_like(joint)

        def shift(row):
            low, high = max(0, -row), min(lag_total, step_count - row)
            to = slice(low * input_count, high * input_count)
            at = slice((row + low) * input_count, (row + high) * input_count)
            gram[to, to] += inner[at, at]

        for row in range(step_count):
            shift(row)

        @pl.when(jnp.logical_not(is_first))
        def _():
            for row in range(-later, 0):
                shift(row)

    def matrix_copy(to_lag, recv=matrix_recv):
        return remote(own_rows, own_rows, matrix_send, recv, at_lag(to_lag, sketch))

    def matrix_twin(to_lag):
        return remote(own_rows, own_rows, twin_send, twin_recv, at_lag(to_lag, twin))

    matrix_hand = remote(held.at[sketch], held.at[sketch], hand_send, twin_recv, partner)
    rest_rows = held.at[sketch, pl.ds(matrix_rows, lag_total - matrix_rows)]
    rest_hand = remote(rest_rows, rest_rows, hand_send, twin_recv, partner)

    @pl.when(is_first)
    def _():
        own.wait()
        own_gram()

    pl.semaphore_wait(barrier, lax.select(is_head, devices - 1, expected))
    for from_lag in range(2, n_lag):
        @pl.when(lag == from_lag)
        def _():
            for to_lag in range(1, from_lag):
                pl.semaphore_signal(
                    risen.at[from_lag - 2], inc=1, device_id=at_lag(to_lag, sketch), device_id_type=MESH
                )

    matrix_own.wait()

    @pl.when(is_first)
    def _():
        for to_lag in reversed(range(1, n_lag)):
            matrix_copy(to_lag, first_recv).start()
            matrix_twin(to_lag).start()
        up(0).start()

    @pl.when(jnp.logical_not(is_first))
    def _():
        for to_lag in range(last):
            @pl.when(lag > to_lag)
            def _():
                matrix_copy(to_lag).start()
        own.wait()
        edge_below(lambda edge: down(0, edge).start())

        @pl.when(is_last)
        def _():
            matrix_twin(last).start()

        own_gram()

    for here in range(1, last):
        @pl.when(lag == here)
        def _():
            for to_lag in range(here + 1, n_lag):
                pl.semaphore_wait(risen.at[to_lag - 2], 1)
                if to_lag == here + 1:
                    up(1).start()
                matrix_copy(to_lag).start()
            matrix_twin(last).start()

    @pl.when(is_head)
    def _():
        loop(devices - 1, lambda index: pl.semaphore_signal(
            all_in, inc=1, device_id=device(lax.rem(place + 1 + index, devices)), device_id_type=MESH
        ))

    def cross(edge):
        for row in range(alone, step_count):
            count = (step_count - row) * input_count
            gram[0:count, count:depth] += 2.0 * edge[(row - alone) * input_count:, 0:(row - alone + 1) * input_count]

    others = held.at[sketch, pl.ds(0, lag_total - matrix_rows)]

    middle_rows = held.at[sketch, pl.ds(0, lag_total - 2 * matrix_rows)]

    @pl.when(is_first)
    def _():
        pltpu.make_async_copy(others, others, matrix_recv).wait()
        matrix_hand.start()

    @pl.when(is_middle)
    def _():
        pltpu.make_async_copy(middle_rows, middle_rows, matrix_recv).wait()
        rest_hand.start()

    @pl.when(is_middle)
    def _():
        edge_below(lambda edge: down(1, edge).start())

    def from_below(edge):
        up(edge).wait_recv()
        joint[...] += outer((0, later), (later, later), cuts[edge], half)

    def from_above(edge):
        down(0, edge).wait_recv()
        joint[...] += outer((later + alone, later), (later + step_count, later), 0, cuts[edge])

    edge_below(from_below)
    edge_above(from_above)
    cross(joint[...])

    whole = gram[...]
    high = whole.astype(jnp.bfloat16)
    rest = whole - high.astype(jnp.float32)
    middle = rest.astype(jnp.bfloat16)
    low = (rest - middle.astype(jnp.float32)).astype(jnp.bfloat16)

    @pl.when(is_last)
    def _():
        if n_lag > 2:
            pltpu.make_async_copy(middle_rows, middle_rows, matrix_recv).wait()

    @pl.when(jnp.logical_not(is_first))
    def _():
        pltpu.make_async_copy(own_rows, own_rows, first_recv).wait()

    matrix_hand.wait_recv()
    mine = held[sketch].reshape(depth, columns)
    both = jnp.concatenate([mine, held[twin].reshape(depth, columns)], axis=1)
    product = jnp.dot(low, both, preferred_element_type=jnp.float32)
    product = product + jnp.dot(middle, both, preferred_element_type=jnp.float32)
    product = product + jnp.dot(high, both, preferred_element_type=jnp.float32)
    square = jnp.sum(product * both.astype(jnp.float32), axis=0, keepdims=True)
    sums[pl.ds(place, 1), :] = square[:, :columns]
    other[...] = square[:, columns:]

    def sum_copy(at, side):
        to = {"lag": lax.div(at, n_probe), "probe": lax.rem(at, n_probe), "sketch": side}
        ref = sums.at[pl.ds(place, 1)]
        src = other if side is twin else ref
        return remote(src, ref, sum_send, sum_recv, to)

    @pl.when(jnp.logical_not(is_head))
    def _():
        pl.semaphore_wait(all_in, 1)

    group = lag * n_probe + probe

    def send_sums(index):
        sum_copy(index, twin).start()
        sum_copy(lax.select(index < group, index, index + 1), sketch).start()

    loop(n_lag * n_probe - 1, send_sums)
    sum_copy(n_lag * n_probe - 1, twin).start()

    @pl.when(is_last)
    def _():
        down(1, 1).start()

    pair.start()

    edge_above(lambda edge: passed(0, edge).start())

    for row in range(step_count):
        weights[pl.ds(row * input_count, depth), row * columns:(row + 1) * columns] = mine

    tile = 128

    def multiply(side, first, last):
        for start in range(first, last, tile):
            block = window[side, pl.ds(later, step_count + later), :, pl.ds(start, tile)]
            product = lax.dot_general(
                block.reshape((step_count + later) * input_count, tile), weights[...], (((0,), (0,)), ((), ())),
                preferred_element_type=jnp.float32,
            )
            for row in range(step_count):
                raw[row, pl.ds(pl.multiple_of(side * half + start, tile), tile), :] = (
                    product[:, row * columns:(row + 1) * columns]
                )

    cut = min(cuts)
    multiply(sketch, 0, cut)
    pair.wait_recv()

    edge_above(lambda edge: passed(0, edge).wait_recv())

    multiply(twin, 0, cut)

    def hand_rest(edge):
        down(1, edge).wait_recv()
        passed(1, edge).start()

    edge_above(hand_rest)

    multiply(sketch, cut, half)

    edge_above(lambda edge: passed(1, edge).wait_recv())

    multiply(twin, cut, half)

    received = window.at[sketch, next_slots]

    @pl.when(is_last)
    def _():
        pair.wait_send()

    @pl.when(jnp.logical_not(is_last))
    def _():
        sent = window.at[sketch, pl.ds(later, step_count + later)]
        pltpu.make_async_copy(sent, sent, pair_send).wait()
        edge_above(lambda edge: up(edge).wait_send())

    @pl.when(is_first)
    def _():
        matrix_hand.wait_send()
        pltpu.make_async_copy(others, others, twin_send).wait()

    @pl.when(jnp.logical_not(is_first))
    def _():
        matrix_twin(last).wait_send()

        @pl.when(jnp.logical_not(is_last))
        def _():
            rest_hand.wait_send()

    @pl.when(jnp.logical_not(is_first))
    def _():
        pltpu.make_async_copy(received, received, down_send).wait()

    pltpu.make_async_copy(others, others, matrix_send).wait()
    landed = sums.at[pl.ds(0, devices - 1)]
    pltpu.make_async_copy(landed, landed, sum_send).wait()
    pltpu.make_async_copy(landed, landed, sum_recv).wait()
    cells = step_count * n_lag * half * n_sketch * n_probe
    mean = lax.max(jnp.sum(sums[...], axis=0, keepdims=True), 0.0) / cells
    factor[...] = jnp.broadcast_to(lax.rsqrt(mean + 1e-06), factor.shape)


def near(sizes, markov, test_matrix):
    n_lag, n_probe, n_sketch = sizes
    step_count, input_count, half = markov.shape
    matrix_rows, _, columns = test_matrix.shape
    lag_total = matrix_rows * n_lag
    later = lag_total - 1
    dma = pltpu.SemaphoreType.DMA
    return pl.pallas_call(
        functools.partial(near_kernel, sizes, (half * 7 // 8, half * 5 // 8)),
        out_shape=[
            pltpu.VMEM((step_count, half * n_sketch, columns), jnp.float32),
            pltpu.VMEM((8, columns), jnp.float32),
        ],
        in_specs=[pl.BlockSpec(memory_space=pltpu.HBM)] * 2,
        out_specs=[pl.BlockSpec(memory_space=pltpu.VMEM)] * 2,
        scratch_shapes=[
            pltpu.VMEM((n_sketch, step_count + 2 * later, input_count, half), jnp.bfloat16),
            pltpu.VMEM((n_sketch, lag_total, input_count, columns), jnp.bfloat16),
            pltpu.VMEM(((step_count + later) * input_count, step_count * columns), jnp.bfloat16),
            pltpu.VMEM((lag_total * input_count, lag_total * input_count), jnp.float32),
            pltpu.VMEM((later * input_count, later * input_count), jnp.float32),
            pltpu.VMEM((1, columns), jnp.float32),
            pltpu.VMEM((n_lag * n_probe * n_sketch, columns), jnp.float32),
            dma, dma, dma, dma, dma, dma, dma, dma, dma, dma,
            dma, dma((2,)), dma, dma, dma((2,)), dma, dma,
            pltpu.SemaphoreType.REGULAR,
            pltpu.SemaphoreType.REGULAR((n_lag - 2,)),
        ],
        compiler_params=pltpu.CompilerParams(
            collective_id=1, has_side_effects=True, vmem_limit_bytes=59 * 1024 * 1024
        ),
    )(markov, test_matrix)


def is_near(sizes, markov, test_matrix):
    n_lag, n_probe, n_sketch = sizes
    step_count, input_count, half = markov.shape
    lag_total = test_matrix.shape[0] * n_lag
    return n_sketch == 2 and n_lag > 2 and 1 < lag_total <= step_count and half % 512 == 0


def scale_kernel(raw, factor, out, held, sem):
    step_count, probes, columns = raw.shape
    pieces = 8
    part = probes // pieces
    gain = factor[0:1, :]
    for row in range(step_count):
        for piece in range(pieces):
            place = pl.ds(piece * part, part)
            held[row, place] = (raw[row, place] * gain).astype(held.dtype)
            pltpu.make_async_copy(held.at[row, place], out.at[row, place], sem).start()
    pltpu.make_async_copy(held, out, sem).wait()


def scale(raw, factor):
    step_count, probes, columns = raw.shape
    return pl.pallas_call(
        scale_kernel,
        out_shape=jax.ShapeDtypeStruct(raw.shape, jnp.bfloat16),
        in_specs=[pl.BlockSpec(memory_space=pltpu.VMEM)] * 2,
        out_specs=pl.BlockSpec(memory_space=pltpu.HBM),
        scratch_shapes=[
            pltpu.VMEM(raw.shape, jnp.bfloat16),
            pltpu.SemaphoreType.DMA,
        ],
        compiler_params=pltpu.CompilerParams(vmem_limit_bytes=16 * 1024 * 1024),
    )(raw, factor)


def local(sizes, markov, test_matrix):
    if is_near(sizes, markov, test_matrix):
        return scale(*near(sizes, markov, test_matrix))
    n_lag, n_probe, n_sketch = sizes
    step_count, input_count, half = markov.shape
    matrix_rows, _, columns = test_matrix.shape
    lag_total = matrix_rows * n_lag
    steps, pieces = plan(step_count, lag_total)
    count = max(len(pieces), 1)
    pairs = max(n_sketch - 1, 1)
    probes = half * n_sketch
    dma = pltpu.SemaphoreType.DMA
    raw, factor = pl.pallas_call(
        functools.partial(gather_kernel, sizes),
        out_shape=[
            pltpu.VMEM((step_count, probes, columns), jnp.float32),
            pltpu.VMEM((8, columns), jnp.float32),
        ],
        in_specs=[pl.BlockSpec(memory_space=pltpu.HBM)] * 2,
        out_specs=[pl.BlockSpec(memory_space=pltpu.VMEM)] * 2,
        scratch_shapes=[
            pltpu.VMEM((n_sketch, steps, input_count, half), jnp.bfloat16),
            pltpu.VMEM((lag_total, input_count, columns), jnp.bfloat16),
            pltpu.VMEM((steps * input_count, step_count * columns), jnp.bfloat16),
            pltpu.VMEM((n_lag * n_probe, columns), jnp.float32),
            dma, dma, dma, dma,
            dma((pairs,)), dma((pairs,)),
            dma((count,)), dma((count,)),
            dma((count, pairs)), dma((count, pairs)),
            dma, dma,
        ],
        compiler_params=pltpu.CompilerParams(
            collective_id=0, has_side_effects=True, vmem_limit_bytes=59 * 1024 * 1024
        ),
    )(markov, test_matrix)
    return scale(raw, factor)


def solution(mesh):
    sizes = tuple(mesh.shape[name] for name in ("lag", "probe", "sketch"))
    return jax.shard_map(
        functools.partial(local, sizes),
        mesh=mesh,
        in_specs=(P("lag", None, ("probe", "sketch")), P("lag", None, "sketch")),
        out_specs=P("lag", "probe", "sketch"),
        check_vma=False,
    )
```

```python
import functools

import jax
import jax.numpy as jnp
from jax import lax
from jax.experimental import pallas as pl
from jax.experimental.pallas import tpu as pltpu
from jax.sharding import PartitionSpec as P

MESH = pl.DeviceIdType.MESH
UNROLL = 32


def loop(count, body):
    if count <= UNROLL:
        for index in range(count):
            body(index)
    else:
        def step(index, carry):
            body(index)
            return carry
        lax.fori_loop(0, count, step, 0)


def plan(step_count, lag_total):
    steps = step_count + lag_total - 1
    blocks = (steps - 1) // step_count
    pieces = []
    for ahead in range(1, blocks + 1):
        used = min(step_count, steps - ahead * step_count)
        if blocks == 1:
            pieces += [(ahead, at, 1) for at in range(used)]
        else:
            pieces.append((ahead, 0, used))
    return steps, pieces


def gather_kernel(
    sizes, markov, matrix, raw, factor,
    window, held, weights, sums,
    own_sem, matrix_own_sem, matrix_send, matrix_recv,
    pair_send, pair_recv, lag_send, lag_recv, next_send, next_recv, sum_send, sum_recv,
):
    n_lag, n_probe, n_sketch = sizes
    step_count, input_count, half = markov.shape
    matrix_rows = matrix.shape[0]
    columns = matrix.shape[2]
    lag_total = matrix_rows * n_lag
    steps, pieces = plan(step_count, lag_total)
    lag = lax.axis_index("lag")
    probe = lax.axis_index("probe")
    sketch = lax.axis_index("sketch")
    flat = lag * n_probe + probe
    peers = n_lag * n_probe - 1

    def peer(index):
        other = lax.rem(flat + 1 + index, peers + 1)
        return {
            "lag": lax.div(other, n_probe),
            "probe": lax.rem(other, n_probe),
            "sketch": sketch,
        }

    def partner(index):
        return {"lag": lag, "probe": probe, "sketch": lax.rem(sketch + 1 + index, n_sketch)}

    def lag_peer(index):
        return {"lag": lax.rem(lag + 1 + index, n_lag), "probe": probe, "sketch": sketch}

    barrier = pltpu.get_barrier_semaphore()

    def greet(index):
        pl.semaphore_signal(barrier, inc=1, device_id=peer(index), device_id_type=MESH)

    for index in range(n_sketch - 1):
        pl.semaphore_signal(barrier, inc=1, device_id=partner(index), device_id_type=MESH)
    loop(peers, greet)

    own = pltpu.make_async_copy(markov, window.at[sketch, pl.ds(0, step_count)], own_sem)
    own.start()
    matrix_own = pltpu.make_async_copy(
        matrix, held.at[pl.ds(lag * matrix_rows, matrix_rows)], matrix_own_sem
    )
    matrix_own.start()
    weights[...] = jnp.zeros_like(weights)
    for ahead, at, count in pieces:
        @pl.when(lag + ahead >= n_lag)
        def _():
            place = pl.ds(ahead * step_count + at, count)
            window[:, place] = jnp.zeros((n_sketch, count, input_count, half), window.dtype)

    matrix_own.wait()
    pl.semaphore_wait(barrier, peers + n_sketch - 1)

    def lag_copy(number):
        ahead, at, count = pieces[number]
        return pltpu.make_async_remote_copy(
            src_ref=markov.at[pl.ds(at, count)],
            dst_ref=window.at[sketch, pl.ds(ahead * step_count + at, count)],
            send_sem=lag_send.at[number],
            recv_sem=lag_recv.at[number],
            device_id={"lag": lax.max(lag - ahead, 0), "probe": probe, "sketch": sketch},
            device_id_type=MESH,
        )

    def pair_copy(index):
        return pltpu.make_async_remote_copy(
            src_ref=markov,
            dst_ref=window.at[sketch, pl.ds(0, step_count)],
            send_sem=pair_send.at[index],
            recv_sem=pair_recv.at[index],
            device_id=partner(index),
            device_id_type=MESH,
        )

    def next_copy(number, index):
        ahead, at, count = pieces[number]
        place = window.at[sketch, pl.ds(ahead * step_count + at, count)]
        return pltpu.make_async_remote_copy(
            src_ref=place,
            dst_ref=place,
            send_sem=next_send.at[number, index],
            recv_sem=next_recv.at[number, index],
            device_id=partner(index),
            device_id_type=MESH,
        )

    def matrix_copy(index):
        return pltpu.make_async_remote_copy(
            src_ref=held.at[pl.ds(lag * matrix_rows, matrix_rows)],
            dst_ref=held.at[pl.ds(lag * matrix_rows, matrix_rows)],
            send_sem=matrix_send,
            recv_sem=matrix_recv,
            device_id=lag_peer(index),
            device_id_type=MESH,
        )

    loop(n_lag - 1, lambda index: matrix_copy(index).start())
    for number in range(0, 1):
        @pl.when(lag >= pieces[number][0])
        def _():
            lag_copy(number).start()
    for index in range(n_sketch - 1):
        pair_copy(index).start()
    for number in range(1, len(pieces)):
        @pl.when(lag >= pieces[number][0])
        def _():
            lag_copy(number).start()

    if n_lag > 1:
        arrived = held.at[pl.ds(0, (n_lag - 1) * matrix_rows)]
        pltpu.make_async_copy(arrived, arrived, matrix_recv).wait()
        pltpu.make_async_copy(arrived, arrived, matrix_send).wait()
    for row in range(step_count):
        weights[pl.ds(row * input_count, lag_total * input_count), row * columns:(row + 1) * columns] = (
            held[...].reshape(lag_total * input_count, columns)
        )

    def forward(number):
        @pl.when(lag + pieces[number][0] < n_lag)
        def _():
            lag_copy(number).wait_recv()
            for index in range(n_sketch - 1):
                next_copy(number, index).start()

    def landed(number):
        @pl.when(lag + pieces[number][0] < n_lag)
        def _():
            for index in range(n_sketch - 1):
                next_copy(number, index).wait()

    tile = min(256, half)
    group = 2 if step_count % 2 == 0 else 1

    def compute(first, total):
        depth = (lag_total + group - 1) * input_count
        weight = weights[pl.ds(first * input_count, depth), first * columns:(first + group) * columns]
        for side in range(n_sketch):
            def body(at, total):
                start = pl.multiple_of(at * tile, tile)
                block = window[side, pl.ds(first, lag_total + group - 1), :, pl.ds(start, tile)]
                product = lax.dot_general(
                    block.reshape(depth, tile), weight, (((0,), (0,)), ((), ())),
                    preferred_element_type=jnp.float32,
                )
                for row in range(group):
                    part = product[:, row * columns:(row + 1) * columns]
                    raw[first + row, pl.ds(side * half + start, tile), :] = part
                    total = total + jnp.sum((part * part).reshape(tile // 8, 8, columns), axis=0)
                return total
            total = lax.fori_loop(0, half // tile, body, total, unroll=depth <= 512)
        return total

    own.wait()
    total = jnp.zeros((8, columns), jnp.float32)
    done = 0
    paired = False
    for first in range(0, step_count, group):
        need = first + group - 1 + lag_total
        ready = done
        while ready < len(pieces) and pieces[ready][0] * step_count + pieces[ready][1] < need:
            forward(ready)
            ready += 1
        if not paired:
            for index in range(n_sketch - 1):
                pair_copy(index).wait()
            paired = True
        for number in range(done, ready):
            landed(number)
        done = ready
        total = compute(first, total)

    sums[pl.ds(flat, 1), :] = jnp.sum(total, axis=0, keepdims=True)

    def sum_copy(index):
        place = sums.at[pl.ds(flat, 1)]
        return pltpu.make_async_remote_copy(
            src_ref=place,
            dst_ref=place,
            send_sem=sum_send,
            recv_sem=sum_recv,
            device_id=peer(index),
            device_id_type=MESH,
        )

    loop(peers, lambda index: sum_copy(index).start())
    for number in range(len(pieces)):
        @pl.when(lag >= pieces[number][0])
        def _():
            lag_copy(number).wait_send()
    if peers:
        arrived = sums.at[pl.ds(0, peers)]
        pltpu.make_async_copy(arrived, arrived, sum_recv).wait()
        pltpu.make_async_copy(arrived, arrived, sum_send).wait()
    cells = step_count * n_lag * half * n_sketch * n_probe
    mean = jnp.sum(sums[...], axis=0, keepdims=True) / cells
    factor[...] = jnp.broadcast_to(lax.rsqrt(mean + 1e-06), factor.shape)


def near_kernel(
    sizes, cuts, markov, matrix, raw, factor,
    window, held, weights, gram, joint, other, sums,
    own_sem, matrix_own_sem, matrix_send, matrix_recv, first_recv, twin_send, twin_recv, hand_send, pair_send, pair_recv,
    down_send, down_recv, up_send, up_recv, pass_recv, sum_send, sum_recv, all_in, risen,
):
    n_lag, n_probe, n_sketch = sizes
    step_count, input_count, half = markov.shape
    columns = matrix.shape[2]
    matrix_rows = matrix.shape[0]
    lag_total = matrix_rows * n_lag
    depth = lag_total * input_count
    later = lag_total - 1
    alone = step_count - later
    lag = lax.axis_index("lag")
    probe = lax.axis_index("probe")
    sketch = lax.axis_index("sketch")
    twin = 1 - sketch
    place = (lag * n_probe + probe) * n_sketch + sketch
    devices = n_lag * n_probe * n_sketch
    is_first = lag == 0
    is_last = lag == n_lag - 1
    is_middle = jnp.logical_not(jnp.logical_or(is_first, is_last))
    head = n_probe * n_sketch - 1
    is_head = place == head
    below = {"lag": lax.max(lag - 1, 0), "probe": probe, "sketch": sketch}
    above = {"lag": lax.min(lag + 1, n_lag - 1), "probe": probe, "sketch": sketch}
    partner = {"lag": lag, "probe": probe, "sketch": twin}

    def device(index):
        group = lax.div(index, n_sketch)
        return {
            "lag": lax.div(group, n_probe),
            "probe": lax.rem(group, n_probe),
            "sketch": lax.rem(index, n_sketch),
        }

    last = n_lag - 1

    def at_lag(to_lag, side):
        return {"lag": to_lag, "probe": probe, "sketch": side}

    barrier = pltpu.get_barrier_semaphore()

    def greet(to):
        pl.semaphore_signal(barrier, inc=1, device_id=to, device_id_type=MESH)

    @pl.when(jnp.logical_not(is_first))
    def _():
        greet(at_lag(0, sketch))
        greet(at_lag(0, twin))

    for to_lag in range(1, n_lag):
        @pl.when(lag < to_lag)
        def _():
            greet(at_lag(to_lag, sketch))

    greet(partner)

    @pl.when(probe < n_probe - 1)
    def _():
        greet(device(head))

    expected = lax.select(is_first, 2 * n_lag - 1, lag + 1)

    own_slots = pl.ds(later, step_count)
    next_slots = pl.ds(later + step_count, later)
    own_rows = held.at[sketch, pl.ds(lag * matrix_rows, matrix_rows)]
    matrix_own = pltpu.make_async_copy(matrix, own_rows, matrix_own_sem)
    matrix_own.start()
    own = pltpu.make_async_copy(markov, window.at[sketch, own_slots], own_sem)
    own.start()
    weights[...] = jnp.zeros_like(weights)

    @pl.when(is_last)
    def _():
        window[:, next_slots] = jnp.zeros((n_sketch, later, input_count, half), window.dtype)

    def parts(edge):
        return pl.ds(0, cuts[edge]), pl.ds(cuts[edge], half - cuts[edge])

    def remote(src, dst, send, recv, to):
        return pltpu.make_async_remote_copy(
            src_ref=src, dst_ref=dst, send_sem=send, recv_sem=recv, device_id=to, device_id_type=MESH
        )

    def down(part, edge):
        return remote(
            window.at[sketch, pl.ds(later, later), :, parts(edge)[part]],
            window.at[sketch, next_slots, :, parts(edge)[part]],
            down_send, down_recv.at[part], below,
        )

    def up(edge):
        return remote(
            window.at[sketch, pl.ds(later + alone, later), :, parts(edge)[1]],
            window.at[sketch, pl.ds(0, later), :, parts(edge)[1]],
            up_send, up_recv, above,
        )

    def edge_above(body):
        for edge in range(2):
            pl.when(is_first if edge == 0 else is_middle)(functools.partial(body, edge))

    def edge_below(body):
        for edge in range(2):
            pl.when(lag == 1 if edge == 0 else lag > 1)(functools.partial(body, edge))

    def passed(part, edge):
        ref = window.at[sketch, next_slots, :, parts(edge)[part]]
        return remote(ref, ref, pair_send, pass_recv.at[part], partner)

    pair = remote(
        window.at[sketch, own_slots], window.at[sketch, own_slots], pair_send, pair_recv, partner
    )

    def outer(first, second, start, stop):
        def rows(slots):
            slot, count = slots
            return window[sketch, pl.ds(slot, count), :, start:stop].reshape(count * input_count, stop - start)
        return lax.dot_general(
            rows(first), rows(second), (((1,), (1,)), ((), ())), preferred_element_type=jnp.float32
        )

    def own_gram():
        inner = outer((later, step_count), (later, step_count), 0, half)
        gram[...] = jnp.zeros_like(gram)
        joint[...] = jnp.zeros_like(joint)

        def shift(row):
            low, high = max(0, -row), min(lag_total, step_count - row)
            to = slice(low * input_count, high * input_count)
            at = slice((row + low) * input_count, (row + high) * input_count)
            gram[to, to] += inner[at, at]

        for row in range(step_count):
            shift(row)

        @pl.when(jnp.logical_not(is_first))
        def _():
            for row in range(-later, 0):
                shift(row)

    def matrix_copy(to_lag, recv=matrix_recv):
        return remote(own_rows, own_rows, matrix_send, recv, at_lag(to_lag, sketch))

    def matrix_twin(to_lag):
        return remote(own_rows, own_rows, twin_send, twin_recv, at_lag(to_lag, twin))

    matrix_hand = remote(held.at[sketch], held.at[sketch], hand_send, twin_recv, partner)
    rest_rows = held.at[sketch, pl.ds(matrix_rows, lag_total - matrix_rows)]
    rest_hand = remote(rest_rows, rest_rows, hand_send, twin_recv, partner)

    @pl.when(is_first)
    def _():
        own.wait()
        own_gram()

    pl.semaphore_wait(barrier, lax.select(is_head, devices - 1, expected))
    for from_lag in range(2, n_lag):
        @pl.when(lag == from_lag)
        def _():
            for to_lag in range(1, from_lag):
                pl.semaphore_signal(
                    risen.at[from_lag - 2], inc=1, device_id=at_lag(to_lag, sketch), device_id_type=MESH
                )

    matrix_own.wait()

    @pl.when(is_first)
    def _():
        for to_lag in reversed(range(1, n_lag)):
            matrix_copy(to_lag, first_recv).start()
            matrix_twin(to_lag).start()
        up(0).start()

    @pl.when(jnp.logical_not(is_first))
    def _():
        for to_lag in range(last):
            @pl.when(lag > to_lag)
            def _():
                matrix_copy(to_lag).start()
        own.wait()
        edge_below(lambda edge: down(0, edge).start())

        @pl.when(is_last)
        def _():
            matrix_twin(last).start()

        own_gram()

    for here in range(1, last):
        @pl.when(lag == here)
        def _():
            for to_lag in range(here + 1, n_lag):
                pl.semaphore_wait(risen.at[to_lag - 2], 1)
                if to_lag == here + 1:
                    up(1).start()
                matrix_copy(to_lag).start()
            matrix_twin(last).start()

    @pl.when(is_head)
    def _():
        loop(devices - 1, lambda index: pl.semaphore_signal(
            all_in, inc=1, device_id=device(lax.rem(place + 1 + index, devices)), device_id_type=MESH
        ))

    def cross(edge):
        for row in range(alone, step_count):
            count = (step_count - row) * input_count
            gram[0:count, count:depth] += 2.0 * edge[(row - alone) * input_count:, 0:(row - alone + 1) * input_count]

    others = held.at[sketch, pl.ds(0, lag_total - matrix_rows)]

    middle_rows = held.at[sketch, pl.ds(0, lag_total - 2 * matrix_rows)]

    @pl.when(is_first)
    def _():
        pltpu.make_async_copy(others, others, matrix_recv).wait()
        matrix_hand.start()

    @pl.when(is_middle)
    def _():
        pltpu.make_async_copy(middle_rows, middle_rows, matrix_recv).wait()
        rest_hand.start()

    @pl.when(is_middle)
    def _():
        edge_below(lambda edge: down(1, edge).start())

    pair.start()

    def from_below(edge):
        up(edge).wait_recv()
        joint[...] += outer((0, later), (later, later), cuts[edge], half)

    def from_above(edge):
        down(0, edge).wait_recv()
        joint[...] += outer((later + alone, later), (later + step_count, later), 0, cuts[edge])

    edge_below(from_below)
    edge_above(from_above)
    cross(joint[...])

    whole = gram[...]
    high = whole.astype(jnp.bfloat16)
    rest = whole - high.astype(jnp.float32)
    middle = rest.astype(jnp.bfloat16)
    low = (rest - middle.astype(jnp.float32)).astype(jnp.bfloat16)

    @pl.when(is_last)
    def _():
        if n_lag > 2:
            pltpu.make_async_copy(middle_rows, middle_rows, matrix_recv).wait()

    @pl.when(jnp.logical_not(is_first))
    def _():
        pltpu.make_async_copy(own_rows, own_rows, first_recv).wait()

    matrix_hand.wait_recv()
    mine = held[sketch].reshape(depth, columns)
    both = jnp.concatenate([mine, held[twin].reshape(depth, columns)], axis=1)
    product = jnp.dot(
        jnp.concatenate([low, middle, high], axis=1), jnp.concatenate([both, both, both], axis=0),
        preferred_element_type=jnp.float32,
    )
    square = jnp.sum(product * both.astype(jnp.float32), axis=0, keepdims=True)
    sums[pl.ds(place, 1), :] = square[:, :columns]
    other[...] = square[:, columns:]

    def sum_copy(at, side):
        to = {"lag": lax.div(at, n_probe), "probe": lax.rem(at, n_probe), "sketch": side}
        ref = sums.at[pl.ds(place, 1)]
        src = other if side is twin else ref
        return remote(src, ref, sum_send, sum_recv, to)

    @pl.when(jnp.logical_not(is_head))
    def _():
        pl.semaphore_wait(all_in, 1)

    group = lag * n_probe + probe

    def send_sums(index):
        sum_copy(index, twin).start()
        sum_copy(lax.select(index < group, index, index + 1), sketch).start()

    loop(n_lag * n_probe - 1, send_sums)
    sum_copy(n_lag * n_probe - 1, twin).start()

    @pl.when(is_last)
    def _():
        down(1, 1).start()

    edge_above(lambda edge: passed(0, edge).start())

    for row in range(step_count):
        weights[pl.ds(row * input_count, depth), row * columns:(row + 1) * columns] = mine

    tile = 128

    def multiply(side, first, last):
        for start in range(first, last, tile):
            block = window[side, pl.ds(later, step_count + later), :, pl.ds(start, tile)]
            product = lax.dot_general(
                block.reshape((step_count + later) * input_count, tile), weights[...], (((0,), (0,)), ((), ())),
                preferred_element_type=jnp.float32,
            )
            for row in range(step_count):
                raw[row, pl.ds(pl.multiple_of(side * half + start, tile), tile), :] = (
                    product[:, row * columns:(row + 1) * columns]
                )

    cut = min(cuts)
    multiply(sketch, 0, cut)
    pair.wait_recv()

    edge_above(lambda edge: passed(0, edge).wait_recv())

    multiply(twin, 0, cut)

    def hand_rest(edge):
        down(1, edge).wait_recv()
        passed(1, edge).start()

    edge_above(hand_rest)

    multiply(sketch, cut, half)

    edge_above(lambda edge: passed(1, edge).wait_recv())

    multiply(twin, cut, half)

    received = window.at[sketch, next_slots]

    @pl.when(is_last)
    def _():
        pair.wait_send()

    @pl.when(jnp.logical_not(is_last))
    def _():
        sent = window.at[sketch, pl.ds(later, step_count + later)]
        pltpu.make_async_copy(sent, sent, pair_send).wait()
        edge_above(lambda edge: up(edge).wait_send())

    @pl.when(is_first)
    def _():
        matrix_hand.wait_send()
        pltpu.make_async_copy(others, others, twin_send).wait()

    @pl.when(jnp.logical_not(is_first))
    def _():
        matrix_twin(last).wait_send()

        @pl.when(jnp.logical_not(is_last))
        def _():
            rest_hand.wait_send()

    @pl.when(jnp.logical_not(is_first))
    def _():
        pltpu.make_async_copy(received, received, down_send).wait()

    pltpu.make_async_copy(others, others, matrix_send).wait()
    landed = sums.at[pl.ds(0, devices - 1)]
    pltpu.make_async_copy(landed, landed, sum_send).wait()
    pltpu.make_async_copy(landed, landed, sum_recv).wait()
    cells = step_count * n_lag * half * n_sketch * n_probe
    mean = lax.max(jnp.sum(sums[...], axis=0, keepdims=True), 0.0) / cells
    factor[...] = jnp.broadcast_to(lax.rsqrt(mean + 1e-06), factor.shape)


def near(sizes, markov, test_matrix):
    n_lag, n_probe, n_sketch = sizes
    step_count, input_count, half = markov.shape
    matrix_rows, _, columns = test_matrix.shape
    lag_total = matrix_rows * n_lag
    later = lag_total - 1
    dma = pltpu.SemaphoreType.DMA
    return pl.pallas_call(
        functools.partial(near_kernel, sizes, (half * 7 // 8, half * 5 // 8)),
        out_shape=[
            pltpu.VMEM((step_count, half * n_sketch, columns), jnp.float32),
            pltpu.VMEM((8, columns), jnp.float32),
        ],
        in_specs=[pl.BlockSpec(memory_space=pltpu.HBM)] * 2,
        out_specs=[pl.BlockSpec(memory_space=pltpu.VMEM)] * 2,
        scratch_shapes=[
            pltpu.VMEM((n_sketch, step_count + 2 * later, input_count, half), jnp.bfloat16),
            pltpu.VMEM((n_sketch, lag_total, input_count, columns), jnp.bfloat16),
            pltpu.VMEM(((step_count + later) * input_count, step_count * columns), jnp.bfloat16),
            pltpu.VMEM((lag_total * input_count, lag_total * input_count), jnp.float32),
            pltpu.VMEM((later * input_count, later * input_count), jnp.float32),
            pltpu.VMEM((1, columns), jnp.float32),
            pltpu.VMEM((n_lag * n_probe * n_sketch, columns), jnp.float32),
            dma, dma, dma, dma, dma, dma, dma, dma, dma, dma,
            dma, dma((2,)), dma, dma, dma((2,)), dma, dma,
            pltpu.SemaphoreType.REGULAR,
            pltpu.SemaphoreType.REGULAR((n_lag - 2,)),
        ],
        compiler_params=pltpu.CompilerParams(
            collective_id=1, has_side_effects=True, vmem_limit_bytes=59 * 1024 * 1024
        ),
    )(markov, test_matrix)


def is_near(sizes, markov, test_matrix):
    n_lag, n_probe, n_sketch = sizes
    step_count, input_count, half = markov.shape
    lag_total = test_matrix.shape[0] * n_lag
    return n_sketch == 2 and n_lag > 2 and 1 < lag_total <= step_count and half % 512 == 0


def scale_kernel(raw, factor, out, held, sem):
    step_count, probes, columns = raw.shape
    pieces = 16
    part = probes // pieces
    gain = factor[0:1, :]
    for row in range(step_count):
        for piece in range(pieces):
            place = pl.ds(piece * part, part)
            held[row, place] = (raw[row, place] * gain).astype(held.dtype)
            pltpu.make_async_copy(held.at[row, place], out.at[row, place], sem).start()
    pltpu.make_async_copy(held, out, sem).wait()


def scale(raw, factor):
    step_count, probes, columns = raw.shape
    return pl.pallas_call(
        scale_kernel,
        out_shape=jax.ShapeDtypeStruct(raw.shape, jnp.bfloat16),
        in_specs=[pl.BlockSpec(memory_space=pltpu.VMEM)] * 2,
        out_specs=pl.BlockSpec(memory_space=pltpu.HBM),
        scratch_shapes=[
            pltpu.VMEM(raw.shape, jnp.bfloat16),
            pltpu.SemaphoreType.DMA,
        ],
        compiler_params=pltpu.CompilerParams(vmem_limit_bytes=16 * 1024 * 1024),
    )(raw, factor)


def local(sizes, markov, test_matrix):
    if is_near(sizes, markov, test_matrix):
        return scale(*near(sizes, markov, test_matrix))
    n_lag, n_probe, n_sketch = sizes
    step_count, input_count, half = markov.shape
    matrix_rows, _, columns = test_matrix.shape
    lag_total = matrix_rows * n_lag
    steps, pieces = plan(step_count, lag_total)
    count = max(len(pieces), 1)
    pairs = max(n_sketch - 1, 1)
    probes = half * n_sketch
    dma = pltpu.SemaphoreType.DMA
    raw, factor = pl.pallas_call(
        functools.partial(gather_kernel, sizes),
        out_shape=[
            pltpu.VMEM((step_count, probes, columns), jnp.float32),
            pltpu.VMEM((8, columns), jnp.float32),
        ],
        in_specs=[pl.BlockSpec(memory_space=pltpu.HBM)] * 2,
        out_specs=[pl.BlockSpec(memory_space=pltpu.VMEM)] * 2,
        scratch_shapes=[
            pltpu.VMEM((n_sketch, steps, input_count, half), jnp.bfloat16),
            pltpu.VMEM((lag_total, input_count, columns), jnp.bfloat16),
            pltpu.VMEM((steps * input_count, step_count * columns), jnp.bfloat16),
            pltpu.VMEM((n_lag * n_probe, columns), jnp.float32),
            dma, dma, dma, dma,
            dma((pairs,)), dma((pairs,)),
            dma((count,)), dma((count,)),
            dma((count, pairs)), dma((count, pairs)),
            dma, dma,
        ],
        compiler_params=pltpu.CompilerParams(
            collective_id=0, has_side_effects=True, vmem_limit_bytes=59 * 1024 * 1024
        ),
    )(markov, test_matrix)
    return scale(raw, factor)


def solution(mesh):
    sizes = tuple(mesh.shape[name] for name in ("lag", "probe", "sketch"))
    return jax.shard_map(
        functools.partial(local, sizes),
        mesh=mesh,
        in_specs=(P("lag", None, ("probe", "sketch")), P("lag", None, "sketch")),
        out_specs=P("lag", "probe", "sketch"),
        check_vma=False,
    )
```
